128 devices in a mesh: feat: 8 (over y, core), dom: 16 (over x, z).
Axes of the slice: x: 4, y: 4, z: 4, core: 2. Of those that a mesh axis runs over, the one named last changes fastest.
Arguments:
- features: bfloat16 [768, 16, 2048], P('feat', 'dom'), may hold values from -6 to 6
- first_weight: bfloat16 [768, 1024], P('feat'), may hold values from -4 to 4
- second_weight: bfloat16 [1024, 153], replicated, may hold values from -6 to 6
- degree: int32 [16, 2048], P('dom', 'feat'), may hold values from 1 to 801, as said below
- neighbour_block: int32 [16, 16, 6], P('dom', 'feat'), may hold values from -1 to 31, as said below
- neighbour_mask: int32 [16, 16, 6, 128, 128], P('dom', 'feat'), may hold values from 0 to 1, as said below
- upstream: bfloat16 [16, 2048, 153], P('dom', 'feat'), may hold values from -0.078125 to 0.078125
Outputs:
- hidden: bfloat16 [16, 2048, 1024], P('dom', 'feat')
- grad_first: float32 [768, 1024], P('feat')
- grad_second: float32 [1024, 153], replicated
The draws below stay inside these ranges and needn't reach their ends.
Inputs may be any that keep to these rules, and one draw needn't show every extreme that they name: `neighbour_block`: within each group the block pattern is symmetric: the block row of block t names block c in some slot exactly when the block row of c names t. A block row names distinct blocks other than its own, live ones in its first slots and -1 in the others; in every group some block row has all 6 slots live. `neighbour_mask`: all zeros in slots that hold -1. The mask in the slot where block t names c is the transpose of the mask in the slot where c names t. `degree`: at least one plus the number of ones in the node's rows of its block row's masks.
All inputs are finite; a program needn't handle non-finite values.
Results may differ from the reference program's by a relative error of at most 0.018.
Values may be sent and summed in bfloat16 or wider, within the bound.
No kernel may reach another device: no remote copies, remote signals or barrier semaphores. Data moves between devices by JAX's collectives and lax.ppermute only.
A program may use at most 128 MiB of HBM per device.

```python
import jax
import jax.numpy as jnp
from jax import lax

F = 768
H = 1024
C = 153
BLK = 128
K = 6
RB = 2
NP = 2048
NODES = 32768
N_FEAT = 8
N_DOM = 16


def window_graph(key):
    group_blocks = N_DOM * RB
    half_count = K // 2

    def per_group(group_index):
        group_key = jax.random.fold_in(key, group_index)
        key_order = jax.random.fold_in(group_key, 11)
        key_offset = jax.random.fold_in(group_key, 12)
        key_weight = jax.random.fold_in(group_key, 13)
        key_hub = jax.random.fold_in(group_key, 14)
        key_pair = jax.random.fold_in(group_key, 15)
        key_mask = jax.random.fold_in(group_key, 16)
        ordering = jax.random.permutation(key_order, group_blocks)
        position = jnp.argsort(ordering)
        offsets = jax.random.permutation(key_offset, (group_blocks - 1) // 2)[:half_count] + 1
        signed = jnp.concatenate([offsets, -offsets])
        own_block = jnp.arange(group_blocks)
        candidate = ordering[(position[:, None] + signed[None, :]) % group_blocks]
        weights = jax.random.randint(key_weight, (group_blocks,), 1, 5)
        hub_block = jax.random.randint(key_hub, (), 0, group_blocks)
        low_block = jnp.minimum(own_block[:, None], candidate)
        high_block = jnp.maximum(own_block[:, None], candidate)
        pair_id = low_block * group_blocks + high_block

        def pair_roll(pair_index):
            return jax.random.randint(jax.random.fold_in(key_pair, pair_index), (), 0, 16)
        rolled = jax.vmap(jax.vmap(pair_roll))(pair_id)
        kept = (rolled < weights[low_block] * weights[high_block]) | (low_block == hub_block) | (high_block == hub_block)
        sort_key = jnp.where(kept, 0, K) + jnp.arange(K)[None, :]
        sort_order = jnp.argsort(sort_key, axis=1)
        candidate = jnp.take_along_axis(candidate, sort_order, 1)
        kept = jnp.take_along_axis(kept, sort_order, 1)
        pair_id = jnp.take_along_axis(pair_id, sort_order, 1)
        flipped = own_block[:, None] > candidate

        def pair_mask(pair_index, transposed, is_live):
            drawn = jax.random.randint(jax.random.fold_in(key_mask, pair_index), (BLK, BLK), 0, 8)
            chosen = (drawn == 0).astype(jnp.int32)
            chosen = jnp.where(transposed, chosen.T, chosen)
            return jnp.where(is_live, chosen, 0)
        block_masks = jax.vmap(jax.vmap(pair_mask))(pair_id, flipped, kept)
        linked = jnp.where(kept, candidate, -1)
        return (linked, block_masks)
    linked, block_masks = jax.vmap(per_group)(jnp.arange(N_FEAT))
    linked = linked.reshape(N_FEAT, N_DOM, RB, K).transpose(1, 0, 2, 3).reshape(N_DOM, N_FEAT * RB, K)
    block_masks = block_masks.reshape(N_FEAT, N_DOM, RB, K, BLK, BLK).transpose(1, 0, 2, 3, 4, 5)
    block_masks = block_masks.reshape(N_DOM, N_FEAT * RB, K, BLK, BLK)
    return (linked.astype(jnp.int32), block_masks.astype(jnp.int32))


def draw_neighbour_block(key, part):
    linked, block_masks = window_graph(key)
    return linked


def draw_neighbour_mask(key, part):
    linked, block_masks = window_graph(key)
    return block_masks


def draw_degree(key, part):
    linked, block_masks = window_graph(key)
    key = jax.random.fold_in(key, 3)
    key_top = jax.random.fold_in(key, 7)
    counted = jnp.sum(block_masks, axis=(2, 4)).reshape(N_DOM * N_FEAT * RB * BLK)
    beyond = jax.random.randint(key, counted.shape, 0, 33)
    values = 1 + counted + beyond
    chosen_node = jax.random.randint(key_top, (), 0, N_DOM * N_FEAT * RB * BLK)
    positions = jnp.arange(N_DOM * N_FEAT * RB * BLK)
    values = jnp.where(positions == chosen_node, K * BLK + 33, values)
    return values.reshape(N_DOM, N_FEAT * RB * BLK).astype(jnp.int32)


def block_scale(key, dims, split, smallest, top_value):
    factor_of = 1.0
    for dim, parts in split:
        heights = jax.random.uniform(jax.random.fold_in(jax.random.fold_in(key, 6), dim), (parts,), jnp.float32, smallest / len(split), top_value / len(split))
        factor_of = factor_of * jnp.repeat(jnp.exp(heights), dims[dim] // parts).reshape((-1,) + (1,) * (len(dims) - 1 - dim))
    return factor_of


def scatter_about(stream_key, dims, deviation, reach, pieces=(), dtype=jnp.bfloat16):
    entries = deviation * jax.random.normal(stream_key, dims, jnp.float32)
    if pieces:
        entries = entries * block_scale(stream_key, dims, pieces, -0.22, 0.18)
    return jnp.clip(entries, -reach, reach).astype(dtype)


def setup_inputs(seed: int = 0) -> dict:
    key_list = jax.random.split(jax.random.key(seed), 8)
    return {
        "features": scatter_about(key_list[0], (F, N_DOM, NP), 1.0, 6.0, ((0, 8), (1, 16))),
        "first_weight": scatter_about(key_list[1], (F, H), 0.3, 4.0, ((0, 8),)),
        "second_weight": scatter_about(key_list[2], (H, C), 0.6, 6.0),
        "degree": draw_degree(jax.random.fold_in(key_list[7], 71), 0),
        "neighbour_block": draw_neighbour_block(jax.random.fold_in(key_list[7], 71), 0),
        "neighbour_mask": draw_neighbour_mask(jax.random.fold_in(key_list[7], 71), 0),
        "upstream": scatter_about(key_list[6], (N_DOM, NP, C), (1.0 / NODES ** 0.5), 0.078125, ((0, 16), (1, 8))),
    }


def group_view(field):
    width = field.shape[-1]
    shaped = field.reshape(N_DOM, N_FEAT, RB, BLK, width)
    return shaped.transpose(1, 0, 2, 3, 4).reshape(N_FEAT, N_DOM * RB, BLK, width)

def aggregate(field, neighbour_block, neighbour_mask):
    groups = group_view(field)
    group_of = (jnp.arange(N_FEAT * RB) // RB).astype(jnp.int32)

    def per_partition(pair_items):
        neighbours, block_mask = pair_items
        blocks = groups[group_of[:, None], jnp.maximum(neighbours, 0).astype(jnp.int32)]
        summed = jnp.einsum('bkij,bkjh->bih', block_mask.astype(jnp.float32), blocks.astype(jnp.float32))
        return summed.reshape(N_FEAT * RB * BLK, field.shape[-1])
    return lax.map(per_partition, (neighbour_block, neighbour_mask))

def reference(features, first_weight, second_weight, degree, neighbour_block, neighbour_mask, upstream):
    slice_width = F // N_FEAT
    node_count = N_DOM * NP
    projected = jnp.zeros((node_count, H), jnp.float32)
    for feature_slice in range(N_FEAT):
        columns = features[feature_slice * slice_width:(feature_slice + 1) * slice_width].reshape(slice_width, node_count)
        weight_rows = first_weight[feature_slice * slice_width:(feature_slice + 1) * slice_width]
        partial_sum = jnp.dot(columns.T, weight_rows, preferred_element_type=jnp.float32)
        projected = projected + lax.optimization_barrier(partial_sum.astype(jnp.bfloat16)).astype(jnp.float32)
    projected = projected.reshape(N_DOM, NP, H)
    inverse_root = lax.rsqrt(degree.astype(jnp.float32))[:, :, None]
    scaled_zero = (inverse_root * projected).astype(jnp.bfloat16)
    mixed_zero = inverse_root * (scaled_zero.astype(jnp.float32) + aggregate(scaled_zero, neighbour_block, neighbour_mask))
    sigma = jax.nn.sigmoid(mixed_zero)
    hidden = (mixed_zero * sigma).astype(jnp.bfloat16)
    scaled_one = (inverse_root * hidden.astype(jnp.float32)).astype(jnp.bfloat16)
    mixed_one = (inverse_root * (scaled_one.astype(jnp.float32) + aggregate(scaled_one, neighbour_block, neighbour_mask))).astype(jnp.bfloat16)
    grad_second = jnp.dot(mixed_one.reshape(node_count, H).T, upstream.reshape(node_count, C), preferred_element_type=jnp.float32)
    back_product = jnp.dot(upstream.reshape(node_count, C), second_weight.T, preferred_element_type=jnp.float32).reshape(N_DOM, NP, H)
    back_one = (inverse_root * back_product).astype(jnp.bfloat16)
    pulled_one = back_one.astype(jnp.float32) + aggregate(back_one, neighbour_block, neighbour_mask)
    slope = sigma * (1.0 + mixed_zero * (1.0 - sigma))
    back_zero = (inverse_root * inverse_root * pulled_one * slope).astype(jnp.bfloat16)
    grad_rows = (inverse_root * (back_zero.astype(jnp.float32) + aggregate(back_zero, neighbour_block, neighbour_mask))).astype(jnp.bfloat16)
    grad_first = jnp.dot(features.reshape(F, node_count), grad_rows.reshape(node_count, H), preferred_element_type=jnp.float32)
    return (hidden, grad_first, grad_second)
```

```python
import jax
import jax.numpy as jnp
from jax import lax
from jax.experimental import pallas as pl
from jax.experimental.pallas import tpu as pltpu
from jax.sharding import Mesh
from jax.sharding import PartitionSpec as P

BF = jnp.bfloat16
F32 = jnp.float32
I32 = jnp.int32
VMEM = pl.BlockSpec(memory_space=pltpu.VMEM)
SMEM = pl.BlockSpec(memory_space=pltpu.SMEM)
LIMIT = 48 * 1024 * 1024
RING = (0, 1, -1, 2)
NT = (((1,), (1,)), ((), ()))


def dot(a, b, dims=(((1,), (0,)), ((), ()))):
    return lax.dot_general(a, b, dims, preferred_element_type=F32)


def columns_of(row):
    return jnp.broadcast_to(row, (128, 128)).T


def halves(a, b):
    low = lax.broadcasted_iota(I32, a.shape, 1) < 64
    return jnp.where(low, a, pltpu.roll(b, 64, 1)), jnp.where(low, pltpu.roll(a, 64, 1), b)


def owner(block):
    return (block % 4) * 4 + block // 4


def mask_kernel(mask_ref, out_ref):
    for b in range(2):
        for k in range(6):
            out_ref[b, :, k * 128 : k * 128 + 128] = mask_ref[b, k].astype(F32).astype(BF)


def project_kernel(*refs):
    x_ref, up_ref, sw_ref, deg_ref, at_ref = refs[:5]
    w_refs, out_ref = refs[5:13], refs[13]
    sources = []
    for flip in range(2):
        for shift in RING:
            y, core = (at_ref[3] + shift + 4) % 4, (at_ref[4] + flip) % 2
            sources.append(y * 2 + core)
    for b in range(2):
        row = lax.rsqrt(deg_ref[b : b + 1, :].astype(F32))
        inv = columns_of(row)
        rows = pl.ds(b * 128, 128)
        x = jnp.concatenate([x_ref[f, :, rows] for f in sources], axis=0)
        for j in range(4):
            cols = pl.ds(j * 256, 256)
            w = jnp.concatenate([w_ref[:, cols] for w_ref in w_refs], axis=0)
            sz = dot(x, w, (((0,), (0,)), ((), ())))
            bo = (row * dot(sw_ref[cols, :], up_ref[rows, :], NT)).astype(BF)
            for h in range(2):
                s = (inv * sz[:, h * 128 : h * 128 + 128]).T.astype(BF)
                for q in range(2):
                    d = owner(j * 4 + h * 2 + q)
                    out_ref[d, b, 0:64, :] = s[q * 64 : q * 64 + 64]
                    out_ref[d, b, 64:128, :] = bo[h * 128 + q * 64 : h * 128 + q * 64 + 64]


def mix_kernel(
    v_ref, m_ref, small_ref, links_ref, at_ref, hid_ref, mo_ref, g0_ref, g1_ref, g2_ref, g3_ref, v2_ref
):
    def inverse(d, h):
        return lax.rsqrt(small_ref[d, h : h + 1, :].astype(F32))

    def spread(d, h, source):
        t = d * 2 + h
        named = [source[links_ref[d, 2, h * 6 + k]] for k in range(6)]
        return source[t].astype(F32) + dot(jnp.concatenate(named, axis=1), m_ref[t], NT)

    for d in range(16):
        for h in range(2):
            inv = inverse(d, h)
            total = spread(d, h, v_ref)
            m = inv * total[0:64]
            s = jax.nn.sigmoid(m)
            hid = (m * s).astype(BF)
            hid_ref[d, :, h * 128 : h * 128 + 128] = hid
            slope = s * (1.0 + m * (1.0 - s))
            v2_ref[d * 2 + h, 0:64] = (inv * hid.astype(F32)).astype(BF)
            v2_ref[d * 2 + h, 64:128] = (inv * inv * total[64:128] * slope).astype(BF)
    for shift, g_ref in zip(RING, (g0_ref, g1_ref, g2_ref, g3_ref)):
        for z in range(4):
            d = ((at_ref[1] + shift + 4) % 4) * 4 + z
            for h in range(2):
                total = (inverse(d, h) * spread(d, h, v2_ref)).astype(BF)
                mo_ref[d, :, h * 128 : h * 128 + 128] = total[0:64]
                g_ref[z, :, h * 128 : h * 128 + 128] = total[64:128]


def second_kernel(u_ref, mo_ref, out_ref):
    total = jnp.zeros((160, 64), F32)
    for d in range(16):
        total = total + dot(u_ref[d], mo_ref[d], NT)
    out_ref[...] = jnp.concatenate([total[:80], total[80:]], axis=1).astype(BF)


def weigh_kernel(x0_ref, x1_ref, x2_ref, x3_ref, g0_ref, g1_ref, g2_ref, g3_ref, at_ref, out_ref):
    rights = []
    for shift in RING:
        z = (at_ref[2] + shift + 4) % 4
        rights.append(jnp.concatenate([g[z] for g in (g0_ref, g1_ref, g2_ref, g3_ref)], axis=0))
    for f in range(8):
        acc = jnp.zeros((96, 256), F32)
        for x_ref, right in zip((x0_ref, x1_ref, x2_ref, x3_ref), rights):
            acc = acc + dot(x_ref[f], right, NT)
        for p in range(2):
            g = acc[:, p * 128 : p * 128 + 128]
            for part, shift in zip(halves(g[:48], g[48:]), RING[2 * p : 2 * p + 2]):
                out_ref[f, (at_ref[1] - shift + 4) % 4] = part.astype(BF)


def add_kernel(part_ref, s0_ref, s1_ref, s2_ref, s3_ref, hid_ref, out_ref):
    first = part_ref[0].astype(F32)
    for i in range(1, 32):
        first = first + part_ref[i].astype(F32)
    second = s0_ref[...].astype(F32)
    for ref in (s1_ref, s2_ref, s3_ref):
        second = second + ref[...].astype(F32)
    both = jnp.concatenate([first, second], axis=0).astype(BF)
    for d in range(16):
        out_ref[d, 0:128] = both
        out_ref[d, 128:192] = hid_ref[d, :, 0:128]
        out_ref[d, 192:256] = hid_ref[d, :, 128:256]


def final_kernel(in_ref, hidden_ref, first_ref, second_ref):
    for j in range(8):
        cols = pl.ds(j * 128, 128)
        even, odd = owner(2 * j), owner(2 * j + 1)
        one, two = halves(in_ref[even, 0:128].astype(F32), in_ref[odd, 0:128].astype(F32))
        first_ref[0:48, cols] = one[:48]
        first_ref[48:96, cols] = two[:48]
        second_ref[0:80, cols] = one[48:]
        second_ref[80:153, cols] = two[48:121]
        for h in range(2):
            rows = pl.ds(128 + h * 64, 64)
            both = jnp.concatenate([in_ref[even, rows], in_ref[odd, rows]], axis=0)
            hidden_ref[h * 128 : h * 128 + 128, cols] = both.astype(F32).T.astype(BF)


def call(kernel, shape, specs, scratch=(), flops=0, moved=0):
    return pl.pallas_call(
        kernel,
        out_shape=shape,
        in_specs=specs,
        out_specs=jax.tree.map(lambda _: VMEM, shape),
        scratch_shapes=list(scratch),
        compiler_params=pltpu.CompilerParams(vmem_limit_bytes=LIMIT),
        cost_estimate=pl.CostEstimate(flops=flops, bytes_accessed=moved, transcendentals=0),
    )


def fetch(value, axis, shift):
    return lax.ppermute(value, axis, [((i + shift) % 4, i) for i in range(4)])


def ring(value, axis):
    return [value] + [fetch(value, axis, shift) for shift in RING[1:]]


def body(features, first_weight, second_weight, degree, neighbour_block, neighbour_mask, upstream):
    feat, dom = ("y", "c"), ("x", "z")
    shape = jax.ShapeDtypeStruct
    x, z = lax.axis_index("x"), lax.axis_index("z")
    at = jnp.stack([x * 4 + z, x, z, lax.axis_index("y"), lax.axis_index("c")])
    masks = call(mask_kernel, shape((2, 128, 768), BF), [VMEM], moved=1_200_000)(neighbour_mask[0])
    masks = lax.all_gather(masks, dom, axis=0, tiled=True)
    weights = ring(first_weight, "y")
    weights = weights + [lax.ppermute(w, "c", [(0, 1), (1, 0)]) for w in weights]
    x_own = lax.all_to_all(
        features.reshape(96, 8, 256).transpose(1, 0, 2), feat, 0, 0, tiled=True
    )
    links = jnp.pad(jnp.maximum(neighbour_block.reshape(12), 0), (0, 244))
    small = jnp.concatenate([degree.reshape(2, 128), links.reshape(2, 128)], axis=0)
    up = jnp.pad(upstream[0].T, ((0, 7), (0, 0)))
    x_own, small, up = lax.optimization_barrier((x_own, small, up))
    small = lax.all_to_all(jnp.broadcast_to(small, (16, 4, 128)), dom, 0, 0, tiled=True)
    up = lax.all_to_all(jnp.broadcast_to(up, (16, 160, 256)), dom, 0, 0, tiled=True)

    v = call(
        project_kernel,
        shape((16, 2, 128, 128), BF),
        [VMEM] * 4 + [SMEM] + [VMEM] * 8,
        flops=500_000_000,
        moved=4_000_000,
    )(x_own, upstream[0], second_weight, degree.reshape(2, 128), at, *weights)
    v = lax.all_to_all(v, dom, 0, 0, tiled=True).reshape(32, 128, 128)
    v, x_own = lax.optimization_barrier((v, x_own))
    x_wide = ring(x_own, "z")
    hid, mo, *g = call(
        mix_kernel,
        (shape((16, 64, 256), BF), shape((16, 64, 256), BF)) + (shape((4, 64, 256), BF),) * 4,
        [VMEM, VMEM, VMEM, SMEM, SMEM],
        [pltpu.VMEM((32, 128, 128), BF)],
        flops=1_600_000_000,
        moved=9_000_000,
    )(v, masks, small, small, at)
    g = [g[0]] + [fetch(value, "x", -shift) for value, shift in zip(g[1:], RING[1:])]
    second = call(second_kernel, shape((80, 128), BF), [VMEM] * 2, flops=100_000_000, moved=2_000_000)(
        up, mo
    )
    other = lax.ppermute(second, "c", [(0, 1), (1, 0)])
    second = ring((second.astype(F32) + other.astype(F32)).astype(BF), "y")
    part = call(
        weigh_kernel,
        shape((8, 4, 48, 128), BF),
        [VMEM] * 8 + [SMEM],
        flops=400_000_000,
        moved=3_000_000,
    )(*x_wide, *g, at)
    part = lax.all_to_all(part.reshape(32, 48, 128), ("y", "c", "x"), 0, 0, tiled=True)
    done = call(add_kernel, shape((16, 256, 128), BF), [VMEM] * 6, moved=3_000_000)(part, *second, hid)
    done = lax.all_to_all(done, dom, 0, 0, tiled=True)
    hidden, grad_first, grad_second = call(
        final_kernel,
        (shape((256, 1024), BF), shape((96, 1024), F32), shape((153, 1024), F32)),
        [VMEM],
        moved=2_500_000,
    )(done)
    return (hidden[None], grad_first, grad_second.T)


def solution(mesh):
    wide = Mesh(mesh.devices.reshape(4, 2, 4, 4), ("y", "c", "x", "z"))
    feat, dom = ("y", "c"), ("x", "z")
    placed = (
        P(feat, dom, None),
        P(feat, None),
        P(),
        P(dom, feat),
        P(dom, feat, None),
        P(dom, feat, None, None, None),
        P(dom, feat, None),
    )
    return jax.shard_map(
        body,
        mesh=wide,
        in_specs=placed,
        out_specs=(P(dom, feat, None), P(feat, None), P()),
        check_vma=False,
    )
```

```python
import jax
import jax.numpy as jnp
from jax import lax
from jax.experimental import pallas as pl
from jax.experimental.pallas import tpu as pltpu
from jax.sharding import Mesh
from jax.sharding import PartitionSpec as P

BF = jnp.bfloat16
F32 = jnp.float32
I32 = jnp.int32
VMEM = pl.BlockSpec(memory_space=pltpu.VMEM)
SMEM = pl.BlockSpec(memory_space=pltpu.SMEM)
LIMIT = 48 * 1024 * 1024
RING = (0, 1, -1, 2)
NT = (((1,), (1,)), ((), ()))


def dot(a, b, dims=(((1,), (0,)), ((), ()))):
    return lax.dot_general(a, b, dims, preferred_element_type=F32)


def columns_of(row):
    return jnp.broadcast_to(row, (128, 128)).T


def halves(a, b):
    low = lax.broadcasted_iota(I32, a.shape, 1) < 64
    return jnp.where(low, a, pltpu.roll(b, 64, 1)), jnp.where(low, pltpu.roll(a, 64, 1), b)


def owner(block):
    return (block % 4) * 4 + block // 4


def mask_kernel(mask_ref, up_ref, out_ref):
    for b in range(2):
        for k in range(6):
            out_ref[b * 128 : b * 128 + 128, k * 128 : k * 128 + 128] = (
                mask_ref[b, k].astype(F32).astype(BF)
            )
    out_ref[256:320, 0:256] = up_ref[0:64, :]
    out_ref[256:320, 256:512] = up_ref[64:128, :]
    rest = jnp.concatenate([up_ref[128:153, :].astype(F32), jnp.zeros((39, 256), F32)], axis=0)
    out_ref[256:320, 512:768] = rest.astype(BF)


def project_kernel(*refs):
    x_ref, deg_ref, links_ref, at_ref = refs[:4]
    w_refs, out_ref = refs[4:12], refs[12]
    sources = []
    for flip in range(2):
        for shift in RING:
            y, core = (at_ref[3] + shift + 4) % 4, (at_ref[4] + flip) % 2
            sources.append(y * 2 + core)
    info = []
    for b in range(2):
        degree = deg_ref[b : b + 1, :]
        info += [degree >> 5, degree & 31]
        inv = columns_of(lax.rsqrt(degree.astype(F32)))
        rows = pl.ds(b * 128, 128)
        x = jnp.concatenate([x_ref[f, :, rows] for f in sources], axis=0)
        for j in range(4):
            cols = pl.ds(j * 256, 256)
            w = jnp.concatenate([w_ref[:, cols] for w_ref in w_refs], axis=0)
            sz = dot(x, w, (((0,), (0,)), ((), ())))
            for h in range(2):
                s = (inv * sz[:, h * 128 : h * 128 + 128]).T.astype(BF)
                for q in range(2):
                    d = owner(j * 4 + h * 2 + q)
                    out_ref[d, b * 64 : b * 64 + 64, :] = s[q * 64 : q * 64 + 64]
    info = jnp.concatenate(info + [links_ref[...]] + [jnp.zeros((11, 128), I32)], axis=0)
    info = info.astype(F32).astype(BF)
    for d in range(16):
        out_ref[d, 128:144, :] = info


def mix_kernel(
    v_ref, m_ref, sw_ref, at_ref, hid_ref, second_ref, g0_ref, g1_ref, g2_ref, g3_ref,
    src_ref, v2_ref, inv_ref, stage_ref, links_ref, link_sem,
):
    links = []
    for d in range(16):
        info = v_ref[d, 128:144, :].astype(F32)
        links.append(info[4:5])
        for h in range(2):
            t = d * 2 + h
            inv = lax.rsqrt(info[2 * h : 2 * h + 1] * 32.0 + info[2 * h + 1 : 2 * h + 2])
            inv_ref[t] = inv
            src_ref[t, 0:64] = v_ref[d, h * 64 : h * 64 + 64, :]
            for c in range(3):
                rows = min(64, 160 - 64 * c)
                up = m_ref[d, 256 : 256 + rows, c * 256 + h * 128 : c * 256 + h * 128 + 128]
                src_ref[t, 64 + 64 * c : 64 + 64 * c + rows] = (inv * up.astype(F32)).astype(BF)
    stage_ref[...] = jnp.concatenate(links, axis=0).astype(I32)
    to_scalars = pltpu.make_async_copy(stage_ref, links_ref, link_sem)
    to_scalars.start()
    to_scalars.wait()

    def spread(d, h, source):
        named = [source[links_ref[d, h * 6 + k]] for k in range(6)]
        weights = m_ref[d, h * 128 : h * 128 + 128, :]
        return source[d * 2 + h].astype(F32) + dot(jnp.concatenate(named, axis=1), weights, NT)

    second = jnp.zeros((160, 64), F32)
    for d in range(16):
        ones, pulls = [], []
        for h in range(2):
            t = d * 2 + h
            inv = inv_ref[t]
            total = spread(d, h, src_ref)
            m = inv * total[0:64]
            s = jax.nn.sigmoid(m)
            hid = (m * s).astype(BF)
            hid_ref[d, :, h * 128 : h * 128 + 128] = hid
            ones.append((inv * hid.astype(F32)).astype(BF))
            pull = total[64:224].astype(BF)
            pulls.append(pull)
            slope = s * (1.0 + m * (1.0 - s))
            v2_ref[t] = (inv * inv * dot(sw_ref[...], pull) * slope).astype(BF)
        second = second + dot(jnp.concatenate(pulls, axis=1), jnp.concatenate(ones, axis=1), NT)
    second_ref[...] = jnp.concatenate([second[:80], second[80:]], axis=1).astype(BF)
    for shift, g_ref in zip(RING, (g0_ref, g1_ref, g2_ref, g3_ref)):
        for z in range(4):
            d = ((at_ref[1] + shift + 4) % 4) * 4 + z
            for h in range(2):
                g = inv_ref[d * 2 + h] * spread(d, h, v2_ref)
                g_ref[z, :, h * 128 : h * 128 + 128] = g.astype(BF)


def weigh_kernel(x0_ref, x1_ref, x2_ref, x3_ref, g0_ref, g1_ref, g2_ref, g3_ref, at_ref, out_ref):
    rights = []
    for shift in RING:
        z = (at_ref[2] + shift + 4) % 4
        rights.append(jnp.concatenate([g[z] for g in (g0_ref, g1_ref, g2_ref, g3_ref)], axis=0))
    for f in range(8):
        acc = jnp.zeros((96, 256), F32)
        for x_ref, right in zip((x0_ref, x1_ref, x2_ref, x3_ref), rights):
            acc = acc + dot(x_ref[f], right, NT)
        for p in range(2):
            g = acc[:, p * 128 : p * 128 + 128]
            for part, shift in zip(halves(g[:48], g[48:]), RING[2 * p : 2 * p + 2]):
                out_ref[f, (at_ref[1] - shift + 4) % 4] = part.astype(BF)


def add_kernel(part_ref, s0_ref, s1_ref, s2_ref, s3_ref, hid_ref, out_ref):
    first = part_ref[0].astype(F32)
    for i in range(1, 32):
        first = first + part_ref[i].astype(F32)
    second = s0_ref[...].astype(F32)
    for ref in (s1_ref, s2_ref, s3_ref):
        second = second + ref[...].astype(F32)
    both = jnp.concatenate([first, second], axis=0).astype(BF)
    for d in range(16):
        out_ref[d, 0:128] = both
        out_ref[d, 128:192] = hid_ref[d, :, 0:128]
        out_ref[d, 192:256] = hid_ref[d, :, 128:256]


def final_kernel(in_ref, hidden_ref, first_ref, second_ref):
    for j in range(8):
        cols = pl.ds(j * 128, 128)
        even, odd = owner(2 * j), owner(2 * j + 1)
        one, two = halves(in_ref[even, 0:128].astype(F32), in_ref[odd, 0:128].astype(F32))
        first_ref[0:48, cols] = one[:48]
        first_ref[48:96, cols] = two[:48]
        second_ref[0:80, cols] = one[48:]
        second_ref[80:153, cols] = two[48:121]
        for h in range(2):
            rows = pl.ds(128 + h * 64, 64)
            both = jnp.concatenate([in_ref[even, rows], in_ref[odd, rows]], axis=0)
            hidden_ref[h * 128 : h * 128 + 128, cols] = both.astype(F32).T.astype(BF)


def call(kernel, shape, specs, scratch=(), flops=0, moved=0):
    return pl.pallas_call(
        kernel,
        out_shape=shape,
        in_specs=specs,
        out_specs=jax.tree.map(lambda _: VMEM, shape),
        scratch_shapes=list(scratch),
        compiler_params=pltpu.CompilerParams(vmem_limit_bytes=LIMIT),
        cost_estimate=pl.CostEstimate(flops=flops, bytes_accessed=moved, transcendentals=0),
    )


def fetch(value, axis, shift):
    return lax.ppermute(value, axis, [((i + shift) % 4, i) for i in range(4)])


def ring(value, axis):
    return [value] + [fetch(value, axis, shift) for shift in RING[1:]]


def body(features, first_weight, second_weight, degree, neighbour_block, neighbour_mask, upstream):
    feat, dom = ("y", "c"), ("x", "z")
    shape = jax.ShapeDtypeStruct
    x, z = lax.axis_index("x"), lax.axis_index("z")
    at = jnp.stack([x * 4 + z, x, z, lax.axis_index("y"), lax.axis_index("c")])
    masks = call(mask_kernel, shape((320, 768), BF), [VMEM] * 2, moved=1_200_000)(
        neighbour_mask[0], upstream[0].T
    )
    masks = lax.all_gather(masks, dom, axis=0)
    x_own = lax.all_to_all(
        features.reshape(96, 8, 256).transpose(1, 0, 2), feat, 0, 0, tiled=True
    )
    weights = ring(first_weight, "y")
    weights = weights + [lax.ppermute(w, "c", [(0, 1), (1, 0)]) for w in weights]
    links = jnp.pad(jnp.maximum(neighbour_block.reshape(1, 12), 0), ((0, 0), (0, 116)))
    own_second = lax.dynamic_slice(second_weight, ((z * 4 + x) * 64, 0), (64, 153))
    own_second = jnp.pad(own_second, ((0, 0), (0, 7)))
    v = call(
        project_kernel,
        shape((16, 144, 128), BF),
        [VMEM] * 3 + [SMEM] + [VMEM] * 8,
        flops=400_000_000,
        moved=3_000_000,
    )(x_own, degree.reshape(2, 128), links, at, *weights)
    v = lax.all_to_all(v, dom, 0, 0, tiled=True)
    v, x_own = lax.optimization_barrier((v, x_own))
    v, *x_wide = lax.optimization_barrier((v, *ring(x_own, "z")))
    hid, second, *g = call(
        mix_kernel,
        (shape((16, 64, 256), BF), shape((80, 128), BF)) + (shape((4, 64, 256), BF),) * 4,
        [VMEM, VMEM, VMEM, SMEM],
        [
            pltpu.VMEM((32, 224, 128), BF),
            pltpu.VMEM((32, 64, 128), BF),
            pltpu.VMEM((32, 1, 128), F32),
            pltpu.VMEM((16, 128), I32),
            pltpu.SMEM((16, 128), I32),
            pltpu.SemaphoreType.DMA,
        ],
        flops=1_600_000_000,
        moved=10_000_000,
    )(v, masks, own_second, at)
    g = [g[0]] + [fetch(value, "x", -shift) for value, shift in zip(g[1:], RING[1:])]
    other = lax.ppermute(second, "c", [(0, 1), (1, 0)])
    second = ring((second.astype(F32) + other.astype(F32)).astype(BF), "y")
    *g, second[1], second[2], second[3] = lax.optimization_barrier((*g, *second[1:]))
    part = call(
        weigh_kernel,
        shape((8, 4, 48, 128), BF),
        [VMEM] * 8 + [SMEM],
        flops=400_000_000,
        moved=3_000_000,
    )(*x_wide, *g, at)
    part = lax.all_to_all(part.reshape(32, 48, 128), ("y", "c", "x"), 0, 0, tiled=True)
    done = call(add_kernel, shape((16, 256, 128), BF), [VMEM] * 6, moved=3_000_000)(part, *second, hid)
    done = lax.all_to_all(done, dom, 0, 0, tiled=True)
    hidden, grad_first, grad_second = call(
        final_kernel,
        (shape((256, 1024), BF), shape((96, 1024), F32), shape((153, 1024), F32)),
        [VMEM],
        moved=2_500_000,
    )(done)
    return (hidden[None], grad_first, grad_second.T)


def solution(mesh):
    wide = Mesh(mesh.devices.reshape(4, 2, 4, 4), ("y", "c", "x", "z"))
    feat, dom = ("y", "c"), ("x", "z")
    placed = (
        P(feat, dom, None),
        P(feat, None),
        P(),
        P(dom, feat),
        P(dom, feat, None),
        P(dom, feat, None, None, None),
        P(dom, feat, None),
    )
    return jax.shard_map(
        body,
        mesh=wide,
        in_specs=placed,
        out_specs=(P(dom, feat, None), P(feat, None), P()),
        check_vma=False,
    )
```

```python
import functools

import jax
import jax.numpy as jnp
from jax import lax
from jax.experimental import pallas as pl
from jax.experimental.pallas import tpu as pltpu
from jax.sharding import Mesh
from jax.sharding import PartitionSpec as P

BF = jnp.bfloat16
F32 = jnp.float32
I32 = jnp.int32
VMEM = pl.BlockSpec(memory_space=pltpu.VMEM)
SMEM = pl.BlockSpec(memory_space=pltpu.SMEM)
ANY = pl.BlockSpec(memory_space=pl.ANY)
LIMIT = 48 * 1024 * 1024
RING = (0, 1, -1, 2)
NT = (((1,), (1,)), ((), ()))


def dot(a, b, dims=(((1,), (0,)), ((), ()))):
    return lax.dot_general(a, b, dims, preferred_element_type=F32)


def columns_of(row):
    return jnp.broadcast_to(row, (128, 128)).T


def halves(a, b):
    low = lax.broadcasted_iota(I32, a.shape, 1) < 64
    return jnp.where(low, a, pltpu.roll(b, 64, 1)), jnp.where(low, pltpu.roll(a, 64, 1), b)


def owner(block):
    return (block % 4) * 4 + block // 4


def orient_kernel(small_ref, table_ref):
    links = small_ref[0, 2:4, :]
    for d in range(1, 16):
        links = links + small_ref[d, 2:4, :]
    links = links.astype(F32)
    row = jnp.concatenate([links[0:1], links[1:2]], axis=1)
    side = jnp.concatenate([columns_of(links[0:1]), columns_of(links[1:2])], axis=0)
    link_r = jnp.broadcast_to(row, (256, 256)) - 2.0
    link_c = jnp.concatenate([side, side], axis=1) - 2.0
    index_c = lax.broadcasted_iota(I32, (256, 256), 0)
    index_r = lax.broadcasted_iota(I32, (256, 256), 1)
    block_c = ((index_c * 10923) >> 16).astype(F32)
    block_r = ((index_r * 10923) >> 16).astype(F32)
    opposite = (link_c == block_r) & (link_r == block_c)
    paired = ((index_c ^ 1) == index_r) & (link_c >= 0.0) & (link_r >= 0.0)
    opposite = jnp.where(opposite, 1.0, 0.0)
    paired = jnp.where(paired, 1.0, 0.0)
    near = dot(paired.astype(BF), opposite.astype(BF)) + dot(opposite.astype(BF), paired.astype(BF))
    reach = jnp.where((near > 0.0) | (index_c == index_r), 1.0, 0.0).astype(BF)
    for _ in range(7):
        reach = jnp.where(dot(reach, reach) > 0.0, 1.0, 0.0).astype(BF)
    reach = reach.astype(F32)
    label_c = jnp.min(jnp.where(reach > 0.0, index_r.astype(F32), 999.0), axis=1, keepdims=True)
    label_r = jnp.min(jnp.where(reach > 0.0, index_c.astype(F32), 999.0), axis=0, keepdims=True)
    other_r = jnp.sum(opposite * label_c, axis=0, keepdims=True)
    sends_r = (label_r < other_r) & (row >= 2.0)
    table_ref[...] = jnp.where(sends_r, row - 1.0, 0.0).astype(I32)


def mask_kernel(mask_ref, up_ref, a_ref, b_ref):
    for b, out_ref in enumerate((a_ref, b_ref)):
        for k in range(6):
            out_ref[0:128, k * 128 : k * 128 + 128] = mask_ref[b, k].astype(F32).astype(BF)
    a_ref[128:192, 0:256] = up_ref[0:64, :]
    a_ref[128:192, 256:512] = up_ref[64:128, :]
    rest = jnp.concatenate([up_ref[128:153, :].astype(F32), jnp.zeros((39, 256), F32)], axis=0)
    a_ref[128:192, 512:768] = rest.astype(BF)


def select_kernel(which, *refs):
    blocks, table_ref, at_ref, outs = refs[:4], refs[4], refs[5], refs[6:8]
    height = outs[0].shape[0] // 2
    for k, ref in enumerate(blocks):
        if which == 0:
            d = at_ref[1] * 4 + (at_ref[2] + RING[k] + 4) % 4
        else:
            d = ((at_ref[1] + RING[k] + 4) % 4) * 4 + at_ref[2]
        out_ref, base = outs[k // 2], (k % 2) * height
        for m in range(3):
            at = d * 12 + which * 6 + m * 2
            first = jnp.where(table_ref[0, at] > 0, 1.0, 0.0)
            second = jnp.where(table_ref[0, at + 1] > 0, 1.0, 0.0)
            one = ref[0:128, m * 256 : m * 256 + 128].astype(F32)
            two = ref[0:128, m * 256 + 128 : m * 256 + 256].astype(F32)
            out_ref[base : base + 128, m * 128 : m * 128 + 128] = (first * one + second * two).astype(BF)
        if which == 0:
            out_ref[base + 128 : base + 192, :] = ref[128:192, 0:384]
            out_ref[base + 192 : base + 256, :] = ref[128:192, 384:768]


def project_kernel(*refs):
    x_refs, w_refs, small_ref, at_ref = refs[:8], refs[8:12], refs[12], refs[13]
    v_refs, w_ref, t_ref = refs[14:18], refs[18], refs[19]
    for k, shift in enumerate(RING):
        for flip in range(2):
            f = ((at_ref[3] + shift + 4) % 4) * 2 + (at_ref[4] + flip) % 2
            w_ref[f] = w_refs[k][flip]
    w = w_ref[...].reshape(768, 256).astype(F32).T.astype(BF)
    for k, shift in enumerate(RING):
        z = (at_ref[2] + shift + 4) % 4
        degree = small_ref[at_ref[1] * 4 + z].astype(F32)
        inv = lax.rsqrt(jnp.concatenate([degree[0:1], degree[1:2]], axis=1))
        low, high = x_refs[2 * k][...].reshape(384, 256), x_refs[2 * k + 1][...].reshape(384, 256)
        t_ref[k] = (inv * (dot(w[:, 0:384], low) + dot(w[:, 384:768], high))).astype(BF)
        for v_ref, to in zip(v_refs, RING):
            at = pl.multiple_of(((at_ref[1] + to + 4) % 4) * 64, 64)
            v_ref[z] = t_ref[k, pl.ds(at, 64), :]


def places(at_ref):
    found = []
    for i, dx in enumerate(RING):
        for j, dz in enumerate(RING):
            found.append((i, j, ((at_ref[1] + dx + 4) % 4) * 4 + (at_ref[2] + dz + 4) % 4))
    return found


def mix_kernel(*refs):
    v_refs, small_ref, tab_ref, sw_ref, at_ref = refs[:4], refs[4], refs[5], refs[6], refs[7]
    mask_refs = refs[8:24]
    hid_ref, second_ref, g_refs = refs[24], refs[25], refs[26:30]
    ma_ref, mb_ref, src_ref, acc_ref, v2_ref, acc2_ref, inv_ref, sems = refs[30:]
    copies = []
    for i, ref in enumerate(mask_refs):
        to = ma_ref.at[i] if i < 8 else mb_ref.at[i - 8]
        copies.append(pltpu.make_async_copy(ref, to, sems.at[i]))
    for copy in copies:
        copy.start()
    for d in range(16):
        degree = small_ref[d].astype(F32)
        for h in range(2):
            inv_ref[2 * d + h] = lax.rsqrt(degree[h : h + 1])
    for copy in copies:
        copy.wait()
    for i, j, d in places(at_ref):
        at, base = i * 2 + j // 2, (j % 2) * 256 + 128
        v_ref = v_refs[(0, 2, 1, 3)[i]]
        z = (at_ref[2] + RING[j] + 4) % 4
        for h in range(2):
            t = d * 2 + h
            inv = inv_ref[t]
            v = v_ref[z, :, h * 128 : h * 128 + 128]
            src_ref[t, 0:64] = v
            acc_ref[t, 0:64] = v.astype(F32)
            second = (base, 256) if h == 0 else (base + 64, 0)
            for c, rows, (row, lane) in (
                (0, 64, (base, h * 128)), (1, 64, second), (2, 32, (base + 64, 128 + h * 128))
            ):
                up = (inv * ma_ref[at, row : row + rows, lane : lane + 128].astype(F32)).astype(BF)
                src_ref[t, 64 + 64 * c : 64 + 64 * c + rows] = up
                acc_ref[t, 64 + 64 * c : 64 + 64 * c + rows] = up.astype(F32)

    def spread(source, total_ref):
        for i, j, d in places(at_ref):
            for h in range(2):
                t = d * 2 + h
                if h == 0:
                    weights = ma_ref[i * 2 + j // 2, (j % 2) * 256 : (j % 2) * 256 + 128, :]
                else:
                    weights = mb_ref[j * 2 + i // 2, (i % 2) * 128 : (i % 2) * 128 + 128, :]
                named = []
                for m in range(3):
                    c = tab_ref[0, 6 * t + 2 * m] + tab_ref[0, 6 * t + 2 * m + 1]
                    named.append(jnp.maximum(c - 1, 0))
                own = source[t]
                others = jnp.concatenate([source[c] for c in named], axis=1)
                back = dot(own, weights)
                total_ref[t] = total_ref[t] + dot(others, weights, NT)
                for m in range(3):
                    total_ref[named[m]] = total_ref[named[m]] + back[:, m * 128 : m * 128 + 128]

    spread(src_ref, acc_ref)
    second = jnp.zeros((160, 64), F32)
    for d in range(16):
        ones, pulls = [], []
        for h in range(2):
            t = d * 2 + h
            inv = inv_ref[t]
            m = inv * acc_ref[t, 0:64]
            s = jax.nn.sigmoid(m)
            hid = (m * s).astype(BF)
            hid_ref[d, :, h * 128 : h * 128 + 128] = hid
            ones.append((inv * hid.astype(F32)).astype(BF))
            pull = acc_ref[t, 64:224].astype(BF)
            pulls.append(pull)
            slope = s * (1.0 + m * (1.0 - s))
            back = (inv * inv * dot(sw_ref[...], pull) * slope).astype(BF)
            v2_ref[t] = back
            acc2_ref[t] = back.astype(F32)
        second = second + dot(jnp.concatenate(pulls, axis=1), jnp.concatenate(ones, axis=1), NT)
    second_ref[...] = jnp.concatenate([second[:80], second[80:]], axis=1).astype(BF)
    spread(v2_ref, acc2_ref)
    for shift, g_ref in zip(RING, g_refs):
        for z in range(4):
            d = ((at_ref[1] + shift + 4) % 4) * 4 + z
            for h in range(2):
                g_ref[z, :, h * 128 : h * 128 + 128] = (
                    inv_ref[d * 2 + h] * acc2_ref[d * 2 + h]
                ).astype(BF)


def weigh_kernel(*refs):
    x_refs, g_refs, at_ref, out_ref = refs[:8], refs[8:12], refs[12], refs[13]
    rights = []
    for shift in RING:
        z = (at_ref[2] + shift + 4) % 4
        rights.append(jnp.concatenate([g[z] for g in g_refs], axis=0))
    for f in range(8):
        acc = jnp.zeros((96, 256), F32)
        for k, right in enumerate(rights):
            acc = acc + dot(x_refs[2 * k + f // 4][f % 4], right, NT)
        for p in range(2):
            g = acc[:, p * 128 : p * 128 + 128]
            for part, shift in zip(halves(g[:48], g[48:]), RING[2 * p : 2 * p + 2]):
                out_ref[f, (at_ref[1] - shift + 4) % 4] = part.astype(BF)


def add_kernel(part_ref, s0_ref, s1_ref, s2_ref, s3_ref, hid_ref, out_ref):
    first = part_ref[0].astype(F32)
    for i in range(1, 32):
        first = first + part_ref[i].astype(F32)
    second = s0_ref[...].astype(F32)
    for ref in (s1_ref, s2_ref, s3_ref):
        second = second + ref[...].astype(F32)
    both = jnp.concatenate([first, second], axis=0).astype(BF)
    for d in range(16):
        out_ref[d, 0:128] = both
        out_ref[d, 128:192] = hid_ref[d, :, 0:128]
        out_ref[d, 192:256] = hid_ref[d, :, 128:256]


def final_kernel(in_ref, hidden_ref, first_ref, second_ref):
    for j in range(8):
        cols = pl.ds(j * 128, 128)
        even, odd = owner(2 * j), owner(2 * j + 1)
        one, two = halves(in_ref[even, 0:128].astype(F32), in_ref[odd, 0:128].astype(F32))
        first_ref[0:48, cols] = one[:48]
        first_ref[48:96, cols] = two[:48]
        second_ref[0:80, cols] = one[48:]
        second_ref[80:153, cols] = two[48:121]
        for h in range(2):
            rows = pl.ds(128 + h * 64, 64)
            both = jnp.concatenate([in_ref[even, rows], in_ref[odd, rows]], axis=0)
            hidden_ref[h * 128 : h * 128 + 128, cols] = both.astype(F32).T.astype(BF)


def call(kernel, shape, specs, scratch=(), flops=0, moved=0):
    return pl.pallas_call(
        kernel,
        out_shape=shape,
        in_specs=specs,
        out_specs=jax.tree.map(lambda _: VMEM, shape),
        scratch_shapes=list(scratch),
        compiler_params=pltpu.CompilerParams(vmem_limit_bytes=LIMIT),
        cost_estimate=pl.CostEstimate(flops=flops, bytes_accessed=moved, transcendentals=0),
    )


def fetch(value, axis, shift):
    return lax.ppermute(value, axis, [((i + shift) % 4, i) for i in range(4)])


def ring(value, axis):
    return [value] + [fetch(value, axis, shift) for shift in RING[1:]]


def rounds(low, high, axis):
    after = [fetch(low, axis, 1), fetch(high, axis, 1)]
    before = [fetch(low, axis, -1), fetch(high, axis, -1)]
    low2, high2, *rest = lax.optimization_barrier((after[0], before[1], low, high))
    far = [fetch(low2, axis, 1), fetch(high2, axis, -1)]
    return [*rest, low2, after[1], before[0], high2, *far]


def body(features, first_weight, second_weight, degree, neighbour_block, neighbour_mask, upstream):
    feat, dom = ("y", "c"), ("x", "z")
    shape = jax.ShapeDtypeStruct
    x, z = lax.axis_index("x"), lax.axis_index("z")
    at = jnp.stack([x * 4 + z, x, z, lax.axis_index("y"), lax.axis_index("c")])
    links = lax.dynamic_update_slice(
        jnp.zeros((256,), I32), neighbour_block.reshape(12) + 2, ((x * 4 + z) * 12,)
    )
    small = jnp.concatenate([degree.reshape(2, 128), links.reshape(2, 128)], axis=0)
    small = lax.all_to_all(jnp.broadcast_to(small, (16, 4, 128)), dom, 0, 0, tiled=True)
    mask_a, mask_b = call(
        mask_kernel, (shape((192, 768), BF), shape((128, 768), BF)), [VMEM] * 2, moved=1_200_000
    )(neighbour_mask[0], upstream[0].T)
    features, small, mask_a, mask_b = lax.optimization_barrier((features, small, mask_a, mask_b))
    x_own = lax.all_to_all(
        features.reshape(96, 8, 256).transpose(1, 0, 2), feat, 0, 0, tiled=True
    )
    blocks_a, blocks_b = ring(mask_a, "z"), ring(mask_b, "x")
    table = call(orient_kernel, shape((1, 256), I32), [VMEM], flops=300_000_000)(small)

    weight = lax.dynamic_slice(first_weight, (0, z * 256), (96, 256))
    weight = jnp.stack([weight, lax.ppermute(weight, "c", [(0, 1), (1, 0)])])
    weights = ring(weight, "y")
    table, *blocks = lax.optimization_barrier((table, *blocks_a, *blocks_b))
    pair_a, pair_b = shape((512, 384), BF), shape((256, 384), BF)
    sent_a = call(functools.partial(select_kernel, 0), (pair_a, pair_a), [VMEM] * 4 + [SMEM] * 2, moved=2_000_000)(
        *blocks[:4], table, at
    )
    sent_b = call(functools.partial(select_kernel, 1), (pair_b, pair_b), [VMEM] * 4 + [SMEM] * 2, moved=2_000_000)(
        *blocks[4:], table, at
    )
    masks = rounds(*sent_a, "x") + rounds(*sent_b, "z")
    x_wide = rounds(x_own[:4], x_own[4:], "z")
    own_second = lax.dynamic_slice(second_weight, ((z * 4 + x) * 64, 0), (64, 153))
    own_second = jnp.pad(own_second, ((0, 0), (0, 7)))
    part = shape((4, 64, 256), BF)
    v = call(
        project_kernel,
        (part,) * 4,
        [VMEM] * 13 + [SMEM],
        [pltpu.VMEM((8, 96, 256), BF), pltpu.VMEM((4, 256, 256), BF)],
        flops=400_000_000,
        moved=3_000_000,
    )(*x_wide, *weights, small, at)
    v = [v[0]] + [fetch(value, "x", -shift) for value, shift in zip(v[1:], RING[1:])]
    hid, second, *g = call(
        mix_kernel,
        (shape((16, 64, 256), BF), shape((80, 128), BF)) + (part,) * 4,
        [VMEM] * 5 + [SMEM, VMEM, SMEM] + [ANY] * 16,
        [
            pltpu.VMEM((8, 512, 384), BF),
            pltpu.VMEM((8, 256, 384), BF),
            pltpu.VMEM((32, 224, 128), BF),
            pltpu.VMEM((32, 224, 128), F32),
            pltpu.VMEM((32, 64, 128), BF),
            pltpu.VMEM((32, 64, 128), F32),
            pltpu.VMEM((32, 1, 128), F32),
            pltpu.SemaphoreType.DMA((16,)),
        ],
        flops=1_600_000_000,
        moved=10_000_000,
    )(*v, small, table, own_second, at, *masks)
    g = [g[0]] + [fetch(value, "x", -shift) for value, shift in zip(g[1:], RING[1:])]
    other = lax.ppermute(second, "c", [(0, 1), (1, 0)])
    second = ring((second.astype(F32) + other.astype(F32)).astype(BF), "y")
    *g, second[1], second[2], second[3] = lax.optimization_barrier((*g, *second[1:]))
    part = call(
        weigh_kernel,
        shape((8, 4, 48, 128), BF),
        [VMEM] * 12 + [SMEM],
        flops=400_000_000,
        moved=3_000_000,
    )(*x_wide, *g, at)
    part = lax.all_to_all(part.reshape(32, 48, 128), ("y", "c", "x"), 0, 0, tiled=True)
    done = call(add_kernel, shape((16, 256, 128), BF), [VMEM] * 6, moved=3_000_000)(part, *second, hid)
    done = lax.all_to_all(done, dom, 0, 0, tiled=True)
    hidden, grad_first, grad_second = call(
        final_kernel,
        (shape((256, 1024), BF), shape((96, 1024), F32), shape((153, 1024), F32)),
        [VMEM],
        moved=2_500_000,
    )(done)
    return (hidden[None], grad_first, grad_second.T)


def solution(mesh):
    wide = Mesh(mesh.devices.reshape(4, 2, 4, 4), ("y", "c", "x", "z"))
    feat, dom = ("y", "c"), ("x", "z")
    placed = (
        P(feat, dom, None),
        P(feat, None),
        P(),
        P(dom, feat),
        P(dom, feat, None),
        P(dom, feat, None, None, None),
        P(dom, feat, None),
    )
    return jax.shard_map(
        body,
        mesh=wide,
        in_specs=placed,
        out_specs=(P(dom, feat, None), P(feat, None), P()),
        check_vma=False,
    )
```

```python
import functools

import jax
import jax.numpy as jnp
from jax import lax
from jax.experimental import pallas as pl
from jax.experimental.pallas import tpu as pltpu
from jax.sharding import Mesh
from jax.sharding import PartitionSpec as P

BF = jnp.bfloat16
F32 = jnp.float32
I32 = jnp.int32
VMEM = pl.BlockSpec(memory_space=pltpu.VMEM)
SMEM = pl.BlockSpec(memory_space=pltpu.SMEM)
MIB = 1024 * 1024
RING = (0, 1, -1, 2)
NT = (((1,), (1,)), ((), ()))


def dot(a, b, dims=(((1,), (0,)), ((), ()))):
    return lax.dot_general(a, b, dims, preferred_element_type=F32)


def columns_of(row):
    return jnp.broadcast_to(row, (128, 128)).T


def halves(a, b):
    low = lax.broadcasted_iota(I32, a.shape, 1) < 64
    return jnp.where(low, a, pltpu.roll(b, 64, 1)), jnp.where(low, pltpu.roll(a, 64, 1), b)


def owner(block):
    return (block % 4) * 4 + block // 4


def orient_kernel(small_ref, table_ref):
    links = small_ref[0, 2:4, :]
    for d in range(1, 16):
        links = links + small_ref[d, 2:4, :]
    links = links.astype(F32)
    row = jnp.concatenate([links[0:1], links[1:2]], axis=1)
    side = jnp.concatenate([columns_of(links[0:1]), columns_of(links[1:2])], axis=0)
    link_r = jnp.broadcast_to(row, (256, 256)) - 2.0
    link_c = jnp.concatenate([side, side], axis=1) - 2.0
    index_c = lax.broadcasted_iota(I32, (256, 256), 0)
    index_r = lax.broadcasted_iota(I32, (256, 256), 1)
    block_c = ((index_c * 10923) >> 16).astype(F32)
    block_r = ((index_r * 10923) >> 16).astype(F32)
    opposite = (link_c == block_r) & (link_r == block_c)
    paired = ((index_c ^ 1) == index_r) & (link_c >= 0.0) & (link_r >= 0.0)
    opposite = jnp.where(opposite, 1.0, 0.0)
    paired = jnp.where(paired, 1.0, 0.0)
    near = dot(paired.astype(BF), opposite.astype(BF)) + dot(opposite.astype(BF), paired.astype(BF))
    reach = jnp.where((near > 0.0) | (index_c == index_r), 1.0, 0.0).astype(BF)
    for _ in range(7):
        reach = jnp.where(dot(reach, reach) > 0.0, 1.0, 0.0).astype(BF)
    reach = reach.astype(F32)
    label_c = jnp.min(jnp.where(reach > 0.0, index_r.astype(F32), 999.0), axis=1, keepdims=True)
    label_r = jnp.min(jnp.where(reach > 0.0, index_c.astype(F32), 999.0), axis=0, keepdims=True)
    other_r = jnp.sum(opposite * label_c, axis=0, keepdims=True)
    sends_r = (label_r < other_r) & (row >= 2.0)
    table_ref[...] = jnp.where(sends_r, row - 1.0, 0.0).astype(I32)


def mask_kernel(mask_ref, up_ref, a_ref, b_ref):
    for b, out_ref in enumerate((a_ref, b_ref)):
        for k in range(6):
            out_ref[0:128, k * 128 : k * 128 + 128] = mask_ref[b, k].astype(F32).astype(BF)
    a_ref[128:192, 0:256] = up_ref[0:64, :]
    a_ref[128:192, 256:512] = up_ref[64:128, :]
    rest = jnp.concatenate([up_ref[128:153, :].astype(F32), jnp.zeros((39, 256), F32)], axis=0)
    a_ref[128:192, 512:768] = rest.astype(BF)


def select_kernel(which, *refs):
    far = jnp.concatenate([refs[3][...], refs[4][...]], axis=0)
    blocks, table_ref, at_ref, out_ref = refs[:3] + (far,), refs[5], refs[6], refs[7]
    height = out_ref.shape[0] // 4
    for k, block in enumerate(blocks):
        if which == 0:
            d = at_ref[1] * 4 + (at_ref[2] + RING[k] + 4) % 4
        else:
            d = ((at_ref[1] + RING[k] + 4) % 4) * 4 + at_ref[2]
        base = k * height
        for m in range(3):
            at = d * 12 + which * 6 + m * 2
            first = jnp.where(table_ref[0, at] > 0, 1.0, 0.0)
            second = jnp.where(table_ref[0, at + 1] > 0, 1.0, 0.0)
            one = block[0:128, m * 256 : m * 256 + 128].astype(F32)
            two = block[0:128, m * 256 + 128 : m * 256 + 256].astype(F32)
            out_ref[base : base + 128, m * 128 : m * 128 + 128] = (first * one + second * two).astype(BF)
        if which == 0:
            out_ref[base + 128 : base + 192, :] = block[128:192, 0:384]
            out_ref[base + 192 : base + 256, :] = block[128:192, 384:768]


def features_at(refs, k, f):
    return refs[k][f] if k < 3 else refs[3 + f // 4][f % 4]


def project_kernel(*refs):
    x_refs, w_refs, small_ref, at_ref = refs[:5], refs[5:9], refs[9], refs[10]
    v_refs, w_ref, t_ref = refs[11:15], refs[15], refs[16]
    for k, shift in enumerate(RING):
        for flip in range(2):
            f = ((at_ref[3] + shift + 4) % 4) * 2 + (at_ref[4] + flip) % 2
            w_ref[f] = w_refs[k][flip]
    w = w_ref[...].reshape(768, 256).astype(F32).T.astype(BF)
    for k, shift in enumerate(RING):
        z = (at_ref[2] + shift + 4) % 4
        degree = small_ref[at_ref[1] * 4 + z].astype(F32)
        inv = lax.rsqrt(jnp.concatenate([degree[0:1], degree[1:2]], axis=1))
        whole = jnp.concatenate([features_at(x_refs, k, f) for f in range(8)], axis=0)
        t_ref[k] = (inv * dot(w, whole)).astype(BF)
        for v_ref, to in zip(v_refs, RING):
            at = pl.multiple_of(((at_ref[1] + to + 4) % 4) * 64, 64)
            v_ref[z] = t_ref[k, pl.ds(at, 64), :]


def mix_kernel(*refs):
    v_refs, small_ref, tab_ref, sw_ref, at_ref = refs[:4], refs[4], refs[5], refs[6], refs[7]
    a_refs, b_refs = refs[8:13], refs[13:18]
    hid_ref, second_ref, g_refs = refs[18], refs[19], refs[20:24]
    src_ref, acc_ref, v2_ref, acc2_ref, inv_ref = refs[24:]
    x, z = at_ref[1], at_ref[2]

    def along(step):
        for buffer, first, count in ((0, 0, 4), (1, 0, 4), (2, 0, 4), (3, 0, 2), (4, 2, 2)):
            def turn(k, carry, buffer=buffer, first=first):
                q = k + first
                step(a_refs[buffer], b_refs[buffer], k, min(buffer, 3), q ^ (q >> 1))
                return carry
            lax.fori_loop(0, count, turn, 0)

    for d in range(16):
        degree = small_ref[d].astype(F32)
        for h in range(2):
            inv_ref[2 * d + h] = lax.rsqrt(degree[h : h + 1])

    def prepare(a_ref, b_ref, k, n, shift):
        to = (z + shift) & 3
        d = ((x + RING[n] + 4) & 3) * 4 + to
        v_ref = v_refs[(0, 2, 1, 3)[n]]
        low = a_ref[pl.ds(pl.multiple_of(k * 256 + 128, 64), 64), :]
        high = a_ref[pl.ds(pl.multiple_of(k * 256 + 192, 64), 64), :]
        for h in range(2):
            t = d * 2 + h
            inv = inv_ref[t]
            middle = low[:, 256:384] if h == 0 else high[:, 0:128]
            parts = [low[:, h * 128 : h * 128 + 128], middle, high[0:32, 128 + h * 128 : 256 + h * 128]]
            up = (inv * jnp.concatenate(parts, axis=0).astype(F32)).astype(BF)
            own = jnp.concatenate([v_ref[to, :, h * 128 : h * 128 + 128], up], axis=0)
            src_ref[t] = own
            acc_ref[t] = own.astype(F32)

    along(prepare)

    def spread(source, total_ref):
        def send(t, weights):
            named = []
            for m in range(3):
                c = tab_ref[0, 6 * t + 2 * m] + tab_ref[0, 6 * t + 2 * m + 1]
                named.append(jnp.maximum(c - 1, 0))
            own = source[t]
            others = jnp.concatenate([source[c] for c in named], axis=1)
            return named, dot(own, weights), dot(others, weights, NT)

        def both(a_ref, b_ref, k, n, shift):
            t_a = (((x + RING[n] + 4) & 3) * 4 + ((z + shift) & 3)) * 2
            t_b = (((x + shift) & 3) * 4 + ((z + RING[n] + 4) & 3)) * 2 + 1
            sent = [
                (t_a, *send(t_a, a_ref[pl.ds(pl.multiple_of(k * 256, 128), 128), :])),
                (t_b, *send(t_b, b_ref[pl.ds(pl.multiple_of(k * 128, 128), 128), :])),
            ]
            for t, named, back, forth in sent:
                total_ref[t] = total_ref[t] + forth
                for m in range(3):
                    total_ref[named[m]] = total_ref[named[m]] + back[:, m * 128 : m * 128 + 128]

        along(both)

    spread(src_ref, acc_ref)

    def turn(d, second):
        ones, pulls = [], []
        for h in range(2):
            t = d * 2 + h
            inv = inv_ref[t]
            m = inv * acc_ref[t, 0:64]
            s = jax.nn.sigmoid(m)
            hid = (m * s).astype(BF)
            hid_ref[d, :, h * 128 : h * 128 + 128] = hid
            ones.append((inv * hid.astype(F32)).astype(BF))
            pull = acc_ref[t, 64:224].astype(BF)
            pulls.append(pull)
            slope = s * (1.0 + m * (1.0 - s))
            back = (inv * inv * dot(sw_ref[...], pull) * slope).astype(BF)
            v2_ref[t] = back
            acc2_ref[t] = back.astype(F32)
        return second + dot(jnp.concatenate(pulls, axis=1), jnp.concatenate(ones, axis=1), NT)

    second = lax.fori_loop(0, 16, turn, jnp.zeros((160, 64), F32))
    second_ref[...] = jnp.concatenate([second[:80], second[80:]], axis=1).astype(BF)
    spread(v2_ref, acc2_ref)
    for shift, g_ref in zip(RING, g_refs):
        for k in range(4):
            d = ((x + shift + 4) & 3) * 4 + k
            for h in range(2):
                g_ref[k, :, h * 128 : h * 128 + 128] = (
                    inv_ref[d * 2 + h] * acc2_ref[d * 2 + h]
                ).astype(BF)


def weigh_kernel(*refs):
    x_refs, g_refs, at_ref, out_ref = refs[:5], refs[5:9], refs[9], refs[10]
    rights = []
    for shift in RING:
        z = (at_ref[2] + shift + 4) % 4
        rights.append(jnp.concatenate([g[z] for g in g_refs], axis=0))
    for f in range(8):
        acc = jnp.zeros((96, 256), F32)
        for k, right in enumerate(rights):
            acc = acc + dot(features_at(x_refs, k, f), right, NT)
        for p in range(2):
            g = acc[:, p * 128 : p * 128 + 128]
            for part, shift in zip(halves(g[:48], g[48:]), RING[2 * p : 2 * p + 2]):
                out_ref[f, (at_ref[1] - shift + 4) % 4] = part.astype(BF)


def add_kernel(part_ref, s0_ref, s1_ref, s2_ref, s3_ref, hid_ref, out_ref):
    first = part_ref[0].astype(F32)
    for i in range(1, 32):
        first = first + part_ref[i].astype(F32)
    second = s0_ref[...].astype(F32)
    for ref in (s1_ref, s2_ref, s3_ref):
        second = second + ref[...].astype(F32)
    both = jnp.concatenate([first, second], axis=0).astype(BF)
    for d in range(16):
        out_ref[d, 0:128] = both
        out_ref[d, 128:192] = hid_ref[d, :, 0:128]
        out_ref[d, 192:256] = hid_ref[d, :, 128:256]


def final_kernel(in_ref, hidden_ref, first_ref, second_ref):
    for j in range(8):
        cols = pl.ds(j * 128, 128)
        even, odd = owner(2 * j), owner(2 * j + 1)
        one, two = halves(in_ref[even, 0:128].astype(F32), in_ref[odd, 0:128].astype(F32))
        first_ref[0:48, cols] = one[:48]
        first_ref[48:96, cols] = two[:48]
        second_ref[0:80, cols] = one[48:]
        second_ref[80:153, cols] = two[48:121]
        for h in range(2):
            rows = pl.ds(128 + h * 64, 64)
            both = jnp.concatenate([in_ref[even, rows], in_ref[odd, rows]], axis=0)
            hidden_ref[h * 128 : h * 128 + 128, cols] = both.astype(F32).T.astype(BF)


def call(kernel, shape, specs, scratch=(), flops=0, moved=0, limit=8):
    return pl.pallas_call(
        kernel,
        out_shape=shape,
        in_specs=specs,
        out_specs=jax.tree.map(lambda _: VMEM, shape),
        scratch_shapes=list(scratch),
        compiler_params=pltpu.CompilerParams(vmem_limit_bytes=limit * MIB),
        cost_estimate=pl.CostEstimate(flops=flops, bytes_accessed=moved, transcendentals=0),
    )


def fetch(value, axis, shift):
    return lax.ppermute(value, axis, [((i + shift) % 4, i) for i in range(4)])


def ring(value, axis):
    return [value] + [fetch(value, axis, shift) for shift in RING[1:]]


def rounds(value, axis):
    half = value.shape[0] // 2
    after, before = fetch(value, axis, 1), fetch(value, axis, -1)
    return [value, after, before, fetch(after[:half], axis, 1), fetch(before[half:], axis, -1)]


def body(features, first_weight, second_weight, degree, neighbour_block, neighbour_mask, upstream):
    feat, dom = ("y", "c"), ("x", "z")
    shape = jax.ShapeDtypeStruct
    x, z = lax.axis_index("x"), lax.axis_index("z")
    at = jnp.stack([x * 4 + z, x, z, lax.axis_index("y"), lax.axis_index("c")])
    x_own = lax.all_to_all(
        features.reshape(96, 8, 256).transpose(1, 0, 2), feat, 0, 0, tiled=True
    )
    mask_a, mask_b = call(
        mask_kernel, (shape((192, 768), BF), shape((128, 768), BF)), [VMEM] * 2, moved=1_200_000
    )(neighbour_mask[0], upstream[0].T)
    links = lax.dynamic_update_slice(
        jnp.zeros((256,), I32), neighbour_block.reshape(12) + 2, ((x * 4 + z) * 12,)
    )
    small = jnp.concatenate([degree.reshape(2, 128), links.reshape(2, 128)], axis=0)
    small = jnp.broadcast_to(small, (16, 4, 128))
    small, x_own = lax.optimization_barrier((small, x_own))
    small = lax.all_to_all(small, dom, 0, 0, tiled=True)
    blocks_a, blocks_b = rounds(mask_a, "z"), rounds(mask_b, "x")
    x_wide = rounds(x_own, "z")
    table = call(orient_kernel, shape((1, 256), I32), [VMEM], flops=300_000_000)(small)

    weight = lax.dynamic_slice(first_weight, (0, z * 256), (96, 256))
    weight = jnp.stack([weight, lax.ppermute(weight, "c", [(0, 1), (1, 0)])])
    weights = ring(weight, "y")
    sent_a = call(
        functools.partial(select_kernel, 0), shape((1024, 384), BF), [VMEM] * 5 + [SMEM] * 2,
        moved=2_000_000,
    )(*blocks_a, table, at)
    sent_b = call(
        functools.partial(select_kernel, 1), shape((512, 384), BF), [VMEM] * 5 + [SMEM] * 2,
        moved=2_000_000,
    )(*blocks_b, table, at)
    masks = rounds(sent_a, "x") + rounds(sent_b, "z")
    own_second = lax.dynamic_slice(second_weight, ((z * 4 + x) * 64, 0), (64, 153))
    own_second = jnp.pad(own_second, ((0, 0), (0, 7)))
    part = shape((4, 64, 256), BF)
    v = call(
        project_kernel,
        (part,) * 4,
        [VMEM] * 10 + [SMEM],
        [pltpu.VMEM((8, 96, 256), BF), pltpu.VMEM((4, 256, 256), BF)],
        flops=400_000_000,
        moved=3_000_000,
    )(*x_wide, *weights, small, at)
    v = [v[0]] + [fetch(value, "x", -shift) for value, shift in zip(v[1:], RING[1:])]
    hid, second, *g = call(
        mix_kernel,
        (shape((16, 64, 256), BF), shape((80, 128), BF)) + (part,) * 4,
        [VMEM] * 5 + [SMEM, VMEM, SMEM] + [VMEM] * 10,
        [
            pltpu.VMEM((32, 224, 128), BF),
            pltpu.VMEM((32, 224, 128), F32),
            pltpu.VMEM((32, 64, 128), BF),
            pltpu.VMEM((32, 64, 128), F32),
            pltpu.VMEM((32, 1, 128), F32),
        ],
        flops=1_600_000_000,
        moved=10_000_000,
        limit=24,
    )(*v, small, table, own_second, at, *masks)
    g = [g[0]] + [fetch(value, "x", -shift) for value, shift in zip(g[1:], RING[1:])]
    other = lax.ppermute(second, "c", [(0, 1), (1, 0)])
    second = ring((second.astype(F32) + other.astype(F32)).astype(BF), "y")
    *g, second[1], second[2], second[3] = lax.optimization_barrier((*g, *second[1:]))
    part = call(
        weigh_kernel,
        shape((8, 4, 48, 128), BF),
        [VMEM] * 9 + [SMEM],
        flops=400_000_000,
        moved=3_000_000,
    )(*x_wide, *g, at)
    part = lax.all_to_all(part.reshape(32, 48, 128), ("y", "c", "x"), 0, 0, tiled=True)
    done = call(add_kernel, shape((16, 256, 128), BF), [VMEM] * 6, moved=3_000_000)(part, *second, hid)
    done = lax.all_to_all(done, dom, 0, 0, tiled=True)
    hidden, grad_first, grad_second = call(
        final_kernel,
        (shape((256, 1024), BF), shape((96, 1024), F32), shape((153, 1024), F32)),
        [VMEM],
        moved=2_500_000,
    )(done)
    return (hidden[None], grad_first, grad_second.T)


def solution(mesh):
    wide = Mesh(mesh.devices.reshape(4, 2, 4, 4), ("y", "c", "x", "z"))
    feat, dom = ("y", "c"), ("x", "z")
    placed = (
        P(feat, dom, None),
        P(feat, None),
        P(),
        P(dom, feat),
        P(dom, feat, None),
        P(dom, feat, None, None, None),
        P(dom, feat, None),
    )
    return jax.shard_map(
        body,
        mesh=wide,
        in_specs=placed,
        out_specs=(P(dom, feat, None), P(feat, None), P()),
        check_vma=False,
    )
```

```python
import jax
import jax.numpy as jnp
from jax import lax
from jax.experimental import pallas as pl
from jax.experimental.pallas import tpu as pltpu
from jax.sharding import Mesh
from jax.sharding import PartitionSpec as P

BF = jnp.bfloat16
F32 = jnp.float32
I32 = jnp.int32
VMEM = pl.BlockSpec(memory_space=pltpu.VMEM)
SMEM = pl.BlockSpec(memory_space=pltpu.SMEM)
MIB = 1024 * 1024
RING = (0, 1, -1, 2)
NT = (((1,), (1,)), ((), ()))


def dot(a, b, dims=(((1,), (0,)), ((), ()))):
    return lax.dot_general(a, b, dims, preferred_element_type=F32)


def columns_of(row):
    return jnp.broadcast_to(row, (128, 128)).T


def halves(a, b):
    low = lax.broadcasted_iota(I32, a.shape, 1) < 64
    return jnp.where(low, a, pltpu.roll(b, 64, 1)), jnp.where(low, pltpu.roll(a, 64, 1), b)


def owner(block):
    return (block % 4) * 4 + block // 4


def mask_kernel(mask_ref, up_ref, a_ref, b_ref):
    for b, out_ref in enumerate((a_ref, b_ref)):
        for k in range(6):
            out_ref[0:128, k * 128 : k * 128 + 128] = mask_ref[b, k].astype(F32).astype(BF)
    a_ref[128:192, 0:256] = up_ref[0:64, :]
    a_ref[128:192, 256:512] = up_ref[64:128, :]
    rest = jnp.concatenate([up_ref[128:153, :].astype(F32), jnp.zeros((39, 256), F32)], axis=0)
    a_ref[128:192, 512:768] = rest.astype(BF)


def pack_kernel(a_ref, b_ref, c_ref, d_ref, low_ref, high_ref):
    half = a_ref.shape[0]
    low_ref[0:half] = a_ref[...]
    low_ref[half:] = b_ref[...]
    high_ref[0:half] = c_ref[...]
    high_ref[half:] = d_ref[...]


def features_at(refs, k, f):
    return refs[k][f] if k < 3 else refs[3 + f // 4][f % 4]


def project_kernel(*refs):
    x_refs, w_refs, small_ref, at_ref = refs[:5], refs[5:9], refs[9], refs[10]
    v_refs, w_ref, t_ref = refs[11:15], refs[15], refs[16]
    for k, shift in enumerate(RING):
        for flip in range(2):
            f = ((at_ref[3] + shift + 4) % 4) * 2 + (at_ref[4] + flip) % 2
            w_ref[f] = w_refs[k][flip]
    w = w_ref[...].reshape(768, 256).astype(F32).T.astype(BF)
    for k, shift in enumerate(RING):
        z = (at_ref[2] + shift + 4) % 4
        degree = small_ref[at_ref[1] * 4 + z].astype(F32)
        inv = lax.rsqrt(jnp.concatenate([degree[0:1], degree[1:2]], axis=1))
        whole = jnp.concatenate([features_at(x_refs, k, f) for f in range(8)], axis=0)
        t_ref[k] = (inv * dot(w, whole)).astype(BF)
        for v_ref, to in zip(v_refs, RING):
            at = pl.multiple_of(((at_ref[1] + to + 4) % 4) * 64, 64)
            v_ref[z] = t_ref[k, pl.ds(at, 64), :]


def mix_kernel(*refs):
    v_refs, small_ref, links_ref, sw_ref, at_ref = refs[:4], refs[4], refs[5], refs[6], refs[7]
    a_refs, b_refs = refs[8:16], refs[16:24]
    hid_ref, second_ref, g_refs = refs[24], refs[25], refs[26:30]
    src_ref, v2_ref, inv_ref = refs[30:]
    places = []
    for i, dx in enumerate(RING):
        for j, dz in enumerate(RING):
            places.append((i, j, ((at_ref[1] + dx + 4) & 3) * 4 + ((at_ref[2] + dz + 4) & 3)))

    for d in range(16):
        degree = small_ref[d].astype(F32)
        for h in range(2):
            inv_ref[2 * d + h] = lax.rsqrt(degree[h : h + 1])
    for i, j, d in places:
        a_ref, base = a_refs[2 * i + j // 2], (j % 2) * 192 + 128
        v_ref = v_refs[(0, 2, 1, 3)[i]]
        to = (at_ref[2] + RING[j] + 4) & 3
        for h in range(2):
            t = d * 2 + h
            inv = inv_ref[t]
            src_ref[t, 0:64] = v_ref[to, :, h * 128 : h * 128 + 128]
            for c in range(3):
                rows = min(64, 160 - 64 * c)
                up = a_ref[base : base + rows, c * 256 + h * 128 : c * 256 + h * 128 + 128]
                src_ref[t, 64 + 64 * c : 64 + 64 * c + rows] = (inv * up.astype(F32)).astype(BF)

    def spread(i, j, d, h, source):
        if h == 0:
            weights = a_refs[2 * i + j // 2][(j % 2) * 192 : (j % 2) * 192 + 128, :]
        else:
            weights = b_refs[2 * j + i // 2][(i % 2) * 128 : (i % 2) * 128 + 128, :]
        named = [source[links_ref[d, 2, h * 6 + k]] for k in range(6)]
        return source[d * 2 + h].astype(F32) + dot(jnp.concatenate(named, axis=1), weights, NT)

    second = jnp.zeros((160, 64), F32)
    for i, j, d in places:
        ones, pulls = [], []
        for h in range(2):
            t = d * 2 + h
            inv = inv_ref[t]
            total = spread(i, j, d, h, src_ref)
            m = inv * total[0:64]
            s = jax.nn.sigmoid(m)
            hid = (m * s).astype(BF)
            hid_ref[d, :, h * 128 : h * 128 + 128] = hid
            ones.append((inv * hid.astype(F32)).astype(BF))
            pull = total[64:224].astype(BF)
            pulls.append(pull)
            slope = s * (1.0 + m * (1.0 - s))
            v2_ref[t] = (inv * inv * dot(sw_ref[...], pull) * slope).astype(BF)
        second = second + dot(jnp.concatenate(pulls, axis=1), jnp.concatenate(ones, axis=1), NT)
    second_ref[...] = jnp.concatenate([second[:80], second[80:]], axis=1).astype(BF)
    for i, j, d in places:
        to = (at_ref[2] + RING[j] + 4) & 3
        for h in range(2):
            g = inv_ref[d * 2 + h] * spread(i, j, d, h, v2_ref)
            g_refs[i][to, :, h * 128 : h * 128 + 128] = g.astype(BF)


def turn_kernel(in_ref, out_ref):
    for d in range(16):
        block = in_ref[d].astype(F32)
        both = jnp.concatenate([block[:, 0:128], block[:, 128:256]], axis=0)
        out_ref[d] = both.T.astype(BF)


def weigh_kernel(*refs):
    x_refs, g_refs, at_ref, out_ref = refs[:5], refs[5:9], refs[9], refs[10]
    rights = []
    for shift in RING:
        z = (at_ref[2] + shift + 4) % 4
        rights.append(jnp.concatenate([g[z] for g in g_refs], axis=0))
    for f in range(8):
        acc = jnp.zeros((96, 256), F32)
        for k, right in enumerate(rights):
            acc = acc + dot(features_at(x_refs, k, f), right, NT)
        for p in range(2):
            g = acc[:, p * 128 : p * 128 + 128]
            for part, shift in zip(halves(g[:48], g[48:]), RING[2 * p : 2 * p + 2]):
                out_ref[f, (at_ref[1] - shift + 4) % 4] = part.astype(BF)


def add_kernel(part_ref, s0_ref, s1_ref, s2_ref, s3_ref, out_ref):
    first = part_ref[0].astype(F32)
    for i in range(1, 32):
        first = first + part_ref[i].astype(F32)
    second = s0_ref[...].astype(F32)
    for ref in (s1_ref, s2_ref, s3_ref):
        second = second + ref[...].astype(F32)
    both = jnp.concatenate([first, second], axis=0).astype(BF)
    for d in range(16):
        out_ref[d] = both


def hidden_kernel(in_ref, out_ref):
    for j in range(8):
        cols = pl.ds(j * 128, 128)
        one, two = halves(in_ref[owner(2 * j)].astype(F32), in_ref[owner(2 * j + 1)].astype(F32))
        out_ref[0:128, cols] = one.astype(BF)
        out_ref[128:256, cols] = two.astype(BF)


def gradient_kernel(in_ref, first_ref, second_ref):
    for j in range(8):
        cols = pl.ds(j * 128, 128)
        one, two = halves(in_ref[owner(2 * j)].astype(F32), in_ref[owner(2 * j + 1)].astype(F32))
        first_ref[0:48, cols] = one[:48]
        first_ref[48:96, cols] = two[:48]
        second_ref[0:80, cols] = one[48:]
        second_ref[80:153, cols] = two[48:121]


def call(kernel, shape, specs, scratch=(), flops=0, moved=0, limit=8):
    return pl.pallas_call(
        kernel,
        out_shape=shape,
        in_specs=specs,
        out_specs=jax.tree.map(lambda _: VMEM, shape),
        scratch_shapes=list(scratch),
        compiler_params=pltpu.CompilerParams(vmem_limit_bytes=limit * MIB),
        cost_estimate=pl.CostEstimate(flops=flops, bytes_accessed=moved, transcendentals=0),
    )


def fetch(value, axis, shift):
    return lax.ppermute(value, axis, [((i + shift) % 4, i) for i in range(4)])


def ring(value, axis):
    return [value] + [fetch(value, axis, shift) for shift in RING[1:]]


def pack(blocks):
    pair = jax.ShapeDtypeStruct((2 * blocks[0].shape[0], 768), BF)
    return call(pack_kernel, (pair, pair), [VMEM] * 4, moved=2_000_000)(*blocks)


def neighbours(low, high, axis):
    after, before = fetch(low, axis, 1), fetch(high, axis, -1)
    return [after, fetch(high, axis, 1), fetch(low, axis, -1), before]


def body(features, first_weight, second_weight, degree, neighbour_block, neighbour_mask, upstream):
    feat, dom = ("y", "c"), ("x", "z")
    shape = jax.ShapeDtypeStruct
    x, z = lax.axis_index("x"), lax.axis_index("z")
    at = jnp.stack([x * 4 + z, x, z, lax.axis_index("y"), lax.axis_index("c")])
    x_own = lax.all_to_all(
        features.reshape(96, 8, 256).transpose(1, 0, 2), feat, 0, 0, tiled=True
    )
    mask_a, mask_b = call(
        mask_kernel, (shape((192, 768), BF), shape((128, 768), BF)), [VMEM] * 2, moved=1_200_000
    )(neighbour_mask[0], upstream[0].T)
    weight = lax.dynamic_slice(first_weight, (0, z * 256), (96, 256))
    other = lax.ppermute(weight, "c", [(0, 1), (1, 0)])
    *blocks, other = lax.optimization_barrier((*ring(mask_a, "z"), *ring(mask_b, "x"), other))
    own_a, own_b = pack(blocks[:4]), pack(blocks[4:])
    weights = ring(jnp.stack([weight, other]), "y")
    links = jnp.pad(jnp.maximum(neighbour_block.reshape(12), 0), (0, 244))
    small = jnp.concatenate([degree.reshape(2, 128), links.reshape(2, 128)], axis=0)
    small = jnp.broadcast_to(small, (16, 4, 128))
    small, x_own = lax.optimization_barrier((small, x_own))
    small = lax.all_to_all(small, dom, 0, 0, tiled=True)
    near_a, near_b = neighbours(*own_a, "x"), neighbours(*own_b, "z")
    x_after, x_before = fetch(x_own, "z", 1), fetch(x_own, "z", -1)
    a0, a3, b0, b3, x_after, x_before, small = lax.optimization_barrier(
        (near_a[0], near_a[3], near_b[0], near_b[3], x_after, x_before, small)
    )
    x_wide = [x_own, x_after, x_before, fetch(x_after[:4], "z", 1), fetch(x_before[4:], "z", -1)]
    masks = [*own_a, a0, *near_a[1:3], a3, fetch(a0, "x", 1), fetch(a3, "x", -1)]
    masks += [*own_b, b0, *near_b[1:3], b3, fetch(b0, "z", 1), fetch(b3, "z", -1)]
    own_second = lax.dynamic_slice(second_weight, ((z * 4 + x) * 64, 0), (64, 153))
    own_second = jnp.pad(own_second, ((0, 0), (0, 7)))
    part = shape((4, 64, 256), BF)
    v = call(
        project_kernel,
        (part,) * 4,
        [VMEM] * 10 + [SMEM],
        [pltpu.VMEM((8, 96, 256), BF), pltpu.VMEM((4, 256, 256), BF)],
        flops=400_000_000,
        moved=3_000_000,
    )(*x_wide, *weights, small, at)
    v = [v[0]] + [fetch(value, "x", -shift) for value, shift in zip(v[1:], RING[1:])]
    hid, second, *g = call(
        mix_kernel,
        (shape((16, 64, 256), BF), shape((80, 128), BF)) + (part,) * 4,
        [VMEM] * 5 + [SMEM, VMEM, SMEM] + [VMEM] * 16,
        [
            pltpu.VMEM((32, 224, 128), BF),
            pltpu.VMEM((32, 64, 128), BF),
            pltpu.VMEM((32, 1, 128), F32),
        ],
        flops=1_600_000_000,
        moved=10_000_000,
        limit=20,
    )(*v, small, small, own_second, at, *masks)
    g = [g[0]] + [fetch(value, "x", -shift) for value, shift in zip(g[1:], RING[1:])]
    other = lax.ppermute(second, "c", [(0, 1), (1, 0)])
    hid, other = lax.optimization_barrier((hid, other))
    tile = shape((16, 128, 128), BF)
    hid = call(turn_kernel, tile, [VMEM], moved=1_000_000)(hid)
    hid = lax.all_to_all(hid, dom, 0, 0, tiled=True)
    second = ring((second.astype(F32) + other.astype(F32)).astype(BF), "y")
    part = call(
        weigh_kernel,
        shape((8, 4, 48, 128), BF),
        [VMEM] * 9 + [SMEM],
        flops=400_000_000,
        moved=3_000_000,
    )(*x_wide, *g, at)
    part, hid, *rest = lax.optimization_barrier((part, hid, *second[1:]))
    part = lax.all_to_all(part.reshape(32, 48, 128), ("y", "c", "x"), 0, 0, tiled=True)
    done = call(add_kernel, tile, [VMEM] * 5, moved=1_000_000)(part, second[0], *rest)
    done = lax.all_to_all(done, dom, 0, 0, tiled=True)
    hidden = call(hidden_kernel, shape((256, 1024), BF), [VMEM], moved=1_000_000)(hid)
    grad_first, grad_second = call(
        gradient_kernel, (shape((96, 1024), F32), shape((153, 1024), F32)), [VMEM], moved=1_500_000
    )(done)
    return (hidden[None], grad_first, grad_second.T)


def solution(mesh):
    wide = Mesh(mesh.devices.reshape(4, 2, 4, 4), ("y", "c", "x", "z"))
    feat, dom = ("y", "c"), ("x", "z")
    placed = (
        P(feat, dom, None),
        P(feat, None),
        P(),
        P(dom, feat),
        P(dom, feat, None),
        P(dom, feat, None, None, None),
        P(dom, feat, None),
    )
    return jax.shard_map(
        body,
        mesh=wide,
        in_specs=placed,
        out_specs=(P(dom, feat, None), P(feat, None), P()),
        check_vma=False,
    )
```

```python
import jax
import jax.numpy as jnp
from jax import lax
from jax.experimental import pallas as pl
from jax.experimental.pallas import tpu as pltpu
from jax.sharding import Mesh
from jax.sharding import PartitionSpec as P

BF = jnp.bfloat16
F32 = jnp.float32
I32 = jnp.int32
VMEM = pl.BlockSpec(memory_space=pltpu.VMEM)
SMEM = pl.BlockSpec(memory_space=pltpu.SMEM)
MIB = 1024 * 1024
RING = (0, 1, -1, 2)
NT = (((1,), (1,)), ((), ()))


def dot(a, b, dims=(((1,), (0,)), ((), ()))):
    return lax.dot_general(a, b, dims, preferred_element_type=F32)


def halves(a, b):
    low = lax.broadcasted_iota(I32, a.shape, 1) < 64
    return jnp.where(low, a, pltpu.roll(b, 64, 1)), jnp.where(low, pltpu.roll(a, 64, 1), b)


def owner(block):
    return (block % 4) * 4 + block // 4


def mask_kernel(mask_ref, up_ref, deg_ref, links_ref, out_ref):
    for b, at in enumerate((0, 192)):
        for k in range(6):
            out_ref[at : at + 128, k * 128 : k * 128 + 128] = mask_ref[b, k].astype(F32).astype(BF)
    out_ref[128:192, 0:256] = up_ref[0:64, :]
    out_ref[128:192, 256:512] = up_ref[64:128, :]
    rest = jnp.concatenate([up_ref[128:153, :].astype(F32), jnp.zeros((39, 256), F32)], axis=0)
    out_ref[128:192, 512:768] = rest.astype(BF)
    info = []
    for b in range(2):
        degree = deg_ref[b : b + 1, :]
        info += [degree >> 5, degree & 31]
    info = jnp.concatenate(info + [links_ref[...], jnp.zeros((11, 128), I32)], axis=0)
    out_ref[320:336, :] = jnp.zeros((16, 768), BF)
    out_ref[320:336, 0:128] = info.astype(F32).astype(BF)


def block_of(m_refs, k, b):
    if k < 3:
        return m_refs[k][b * 192 : b * 192 + 128, :]
    return m_refs[3 + b][0:128, :]


def info_of(m_refs, k):
    rows = m_refs[k][320:336, 0:128] if k < 3 else m_refs[4][128:144, 0:128]
    return rows.astype(F32)


def inverse_of(info, b):
    return lax.rsqrt(info[2 * b : 2 * b + 1] * 32.0 + info[2 * b + 1 : 2 * b + 2])


def upstream_kernel(*refs):
    m_refs, at_ref, out_ref = refs[:5], refs[5], refs[6]
    for k, shift in enumerate(RING):
        info = info_of(m_refs, k)
        inv = jnp.concatenate([inverse_of(info, 0), inverse_of(info, 1)], axis=1)
        z = (at_ref[2] + shift + 4) & 3
        for c in range(3):
            rows = min(64, 160 - 64 * c)
            up = m_refs[k][128 : 128 + rows, c * 256 : c * 256 + 256]
            out_ref[z, c * 64 : c * 64 + rows] = (inv * up.astype(F32)).astype(BF)


def features_at(refs, k, f):
    return refs[k][f] if k < 3 else refs[3 + f // 4][f % 4]


def project_kernel(*refs):
    x_refs, w_refs, m_refs, at_ref = refs[:5], refs[5:9], refs[9:14], refs[14]
    out_ref, w_ref = refs[15:]
    for k, shift in enumerate(RING):
        for flip in range(2):
            f = ((at_ref[3] + shift + 4) & 3) * 2 + ((at_ref[4] + flip) & 1)
            w_ref[f] = w_refs[k][flip]
    w = w_ref[...].reshape(768, 256).astype(F32).T.astype(BF)
    for k, shift in enumerate(RING):
        info = info_of(m_refs, k)
        inv = jnp.concatenate([inverse_of(info, 0), inverse_of(info, 1)], axis=1)
        whole = jnp.concatenate([features_at(x_refs, k, f) for f in range(8)], axis=0)
        out_ref[(at_ref[2] + shift + 4) & 3] = (inv * dot(w, whole)).astype(BF)


def collect(refs, base, src_ref, at_ref):
    rows = refs[0].shape[1]
    for i, ref in enumerate(refs):
        x = (at_ref[1] + RING[min(i, 3)] + 4) & 3
        for j in range(ref.shape[0]):
            d = x * 4 + (j + 2 if i == 4 else j)
            for h in range(2):
                src_ref[2 * d + h, base : base + rows] = ref[j, :, h * 128 : h * 128 + 128]


def scalars(m_refs, stage_ref, links_ref, sem):
    rows = [info_of(m_refs, k)[4:5] for k in range(4)]
    stage_ref[...] = jnp.concatenate(rows + [jnp.zeros((4, 128), F32)], axis=0).astype(I32)
    copy = pltpu.make_async_copy(stage_ref, links_ref, sem)
    copy.start()
    copy.wait()


def spread(src_ref, links_ref, m_refs, k, b, t):
    named = [src_ref[links_ref[k, b * 6 + s]] for s in range(6)]
    total = dot(jnp.concatenate(named, axis=1), block_of(m_refs, k, b), NT)
    return src_ref[t].astype(F32) + total


def first_mix_kernel(*refs):
    s_refs, u_refs, m_refs, sw_ref, at_ref = refs[:5], refs[5:10], refs[10:15], refs[15], refs[16]
    hid_refs, back_ref, second_ref = refs[17:21], refs[21], refs[22]
    src_ref, stage_ref, links_ref, sem = refs[23:]
    scalars(m_refs, stage_ref, links_ref, sem)
    collect(s_refs, 0, src_ref, at_ref)
    collect(u_refs, 256, src_ref, at_ref)
    second = jnp.zeros((160, 256), F32)
    for k, shift in enumerate(RING):
        z = (at_ref[2] + shift + 4) & 3
        info = info_of(m_refs, k)
        for b in range(2):
            inv = inverse_of(info, b)
            lanes = slice(b * 128, b * 128 + 128)
            total = spread(src_ref, links_ref, m_refs, k, b, (at_ref[1] * 4 + z) * 2 + b)
            m = inv * total[0:256]
            s = jax.nn.sigmoid(m)
            hid = (m * s).astype(BF)
            hid_refs[k][:, lanes] = hid
            one = (inv * hid.astype(F32)).astype(BF)
            pull = total[256:416].astype(BF)
            second = second + dot(pull, one, NT)
            slope = s * (1.0 + m * (1.0 - s))
            back_ref[z, :, lanes] = (inv * inv * dot(sw_ref[...], pull) * slope).astype(BF)
    second_ref[...] = second


def second_mix_kernel(*refs):
    b_refs, m_refs, x_refs, second_ref, at_ref = refs[:5], refs[5:10], refs[10:15], refs[15], refs[16]
    out_ref, src_ref, stage_ref, links_ref, sem = refs[17:]
    scalars(m_refs, stage_ref, links_ref, sem)
    collect(b_refs, 0, src_ref, at_ref)
    rights = []
    for k, shift in enumerate(RING):
        z = (at_ref[2] + shift + 4) & 3
        info = info_of(m_refs, k)
        parts = []
        for b in range(2):
            total = spread(src_ref, links_ref, m_refs, k, b, (at_ref[1] * 4 + z) * 2 + b)
            parts.append((inverse_of(info, b) * total).astype(BF))
        rights.append(jnp.concatenate(parts, axis=1))
    seconds = []
    for p in range(2):
        m = second_ref[:, p * 128 : p * 128 + 128]
        seconds += halves(m[:80], m[80:])
    for f in range(8):
        acc = jnp.zeros((96, 256), F32)
        for k, right in enumerate(rights):
            acc = acc + dot(features_at(x_refs, k, f), right, NT)
        for p in range(2):
            g = acc[:, p * 128 : p * 128 + 128]
            for q, part in enumerate(halves(g[:48], g[48:])):
                both = jnp.concatenate([part, seconds[2 * p + q]], axis=0)
                out_ref[f, 2 * p + q] = both.astype(BF)


def add_kernel(part_ref, out_ref):
    total = part_ref[0].astype(F32)
    for i in range(1, 32):
        total = total + part_ref[i].astype(F32)
    total = total.astype(BF)
    for d in range(16):
        out_ref[d] = total


def hidden_kernel(h0_ref, h1_ref, h2_ref, h3_ref, at_ref, out_ref):
    for ref, shift in zip((h0_ref, h1_ref, h2_ref, h3_ref), RING):
        at = pl.multiple_of(((at_ref[2] - shift + 4) & 3) * 256, 256)
        out_ref[:, pl.ds(at, 256)] = ref[...].astype(F32).T.astype(BF)


def gradient_kernel(in_ref, first_ref, second_ref):
    for j in range(8):
        cols = pl.ds(j * 128, 128)
        one, two = halves(in_ref[owner(2 * j)].astype(F32), in_ref[owner(2 * j + 1)].astype(F32))
        first_ref[0:48, cols] = one[:48]
        first_ref[48:96, cols] = two[:48]
        second_ref[0:80, cols] = one[48:]
        second_ref[80:153, cols] = two[48:121]


def call(kernel, shape, specs, scratch=(), flops=0, moved=0, limit=8):
    return pl.pallas_call(
        kernel,
        out_shape=shape,
        in_specs=specs,
        out_specs=jax.tree.map(lambda _: VMEM, shape),
        scratch_shapes=list(scratch),
        compiler_params=pltpu.CompilerParams(vmem_limit_bytes=limit * MIB),
        cost_estimate=pl.CostEstimate(flops=flops, bytes_accessed=moved, transcendentals=0),
    )


def fetch(value, axis, shift):
    return lax.ppermute(value, axis, [((i + shift) % 4, i) for i in range(4)])


def ring(value, axis):
    return [value] + [fetch(value, axis, shift) for shift in RING[1:]]


def near(value, axis):
    return fetch(value, axis, 1), fetch(value, axis, -1)


def rounds(value, axis, half):
    after, before = near(value, axis)
    return [value, after, before, fetch(after[:half], axis, 1), fetch(before[half:], axis, -1)]


def body(features, first_weight, second_weight, degree, neighbour_block, neighbour_mask, upstream):
    feat, dom = ("y", "c"), ("x", "z")
    shape = jax.ShapeDtypeStruct
    x, z = lax.axis_index("x"), lax.axis_index("z")
    at = jnp.stack([x * 4 + z, x, z, lax.axis_index("y"), lax.axis_index("c")])
    x_own = lax.all_to_all(
        features.reshape(96, 8, 256).transpose(1, 0, 2), feat, 0, 0, tiled=True
    )
    links = jnp.pad(jnp.maximum(neighbour_block.reshape(1, 12), 0), ((0, 0), (0, 116)))
    mask = call(mask_kernel, shape((336, 768), BF), [VMEM] * 4, moved=1_200_000)(
        neighbour_mask[0], upstream[0].T, degree.reshape(2, 128), links
    )
    weight = lax.dynamic_slice(first_weight, (0, z * 256), (96, 256))
    other = lax.ppermute(weight, "c", [(0, 1), (1, 0)])
    after, before, other = lax.optimization_barrier((*near(mask, "z"), other))
    weights = ring(jnp.stack([weight, other]), "y")
    far = [fetch(after[:192], "z", 1), fetch(before[192:], "z", -1)]
    x_own, *far = lax.optimization_barrier((x_own, *far))
    masks = [mask, after, before, *far]
    scaled = call(upstream_kernel, shape((4, 160, 256), BF), [VMEM] * 5 + [SMEM], moved=1_000_000)(
        *masks, at
    )
    x_after, x_before, after, before = lax.optimization_barrier((*near(x_own, "z"), *near(scaled, "x")))
    x_far = [fetch(x_after[:4], "z", 1), fetch(x_before[4:], "z", -1)]
    far = [fetch(after[:2], "x", 1), fetch(before[2:], "x", -1)]
    *x_far, far_low, far_high = lax.optimization_barrier((*x_far, *far))
    x_wide = [x_own, x_after, x_before, *x_far]
    scaled = [scaled, after, before, far_low, far_high]
    s = call(
        project_kernel,
        shape((4, 256, 256), BF),
        [VMEM] * 14 + [SMEM],
        [pltpu.VMEM((8, 96, 256), BF)],
        flops=400_000_000,
        moved=3_000_000,
    )(*x_wide, *weights, *masks, at)
    s = rounds(s, "x", 2)
    own_second = lax.dynamic_slice(second_weight, (z * 256, 0), (256, 153))
    own_second = jnp.pad(own_second, ((0, 0), (0, 7)))
    links_scratch = [
        pltpu.VMEM((8, 128), I32), pltpu.SMEM((8, 128), I32), pltpu.SemaphoreType.DMA
    ]
    *hid, back, second = call(
        first_mix_kernel,
        (shape((256, 256), BF),) * 4 + (shape((4, 256, 256), BF), shape((160, 256), F32)),
        [VMEM] * 16 + [SMEM],
        [pltpu.VMEM((32, 416, 128), BF), *links_scratch],
        flops=700_000_000,
        moved=8_000_000,
        limit=20,
    )(*s, *scaled, *masks, own_second, at)
    after, before, *hid = lax.optimization_barrier((*near(back, "x"), *hid))
    hid = [hid[0]] + [fetch(value, "z", -shift) for value, shift in zip(hid[1:], RING[1:])]
    back = [back, after, before, fetch(after[:2], "x", 1), fetch(before[2:], "x", -1)]
    part = call(
        second_mix_kernel,
        shape((8, 4, 128, 128), BF),
        [VMEM] * 16 + [SMEM],
        [pltpu.VMEM((32, 256, 128), BF), *links_scratch],
        flops=900_000_000,
        moved=8_000_000,
        limit=20,
    )(*back, *masks, *x_wide, second, at)
    part = lax.all_to_all(part.reshape(32, 128, 128), ("y", "c", "x"), 0, 0, tiled=True)
    tile = shape((16, 128, 128), BF)
    done = call(add_kernel, tile, [VMEM], moved=1_500_000)(part)
    done = lax.all_to_all(done, dom, 0, 0, tiled=True)
    hidden = call(hidden_kernel, shape((256, 1024), BF), [VMEM] * 4 + [SMEM], moved=1_000_000)(*hid, at)
    grad_first, grad_second = call(
        gradient_kernel, (shape((96, 1024), F32), shape((153, 1024), F32)), [VMEM], moved=1_500_000
    )(done)
    return (hidden[None], grad_first, grad_second.T)


def solution(mesh):
    wide = Mesh(mesh.devices.reshape(4, 2, 4, 4), ("y", "c", "x", "z"))
    feat, dom = ("y", "c"), ("x", "z")
    placed = (
        P(feat, dom, None),
        P(feat, None),
        P(),
        P(dom, feat),
        P(dom, feat, None),
        P(dom, feat, None, None, None),
        P(dom, feat, None),
    )
    return jax.shard_map(
        body,
        mesh=wide,
        in_specs=placed,
        out_specs=(P(dom, feat, None), P(feat, None), P()),
        check_vma=False,
    )
```

```python
import jax
import jax.numpy as jnp
from jax import lax
from jax.experimental import pallas as pl
from jax.experimental.pallas import tpu as pltpu
from jax.sharding import Mesh
from jax.sharding import PartitionSpec as P

BF = jnp.bfloat16
F32 = jnp.float32
I32 = jnp.int32
VMEM = pl.BlockSpec(memory_space=pltpu.VMEM)
SMEM = pl.BlockSpec(memory_space=pltpu.SMEM)
MIB = 1024 * 1024
RING = (0, 1, -1, 2)
NT = (((1,), (1,)), ((), ()))


def dot(a, b, dims=(((1,), (0,)), ((), ()))):
    return lax.dot_general(a, b, dims, preferred_element_type=F32)


def halves(a, b):
    low = lax.broadcasted_iota(I32, a.shape, 1) < 64
    return jnp.where(low, a, pltpu.roll(b, 64, 1)), jnp.where(low, pltpu.roll(a, 64, 1), b)


def owner(block):
    return (block % 4) * 4 + block // 4


def mask_kernel(mask_ref, up_ref, deg_ref, links_ref, out_ref):
    for b, at in enumerate((0, 192)):
        for k in range(6):
            out_ref[at : at + 128, k * 128 : k * 128 + 128] = mask_ref[b, k].astype(F32).astype(BF)
    out_ref[128:192, 0:256] = up_ref[0:64, :]
    out_ref[128:192, 256:512] = up_ref[64:128, :]
    rest = jnp.concatenate([up_ref[128:153, :].astype(F32), jnp.zeros((39, 256), F32)], axis=0)
    out_ref[128:192, 512:768] = rest.astype(BF)
    info = []
    for b in range(2):
        degree = deg_ref[b : b + 1, :]
        info += [degree >> 5, degree & 31]
    info = jnp.concatenate(info + [links_ref[...], jnp.zeros((11, 128), I32)], axis=0)
    out_ref[320:336, :] = jnp.zeros((16, 768), BF)
    out_ref[320:336, 0:128] = info.astype(F32).astype(BF)


def block_of(m_refs, k, b):
    if k < 3:
        return m_refs[k][b * 192 : b * 192 + 128, :]
    return m_refs[3 + b][0:128, :]


def info_of(m_refs, k):
    rows = m_refs[k][320:336, 0:128] if k < 3 else m_refs[4][128:144, 0:128]
    return rows.astype(F32)


def inverse_of(info, b):
    return lax.rsqrt(info[2 * b : 2 * b + 1] * 32.0 + info[2 * b + 1 : 2 * b + 2])


def upstream_kernel(*refs):
    m_refs, out_refs = refs[:5], refs[5:7]
    for k, shift in enumerate(RING):
        info = info_of(m_refs, k)
        inv = jnp.concatenate([inverse_of(info, 0), inverse_of(info, 1)], axis=1)
        for c in range(3):
            rows = min(64, 160 - 64 * c)
            up = m_refs[k][128 : 128 + rows, c * 256 : c * 256 + 256]
            out_refs[k // 2][k % 2, c * 64 : c * 64 + rows] = (inv * up.astype(F32)).astype(BF)


def features_at(refs, k, f):
    return refs[2 * k + f // 4][f % 4]


def project_kernel(*refs):
    x_refs, w_refs, m_refs, at_ref = refs[:8], refs[8:12], refs[12:17], refs[17]
    out_refs, w_ref = refs[18:20], refs[20]
    for k, shift in enumerate(RING):
        for flip in range(2):
            f = ((at_ref[3] + shift + 4) & 3) * 2 + ((at_ref[4] + flip) & 1)
            w_ref[f] = w_refs[k][flip]
    w = w_ref[...].reshape(768, 256).astype(F32).T.astype(BF)
    for k, shift in enumerate(RING):
        info = info_of(m_refs, k)
        inv = jnp.concatenate([inverse_of(info, 0), inverse_of(info, 1)], axis=1)
        whole = jnp.concatenate([features_at(x_refs, k, f) for f in range(8)], axis=0)
        out_refs[k // 2][k % 2] = (inv * dot(w, whole)).astype(BF)


def collect(refs, base, src_ref, at_ref):
    rows = refs[0].shape[1]
    for i, ref in enumerate(refs):
        x = (at_ref[1] + RING[i // 2] + 4) & 3
        for j in range(2):
            d = x * 4 + ((at_ref[2] + RING[(i % 2) * 2 + j] + 4) & 3)
            for h in range(2):
                src_ref[2 * d + h, base : base + rows] = ref[j, :, h * 128 : h * 128 + 128]


def scalars(m_refs, stage_ref, links_ref, sem):
    rows = [info_of(m_refs, k)[4:5] for k in range(4)]
    stage_ref[...] = jnp.concatenate(rows + [jnp.zeros((4, 128), F32)], axis=0).astype(I32)
    copy = pltpu.make_async_copy(stage_ref, links_ref, sem)
    copy.start()
    copy.wait()


def spread(src_ref, links_ref, m_refs, k, b, t):
    named = [src_ref[links_ref[k, b * 6 + s]] for s in range(6)]
    total = dot(jnp.concatenate(named, axis=1), block_of(m_refs, k, b), NT)
    return src_ref[t].astype(F32) + total


def first_mix_kernel(*refs):
    s_refs, u_refs, m_refs, sw_ref, at_ref = refs[:8], refs[8:16], refs[16:21], refs[21], refs[22]
    hid_refs, back_refs, second_ref = refs[23:27], refs[27:29], refs[29]
    src_ref, stage_ref, links_ref, sem = refs[30:]
    scalars(m_refs, stage_ref, links_ref, sem)
    collect(s_refs, 0, src_ref, at_ref)
    collect(u_refs, 256, src_ref, at_ref)
    second = jnp.zeros((160, 256), F32)
    for k, shift in enumerate(RING):
        z = (at_ref[2] + shift + 4) & 3
        info = info_of(m_refs, k)
        for b in range(2):
            inv = inverse_of(info, b)
            lanes = slice(b * 128, b * 128 + 128)
            total = spread(src_ref, links_ref, m_refs, k, b, (at_ref[1] * 4 + z) * 2 + b)
            m = inv * total[0:256]
            s = jax.nn.sigmoid(m)
            hid = (m * s).astype(BF)
            hid_refs[k][:, lanes] = hid
            one = (inv * hid.astype(F32)).astype(BF)
            pull = total[256:416].astype(BF)
            second = second + dot(pull, one, NT)
            slope = s * (1.0 + m * (1.0 - s))
            back = inv * inv * dot(sw_ref[...], pull) * slope
            back_refs[k // 2][k % 2, :, lanes] = back.astype(BF)
    second_ref[...] = second


def second_mix_kernel(*refs):
    b_refs, m_refs, x_refs, second_ref, at_ref = refs[:8], refs[8:13], refs[13:21], refs[21], refs[22]
    out_ref, src_ref, stage_ref, links_ref, sem = refs[23:]
    scalars(m_refs, stage_ref, links_ref, sem)
    collect(b_refs, 0, src_ref, at_ref)
    rights = []
    for k, shift in enumerate(RING):
        z = (at_ref[2] + shift + 4) & 3
        info = info_of(m_refs, k)
        parts = []
        for b in range(2):
            total = spread(src_ref, links_ref, m_refs, k, b, (at_ref[1] * 4 + z) * 2 + b)
            parts.append((inverse_of(info, b) * total).astype(BF))
        rights.append(jnp.concatenate(parts, axis=1))
    seconds = []
    for p in range(2):
        m = second_ref[:, p * 128 : p * 128 + 128]
        seconds += halves(m[:80], m[80:])
    for f in range(8):
        acc = jnp.zeros((96, 256), F32)
        for k, right in enumerate(rights):
            acc = acc + dot(features_at(x_refs, k, f), right, NT)
        for p in range(2):
            g = acc[:, p * 128 : p * 128 + 128]
            for q, part in enumerate(halves(g[:48], g[48:])):
                both = jnp.concatenate([part, seconds[2 * p + q]], axis=0)
                out_ref[f, 2 * p + q] = both.astype(BF)


def add_kernel(part_ref, out_ref):
    total = part_ref[0].astype(F32)
    for i in range(1, 32):
        total = total + part_ref[i].astype(F32)
    total = total.astype(BF)
    for d in range(16):
        out_ref[d] = total


def hidden_kernel(h0_ref, h1_ref, h2_ref, h3_ref, at_ref, out_ref):
    for ref, shift in zip((h0_ref, h1_ref, h2_ref, h3_ref), RING):
        at = pl.multiple_of(((at_ref[2] - shift + 4) & 3) * 256, 256)
        out_ref[:, pl.ds(at, 256)] = ref[...].astype(F32).T.astype(BF)


def gradient_kernel(in_ref, first_ref, second_ref):
    for j in range(8):
        cols = pl.ds(j * 128, 128)
        one, two = halves(in_ref[owner(2 * j)].astype(F32), in_ref[owner(2 * j + 1)].astype(F32))
        first_ref[0:48, cols] = one[:48]
        first_ref[48:96, cols] = two[:48]
        second_ref[0:80, cols] = one[48:]
        second_ref[80:153, cols] = two[48:121]


def call(kernel, shape, specs, scratch=(), flops=0, moved=0, limit=20):
    return pl.pallas_call(
        kernel,
        out_shape=shape,
        in_specs=specs,
        out_specs=jax.tree.map(lambda _: VMEM, shape),
        scratch_shapes=list(scratch),
        compiler_params=pltpu.CompilerParams(vmem_limit_bytes=limit * MIB),
        cost_estimate=pl.CostEstimate(flops=flops, bytes_accessed=moved, transcendentals=0),
    )


def fetch(value, axis, shift):
    return lax.ppermute(value, axis, [((i + shift) % 4, i) for i in range(4)])


def ring(value, axis):
    return [value] + [fetch(value, axis, shift) for shift in RING[1:]]


def near(value, axis):
    return fetch(value, axis, 1), fetch(value, axis, -1)


def neighbours(low, high, axis):
    return fetch(low, axis, 1), fetch(high, axis, -1), fetch(high, axis, 1), fetch(low, axis, -1)


def rounds(low, high, found, passed, axis):
    far = fetch(passed[0], axis, 1), fetch(passed[1], axis, -1)
    return [low, high, passed[0], found[2], found[3], passed[1], *far]


def body(features, first_weight, second_weight, degree, neighbour_block, neighbour_mask, upstream):
    feat, dom = ("y", "c"), ("x", "z")
    shape = jax.ShapeDtypeStruct
    x, z = lax.axis_index("x"), lax.axis_index("z")
    at = jnp.stack([x * 4 + z, x, z, lax.axis_index("y"), lax.axis_index("c")])
    x_own = lax.all_to_all(
        features.reshape(96, 8, 256).transpose(1, 0, 2), feat, 0, 0, tiled=True
    )
    links = jnp.pad(jnp.maximum(neighbour_block.reshape(1, 12), 0), ((0, 0), (0, 116)))
    mask = call(mask_kernel, shape((336, 768), BF), [VMEM] * 4, moved=1_200_000)(
        neighbour_mask[0], upstream[0].T, degree.reshape(2, 128), links
    )
    weight = lax.dynamic_slice(first_weight, (0, z * 256), (96, 256))
    other = lax.ppermute(weight, "c", [(0, 1), (1, 0)])
    after, before, other = lax.optimization_barrier((*near(mask, "z"), other))
    weights = ring(jnp.stack([weight, other]), "y")
    x_low, x_high, after, before = lax.optimization_barrier((x_own[:4], x_own[4:], after, before))
    x_near = neighbours(x_low, x_high, "z")
    far = [fetch(after[:192], "z", 1), fetch(before[192:], "z", -1)]
    *passed, far_low, far_high, w1, w2, w3 = lax.optimization_barrier((*x_near[:2], *far, *weights[1:]))
    masks = [mask, after, before, far_low, far_high]
    weights = [weights[0], w1, w2, w3]
    x_wide = rounds(x_low, x_high, x_near, passed, "z")
    half = shape((2, 160, 256), BF)
    scaled = call(upstream_kernel, (half, half), [VMEM] * 5, moved=1_000_000)(*masks)
    u_near = neighbours(*scaled, "x")
    *x_far, u0, u1 = lax.optimization_barrier((*x_wide[6:], *u_near[:2]))
    x_wide = [*x_wide[:6], *x_far]
    scaled = rounds(*scaled, u_near, (u0, u1), "x")
    half = shape((2, 256, 256), BF)
    s = call(
        project_kernel,
        (half, half),
        [VMEM] * 17 + [SMEM],
        [pltpu.VMEM((8, 96, 256), BF)],
        flops=400_000_000,
        moved=3_000_000,
    )(*x_wide, *weights, *masks, at)
    s_near = neighbours(*s, "x")
    s = rounds(*s, s_near, s_near[:2], "x")
    own_second = lax.dynamic_slice(second_weight, (z * 256, 0), (256, 153))
    own_second = jnp.pad(own_second, ((0, 0), (0, 7)))
    links_scratch = [
        pltpu.VMEM((8, 128), I32), pltpu.SMEM((8, 128), I32), pltpu.SemaphoreType.DMA
    ]
    *hid, low, high, second = call(
        first_mix_kernel,
        (shape((256, 256), BF),) * 4 + (half, half, shape((160, 256), F32)),
        [VMEM] * 22 + [SMEM],
        [pltpu.VMEM((32, 416, 128), BF), *links_scratch],
        flops=700_000_000,
        moved=8_000_000,
    )(*s, *scaled, *masks, own_second, at)
    b_near = neighbours(low, high, "x")
    *passed, h1, h2, h3 = lax.optimization_barrier((*b_near[:2], *hid[1:]))
    back = rounds(low, high, b_near, passed, "x")
    hid = [hid[0]] + [fetch(value, "z", -shift) for value, shift in zip((h1, h2, h3), RING[1:])]
    part = call(
        second_mix_kernel,
        shape((8, 4, 128, 128), BF),
        [VMEM] * 22 + [SMEM],
        [pltpu.VMEM((32, 256, 128), BF), *links_scratch],
        flops=900_000_000,
        moved=8_000_000,
    )(*back, *masks, *x_wide, second, at)
    part, *hid = lax.optimization_barrier((part, *hid))
    part = lax.all_to_all(part.reshape(32, 128, 128), ("y", "c", "x"), 0, 0, tiled=True)
    tile = shape((16, 128, 128), BF)
    done = call(add_kernel, tile, [VMEM], moved=1_500_000)(part)
    done = lax.all_to_all(done, dom, 0, 0, tiled=True)
    hidden = call(hidden_kernel, shape((256, 1024), BF), [VMEM] * 4 + [SMEM], moved=1_000_000)(*hid, at)
    grad_first, grad_second = call(
        gradient_kernel, (shape((96, 1024), F32), shape((153, 1024), F32)), [VMEM], moved=1_500_000
    )(done)
    return (hidden[None], grad_first, grad_second.T)


def solution(mesh):
    wide = Mesh(mesh.devices.reshape(4, 2, 4, 4), ("y", "c", "x", "z"))
    feat, dom = ("y", "c"), ("x", "z")
    placed = (
        P(feat, dom, None),
        P(feat, None),
        P(),
        P(dom, feat),
        P(dom, feat, None),
        P(dom, feat, None, None, None),
        P(dom, feat, None),
    )
    return jax.shard_map(
        body,
        mesh=wide,
        in_specs=placed,
        out_specs=(P(dom, feat, None), P(feat, None), P()),
        check_vma=False,
    )
```

```python
import jax
import jax.numpy as jnp
from jax import lax
from jax.experimental import pallas as pl
from jax.experimental.pallas import tpu as pltpu
from jax.sharding import Mesh
from jax.sharding import PartitionSpec as P

BF = jnp.bfloat16
F32 = jnp.float32
I32 = jnp.int32
VMEM = pl.BlockSpec(memory_space=pltpu.VMEM)
SMEM = pl.BlockSpec(memory_space=pltpu.SMEM)
MIB = 1024 * 1024
RING = (0, 1, -1, 2)
NT = (((1,), (1,)), ((), ()))


def dot(a, b, dims=(((1,), (0,)), ((), ()))):
    return lax.dot_general(a, b, dims, preferred_element_type=F32)


def halves(a, b):
    low = lax.broadcasted_iota(I32, a.shape, 1) < 64
    return jnp.where(low, a, pltpu.roll(b, 64, 1)), jnp.where(low, pltpu.roll(a, 64, 1), b)


def owner(block):
    return (block % 4) * 4 + block // 4


def mask_kernel(mask_ref, out_ref):
    for b in range(2):
        for k in range(6):
            out_ref[b * 128 : b * 128 + 128, k * 128 : k * 128 + 128] = (
                mask_ref[b, k].astype(F32).astype(BF)
            )


def node_kernel(up_ref, deg_ref, links_ref, out_ref):
    info, inv = [], []
    for b in range(2):
        degree = deg_ref[b : b + 1, :]
        info += [degree >> 5, degree & 31]
        inv.append(lax.rsqrt(degree.astype(F32)))
    scaled = jnp.concatenate(inv, axis=1) * up_ref[...].astype(F32)
    out_ref[0:160, :] = jnp.concatenate([scaled, jnp.zeros((7, 256), F32)], axis=0).astype(BF)
    info = jnp.concatenate(info + [links_ref[...], jnp.zeros((11, 128), I32)], axis=0)
    out_ref[160:176, 0:128] = info.astype(F32).astype(BF)
    out_ref[160:176, 128:256] = jnp.zeros((16, 128), BF)


def pack_kernel(*refs):
    for k in range(4):
        refs[4 + k // 2][k % 2] = refs[k][0:160, :]


def block_of(m_refs, k, b):
    return m_refs[k][b * 128 : b * 128 + 128, :] if k < 3 else m_refs[3 + b][...]


def info_of(i_refs, k):
    return i_refs[k][160:176, 0:128].astype(F32)


def inverse_of(info, b):
    return lax.rsqrt(info[2 * b : 2 * b + 1] * 32.0 + info[2 * b + 1 : 2 * b + 2])


def features_at(refs, k, f):
    return refs[2 * k + f // 4][f % 4]


def project_kernel(*refs):
    x_refs, w_refs, i_refs, at_ref = refs[:8], refs[8:12], refs[12:16], refs[16]
    out_refs, w_ref = refs[17:19], refs[19]
    for k, shift in enumerate(RING):
        for flip in range(2):
            f = ((at_ref[3] + shift + 4) & 3) * 2 + ((at_ref[4] + flip) & 1)
            w_ref[f] = w_refs[k][flip]
    w = w_ref[...].reshape(768, 256).astype(F32).T.astype(BF)
    for k, shift in enumerate(RING):
        info = info_of(i_refs, k)
        inv = jnp.concatenate([inverse_of(info, 0), inverse_of(info, 1)], axis=1)
        whole = jnp.concatenate([features_at(x_refs, k, f) for f in range(8)], axis=0)
        out_refs[k // 2][k % 2] = (inv * dot(w, whole)).astype(BF)


def collect(refs, base, src_ref, at_ref):
    rows = refs[0].shape[1]
    for i, ref in enumerate(refs):
        x = (at_ref[1] + RING[i // 2] + 4) & 3
        for j in range(2):
            d = x * 4 + ((at_ref[2] + RING[(i % 2) * 2 + j] + 4) & 3)
            for h in range(2):
                src_ref[2 * d + h, base : base + rows] = ref[j, :, h * 128 : h * 128 + 128]


def scalars(i_refs, stage_ref, links_ref, sem):
    rows = [info_of(i_refs, k)[4:5] for k in range(4)]
    stage_ref[...] = jnp.concatenate(rows + [jnp.zeros((4, 128), F32)], axis=0).astype(I32)
    copy = pltpu.make_async_copy(stage_ref, links_ref, sem)
    copy.start()
    copy.wait()


def spread(src_ref, links_ref, m_refs, k, b, t):
    named = [src_ref[links_ref[k, b * 6 + s]] for s in range(6)]
    total = dot(jnp.concatenate(named, axis=1), block_of(m_refs, k, b), NT)
    return src_ref[t].astype(F32) + total


def first_mix_kernel(*refs):
    s_refs, u_refs, m_refs, sw_ref, at_ref = refs[:8], refs[8:16], refs[16:21], refs[21], refs[22]
    i_refs, hid_refs, back_refs, second_ref = refs[23:27], refs[27:31], refs[31:33], refs[33]
    src_ref, stage_ref, links_ref, sem = refs[34:]
    scalars(i_refs, stage_ref, links_ref, sem)
    collect(s_refs, 0, src_ref, at_ref)
    collect(u_refs, 256, src_ref, at_ref)
    second = jnp.zeros((160, 256), F32)
    for k, shift in enumerate(RING):
        z = (at_ref[2] + shift + 4) & 3
        info = info_of(i_refs, k)
        for b in range(2):
            inv = inverse_of(info, b)
            lanes = slice(b * 128, b * 128 + 128)
            total = spread(src_ref, links_ref, m_refs, k, b, (at_ref[1] * 4 + z) * 2 + b)
            m = inv * total[0:256]
            s = jax.nn.sigmoid(m)
            hid = (m * s).astype(BF)
            hid_refs[k][:, lanes] = hid
            one = (inv * hid.astype(F32)).astype(BF)
            pull = total[256:416].astype(BF)
            second = second + dot(pull, one, NT)
            slope = s * (1.0 + m * (1.0 - s))
            back = inv * inv * dot(sw_ref[...], pull) * slope
            back_refs[k // 2][k % 2, :, lanes] = back.astype(BF)
    second_ref[...] = second


def second_mix_kernel(*refs):
    b_refs, m_refs, x_refs, second_ref, at_ref = refs[:8], refs[8:13], refs[13:21], refs[21], refs[22]
    i_refs, out_ref, src_ref, stage_ref, links_ref, sem = refs[23:27], *refs[27:]
    scalars(i_refs, stage_ref, links_ref, sem)
    collect(b_refs, 0, src_ref, at_ref)
    rights = []
    for k, shift in enumerate(RING):
        z = (at_ref[2] + shift + 4) & 3
        info = info_of(i_refs, k)
        parts = []
        for b in range(2):
            total = spread(src_ref, links_ref, m_refs, k, b, (at_ref[1] * 4 + z) * 2 + b)
            parts.append((inverse_of(info, b) * total).astype(BF))
        rights.append(jnp.concatenate(parts, axis=1))
    seconds = []
    for p in range(2):
        m = second_ref[:, p * 128 : p * 128 + 128]
        seconds += halves(m[:80], m[80:])
    for f in range(8):
        acc = jnp.zeros((96, 256), F32)
        for k, right in enumerate(rights):
            acc = acc + dot(features_at(x_refs, k, f), right, NT)
        for p in range(2):
            g = acc[:, p * 128 : p * 128 + 128]
            for q, part in enumerate(halves(g[:48], g[48:])):
                both = jnp.concatenate([part, seconds[2 * p + q]], axis=0)
                out_ref[f, 2 * p + q] = both.astype(BF)


def add_kernel(part_ref, out_ref):
    total = part_ref[0].astype(F32)
    for i in range(1, 32):
        total = total + part_ref[i].astype(F32)
    total = total.astype(BF)
    for d in range(16):
        out_ref[d] = total


def hidden_kernel(h0_ref, h1_ref, h2_ref, h3_ref, at_ref, out_ref):
    for ref, shift in zip((h0_ref, h1_ref, h2_ref, h3_ref), RING):
        at = pl.multiple_of(((at_ref[2] - shift + 4) & 3) * 256, 256)
        out_ref[:, pl.ds(at, 256)] = ref[...].astype(F32).T.astype(BF)


def gradient_kernel(in_ref, first_ref, second_ref):
    for j in range(8):
        cols = pl.ds(j * 128, 128)
        one, two = halves(in_ref[owner(2 * j)].astype(F32), in_ref[owner(2 * j + 1)].astype(F32))
        first_ref[0:48, cols] = one[:48]
        first_ref[48:96, cols] = two[:48]
        second_ref[0:80, cols] = one[48:]
        second_ref[80:153, cols] = two[48:121]


def call(kernel, shape, specs, scratch=(), flops=0, moved=0, limit=20):
    return pl.pallas_call(
        kernel,
        out_shape=shape,
        in_specs=specs,
        out_specs=jax.tree.map(lambda _: VMEM, shape),
        scratch_shapes=list(scratch),
        compiler_params=pltpu.CompilerParams(vmem_limit_bytes=limit * MIB),
        cost_estimate=pl.CostEstimate(flops=flops, bytes_accessed=moved, transcendentals=0),
    )


def fetch(value, axis, shift):
    return lax.ppermute(value, axis, [((i + shift) % 4, i) for i in range(4)])


def ring(value, axis):
    return [value] + [fetch(value, axis, shift) for shift in RING[1:]]


def near(value, axis):
    return fetch(value, axis, 1), fetch(value, axis, -1)


def neighbours(low, high, axis):
    return fetch(low, axis, 1), fetch(high, axis, -1), fetch(high, axis, 1), fetch(low, axis, -1)


def rounds(low, high, found, passed, axis):
    far = fetch(passed[0], axis, 1), fetch(passed[1], axis, -1)
    return [low, high, passed[0], found[2], found[3], passed[1], *far]


def body(features, first_weight, second_weight, degree, neighbour_block, neighbour_mask, upstream):
    feat, dom = ("y", "c"), ("x", "z")
    shape = jax.ShapeDtypeStruct
    x, z = lax.axis_index("x"), lax.axis_index("z")
    at = jnp.stack([x * 4 + z, x, z, lax.axis_index("y"), lax.axis_index("c")])
    x_own = lax.all_to_all(
        features.reshape(96, 8, 256).transpose(1, 0, 2), feat, 0, 0, tiled=True
    )
    links = jnp.pad(jnp.maximum(neighbour_block.reshape(1, 12), 0), ((0, 0), (0, 116)))
    nodes = call(node_kernel, shape((176, 256), BF), [VMEM] * 3, moved=200_000)(
        upstream[0].T, degree.reshape(2, 128), links
    )
    nodes = ring(nodes, "z")
    half = shape((2, 160, 256), BF)
    scaled = call(pack_kernel, (half, half), [VMEM] * 4, moved=600_000)(*nodes)
    weight = lax.dynamic_slice(first_weight, (0, z * 256), (96, 256))
    other = lax.ppermute(weight, "c", [(0, 1), (1, 0)])
    mask = call(mask_kernel, shape((256, 768), BF), [VMEM], moved=1_200_000)(neighbour_mask[0])
    x_low, x_high, *scaled, mask, other = lax.optimization_barrier(
        (x_own[:4], x_own[4:], *scaled, mask, other)
    )
    x_near = neighbours(x_low, x_high, "z")
    u_near = neighbours(*scaled, "x")
    x0, x1, u0, u1, other = lax.optimization_barrier((*x_near[:2], *u_near[:2], other))
    weights = ring(jnp.stack([weight, other]), "y")
    x_wide = rounds(x_low, x_high, x_near, (x0, x1), "z")
    scaled = rounds(*scaled, u_near, (u0, u1), "x")
    *x_far, u2, u3, u4, u5 = lax.optimization_barrier((*x_wide[6:], *scaled[3:5], *scaled[6:]))
    x_wide = [*x_wide[:6], *x_far]
    scaled = [*scaled[:3], u2, u3, scaled[5], u4, u5]
    half = shape((2, 256, 256), BF)
    s = call(
        project_kernel,
        (half, half),
        [VMEM] * 16 + [SMEM],
        [pltpu.VMEM((8, 96, 256), BF)],
        flops=400_000_000,
        moved=3_000_000,
    )(*x_wide, *weights, *nodes, at)
    *s, mask = lax.optimization_barrier((*s, mask))
    s_near = neighbours(*s, "x")
    after, before = near(mask, "z")
    s = rounds(*s, s_near, s_near[:2], "x")
    masks = [mask, after, before, fetch(after[:128], "z", 1), fetch(before[128:], "z", -1)]
    own_second = lax.dynamic_slice(second_weight, (z * 256, 0), (256, 153))
    own_second = jnp.pad(own_second, ((0, 0), (0, 7)))
    links_scratch = [
        pltpu.VMEM((8, 128), I32), pltpu.SMEM((8, 128), I32), pltpu.SemaphoreType.DMA
    ]
    *hid, low, high, second = call(
        first_mix_kernel,
        (shape((256, 256), BF),) * 4 + (half, half, shape((160, 256), F32)),
        [VMEM] * 22 + [SMEM] + [VMEM] * 4,
        [pltpu.VMEM((32, 416, 128), BF), *links_scratch],
        flops=700_000_000,
        moved=8_000_000,
    )(*s, *scaled, *masks, own_second, at, *nodes)
    b_near = neighbours(low, high, "x")
    *passed, h1, h2, h3 = lax.optimization_barrier((*b_near[:2], *hid[1:]))
    back = rounds(low, high, b_near, passed, "x")
    hid = [hid[0]] + [fetch(value, "z", -shift) for value, shift in zip((h1, h2, h3), RING[1:])]
    part = call(
        second_mix_kernel,
        shape((8, 4, 128, 128), BF),
        [VMEM] * 22 + [SMEM] + [VMEM] * 4,
        [pltpu.VMEM((32, 256, 128), BF), *links_scratch],
        flops=900_000_000,
        moved=8_000_000,
    )(*back, *masks, *x_wide, second, at, *nodes)
    part, *hid = lax.optimization_barrier((part, *hid))
    part = lax.all_to_all(part.reshape(32, 128, 128), ("y", "c", "x"), 0, 0, tiled=True)
    tile = shape((16, 128, 128), BF)
    done = call(add_kernel, tile, [VMEM], moved=1_500_000)(part)
    done = lax.all_to_all(done, dom, 0, 0, tiled=True)
    hidden = call(hidden_kernel, shape((256, 1024), BF), [VMEM] * 4 + [SMEM], moved=1_000_000)(*hid, at)
    grad_first, grad_second = call(
        gradient_kernel, (shape((96, 1024), F32), shape((153, 1024), F32)), [VMEM], moved=1_500_000
    )(done)
    return (hidden[None], grad_first, grad_second.T)


def solution(mesh):
    wide = Mesh(mesh.devices.reshape(4, 2, 4, 4), ("y", "c", "x", "z"))
    feat, dom = ("y", "c"), ("x", "z")
    placed = (
        P(feat, dom, None),
        P(feat, None),
        P(),
        P(dom, feat),
        P(dom, feat, None),
        P(dom, feat, None, None, None),
        P(dom, feat, None),
    )
    return jax.shard_map(
        body,
        mesh=wide,
        in_specs=placed,
        out_specs=(P(dom, feat, None), P(feat, None), P()),
        check_vma=False,
    )
```

```python
import jax
import jax.numpy as jnp
from jax import lax
from jax.experimental import pallas as pl
from jax.experimental.pallas import tpu as pltpu
from jax.sharding import Mesh
from jax.sharding import PartitionSpec as P

BF = jnp.bfloat16
F32 = jnp.float32
I32 = jnp.int32
VMEM = pl.BlockSpec(memory_space=pltpu.VMEM)
SMEM = pl.BlockSpec(memory_space=pltpu.SMEM)
MIB = 1024 * 1024
RING = (0, 1, -1, 2)
NT = (((1,), (1,)), ((), ()))


def dot(a, b, dims=(((1,), (0,)), ((), ()))):
    return lax.dot_general(a, b, dims, preferred_element_type=F32)


def halves(a, b):
    low = lax.broadcasted_iota(I32, a.shape, 1) < 64
    return jnp.where(low, a, pltpu.roll(b, 64, 1)), jnp.where(low, pltpu.roll(a, 64, 1), b)


def owner(block):
    return (block % 4) * 4 + block // 4


def mask_kernel(mask_ref, out_ref):
    for b in range(2):
        for k in range(6):
            out_ref[b * 128 : b * 128 + 128, k * 128 : k * 128 + 128] = (
                mask_ref[b, k].astype(F32).astype(BF)
            )


def node_kernel(up_ref, deg_ref, links_ref, out_ref):
    info, inv = [], []
    for b in range(2):
        degree = deg_ref[b : b + 1, :]
        info += [degree >> 5, degree & 31]
        inv.append(lax.rsqrt(degree.astype(F32)))
    scaled = jnp.concatenate(inv, axis=1) * up_ref[...].astype(F32)
    out_ref[0:160, :] = jnp.concatenate([scaled, jnp.zeros((7, 256), F32)], axis=0).astype(BF)
    info = jnp.concatenate(info + [links_ref[...], jnp.zeros((11, 128), I32)], axis=0)
    out_ref[160:176, 0:128] = info.astype(F32).astype(BF)
    out_ref[160:176, 128:256] = jnp.zeros((16, 128), BF)


def pack_kernel(*refs):
    for k in range(4):
        refs[4 + k // 2][k % 2] = refs[k][0:160, :]


def block_of(m_refs, k, b):
    return m_refs[k][b * 128 : b * 128 + 128, :] if k < 3 else m_refs[3 + b][...]


def info_of(i_refs, k):
    return i_refs[k][160:176, 0:128].astype(F32)


def inverse_of(info, b):
    return lax.rsqrt(info[2 * b : 2 * b + 1] * 32.0 + info[2 * b + 1 : 2 * b + 2])


def features_at(refs, k, f):
    return refs[2 * k + f // 4][f % 4]


def project_kernel(*refs):
    x_refs, w_refs, i_refs, at_ref = refs[:8], refs[8:12], refs[12:16], refs[16]
    out_refs, w_ref = refs[17:19], refs[19]
    for k, shift in enumerate(RING):
        for flip in range(2):
            f = ((at_ref[3] + shift + 4) & 3) * 2 + ((at_ref[4] + flip) & 1)
            w_ref[f] = w_refs[k][flip]
    w = w_ref[...].reshape(768, 256).astype(F32).T.astype(BF)
    for k, shift in enumerate(RING):
        info = info_of(i_refs, k)
        inv = jnp.concatenate([inverse_of(info, 0), inverse_of(info, 1)], axis=1)
        whole = jnp.concatenate([features_at(x_refs, k, f) for f in range(8)], axis=0)
        out_refs[k // 2][k % 2] = (inv * dot(w, whole)).astype(BF)


def collect(refs, base, src_ref, at_ref):
    rows = refs[0].shape[1]
    for i, ref in enumerate(refs):
        x = (at_ref[1] + RING[i // 2] + 4) & 3
        for j in range(2):
            d = x * 4 + ((at_ref[2] + RING[(i % 2) * 2 + j] + 4) & 3)
            for h in range(2):
                src_ref[2 * d + h, base : base + rows] = ref[j, :, h * 128 : h * 128 + 128]


def collect_kernel(*refs):
    collect(refs[:8], 0, refs[9], refs[8])


def scalars(i_refs, stage_ref, links_ref, sem):
    rows = [info_of(i_refs, k)[4:5] for k in range(4)]
    stage_ref[...] = jnp.concatenate(rows + [jnp.zeros((4, 128), F32)], axis=0).astype(I32)
    copy = pltpu.make_async_copy(stage_ref, links_ref, sem)
    copy.start()
    copy.wait()


def spread(sources, links_ref, m_refs, k, b, t):
    def field(c):
        parts = [source[c] for source in sources]
        return parts[0] if len(parts) == 1 else jnp.concatenate(parts, axis=0)

    named = [field(links_ref[k, b * 6 + s]) for s in range(6)]
    total = dot(jnp.concatenate(named, axis=1), block_of(m_refs, k, b), NT)
    return field(t).astype(F32) + total


def first_mix_kernel(*refs):
    s_refs, u_ref, m_refs, sw_ref, at_ref = refs[:8], refs[8], refs[9:14], refs[14], refs[15]
    i_refs, hid_refs, back_refs, second_ref = refs[16:20], refs[20:24], refs[24:26], refs[26]
    src_ref, stage_ref, links_ref, sem = refs[27:]
    scalars(i_refs, stage_ref, links_ref, sem)
    collect(s_refs, 0, src_ref, at_ref)
    second = jnp.zeros((160, 256), F32)
    for k, shift in enumerate(RING):
        z = (at_ref[2] + shift + 4) & 3
        info = info_of(i_refs, k)
        for b in range(2):
            inv = inverse_of(info, b)
            lanes = slice(b * 128, b * 128 + 128)
            total = spread((src_ref, u_ref), links_ref, m_refs, k, b, (at_ref[1] * 4 + z) * 2 + b)
            m = inv * total[0:256]
            s = jax.nn.sigmoid(m)
            hid = (m * s).astype(BF)
            hid_refs[k][:, lanes] = hid
            one = (inv * hid.astype(F32)).astype(BF)
            pull = total[256:416].astype(BF)
            second = second + dot(pull, one, NT)
            slope = s * (1.0 + m * (1.0 - s))
            back = inv * inv * dot(sw_ref[...], pull) * slope
            back_refs[k // 2][k % 2, :, lanes] = back.astype(BF)
    second_ref[...] = second


def second_mix_kernel(*refs):
    b_refs, m_refs, x_refs, second_ref, at_ref = refs[:8], refs[8:13], refs[13:21], refs[21], refs[22]
    i_refs, out_ref, src_ref, stage_ref, links_ref, sem = refs[23:27], *refs[27:]
    scalars(i_refs, stage_ref, links_ref, sem)
    collect(b_refs, 0, src_ref, at_ref)
    rights = []
    for k, shift in enumerate(RING):
        z = (at_ref[2] + shift + 4) & 3
        info = info_of(i_refs, k)
        parts = []
        for b in range(2):
            total = spread((src_ref,), links_ref, m_refs, k, b, (at_ref[1] * 4 + z) * 2 + b)
            parts.append((inverse_of(info, b) * total).astype(BF))
        rights.append(jnp.concatenate(parts, axis=1))
    seconds = []
    for p in range(2):
        m = second_ref[:, p * 128 : p * 128 + 128]
        seconds += halves(m[:80], m[80:])
    for f in range(8):
        acc = jnp.zeros((96, 256), F32)
        for k, right in enumerate(rights):
            acc = acc + dot(features_at(x_refs, k, f), right, NT)
        for p in range(2):
            g = acc[:, p * 128 : p * 128 + 128]
            for q, part in enumerate(halves(g[:48], g[48:])):
                both = jnp.concatenate([part, seconds[2 * p + q]], axis=0)
                out_ref[f, 2 * p + q] = both.astype(BF)


def add_kernel(part_ref, out_ref):
    total = part_ref[0].astype(F32)
    for i in range(1, 32):
        total = total + part_ref[i].astype(F32)
    total = total.astype(BF)
    for d in range(16):
        out_ref[d] = total


def hidden_kernel(h0_ref, h1_ref, h2_ref, h3_ref, at_ref, out_ref):
    for ref, shift in zip((h0_ref, h1_ref, h2_ref, h3_ref), RING):
        at = pl.multiple_of(((at_ref[2] - shift + 4) & 3) * 256, 256)
        out_ref[:, pl.ds(at, 256)] = ref[...].astype(F32).T.astype(BF)


def gradient_kernel(in_ref, first_ref, second_ref):
    for j in range(8):
        cols = pl.ds(j * 128, 128)
        one, two = halves(in_ref[owner(2 * j)].astype(F32), in_ref[owner(2 * j + 1)].astype(F32))
        first_ref[0:48, cols] = one[:48]
        first_ref[48:96, cols] = two[:48]
        second_ref[0:80, cols] = one[48:]
        second_ref[80:153, cols] = two[48:121]


def call(kernel, shape, specs, scratch=(), flops=0, moved=0, limit=20):
    return pl.pallas_call(
        kernel,
        out_shape=shape,
        in_specs=specs,
        out_specs=jax.tree.map(lambda _: VMEM, shape),
        scratch_shapes=list(scratch),
        compiler_params=pltpu.CompilerParams(vmem_limit_bytes=limit * MIB),
        cost_estimate=pl.CostEstimate(flops=flops, bytes_accessed=moved, transcendentals=0),
    )


def fetch(value, axis, shift):
    return lax.ppermute(value, axis, [((i + shift) % 4, i) for i in range(4)])


def ring(value, axis):
    return [value] + [fetch(value, axis, shift) for shift in RING[1:]]


def near(value, axis):
    return fetch(value, axis, 1), fetch(value, axis, -1)


def neighbours(low, high, axis):
    return fetch(low, axis, 1), fetch(high, axis, -1), fetch(high, axis, 1), fetch(low, axis, -1)


def rounds(low, high, found, passed, axis):
    far = fetch(passed[0], axis, 1), fetch(passed[1], axis, -1)
    return [low, high, passed[0], found[2], found[3], passed[1], *far]


def body(features, first_weight, second_weight, degree, neighbour_block, neighbour_mask, upstream):
    feat, dom = ("y", "c"), ("x", "z")
    shape = jax.ShapeDtypeStruct
    x, z = lax.axis_index("x"), lax.axis_index("z")
    at = jnp.stack([x * 4 + z, x, z, lax.axis_index("y"), lax.axis_index("c")])
    x_own = lax.all_to_all(
        features.reshape(96, 8, 256).transpose(1, 0, 2), feat, 0, 0, tiled=True
    )
    links = jnp.pad(jnp.maximum(neighbour_block.reshape(1, 12), 0), ((0, 0), (0, 116)))
    nodes = call(node_kernel, shape((176, 256), BF), [VMEM] * 3, moved=200_000)(
        upstream[0].T, degree.reshape(2, 128), links
    )
    nodes = ring(nodes, "z")
    half = shape((2, 160, 256), BF)
    scaled = call(pack_kernel, (half, half), [VMEM] * 4, moved=600_000)(*nodes)
    weight = lax.dynamic_slice(first_weight, (0, z * 256), (96, 256))
    other = lax.ppermute(weight, "c", [(0, 1), (1, 0)])
    mask = call(mask_kernel, shape((256, 768), BF), [VMEM], moved=1_200_000)(neighbour_mask[0])
    own_second = lax.dynamic_slice(second_weight, (z * 256, 0), (256, 153))
    own_second = jnp.pad(own_second, ((0, 0), (0, 7)))
    weights = ring(jnp.stack([weight, other]), "y")
    x_low, x_high, mask, own_second, *weights, n1, n2, n3 = lax.optimization_barrier(
        (x_own[:4], x_own[4:], mask, own_second, *weights, *nodes[1:])
    )
    nodes = [nodes[0], n1, n2, n3]
    x_near = neighbours(x_low, x_high, "z")
    x0, x1, *scaled = lax.optimization_barrier((*x_near[:2], *scaled))
    x_wide = rounds(x_low, x_high, x_near, (x0, x1), "z")
    u_near = neighbours(*scaled, "x")
    scaled = rounds(*scaled, u_near, u_near[:2], "x")
    scaled = call(collect_kernel, shape((32, 160, 128), BF), [VMEM] * 8 + [SMEM], moved=2_600_000)(
        *scaled, at
    )
    half = shape((2, 256, 256), BF)
    s = call(
        project_kernel,
        (half, half),
        [VMEM] * 16 + [SMEM],
        [pltpu.VMEM((8, 96, 256), BF)],
        flops=400_000_000,
        moved=3_000_000,
    )(*x_wide, *weights, *nodes, at)
    *s, mask = lax.optimization_barrier((*s, mask))
    s_near = neighbours(*s, "x")
    after, before = near(mask, "z")
    s0, s1, scaled = lax.optimization_barrier((*s_near[:2], scaled))
    s = rounds(*s, s_near, (s0, s1), "x")
    masks = [mask, after, before, fetch(after[:128], "z", 1), fetch(before[128:], "z", -1)]
    links_scratch = [
        pltpu.VMEM((8, 128), I32), pltpu.SMEM((8, 128), I32), pltpu.SemaphoreType.DMA
    ]
    *hid, low, high, second = call(
        first_mix_kernel,
        (shape((256, 256), BF),) * 4 + (half, half, shape((160, 256), F32)),
        [VMEM] * 15 + [SMEM] + [VMEM] * 4,
        [pltpu.VMEM((32, 256, 128), BF), *links_scratch],
        flops=700_000_000,
        moved=8_000_000,
    )(*s, scaled, *masks, own_second, at, *nodes)
    b_near = neighbours(low, high, "x")
    *passed, h1, h2, h3 = lax.optimization_barrier((*b_near[:2], *hid[1:]))
    back = rounds(low, high, b_near, passed, "x")
    hid = [hid[0]] + [fetch(value, "z", -shift) for value, shift in zip((h1, h2, h3), RING[1:])]
    part = call(
        second_mix_kernel,
        shape((8, 4, 128, 128), BF),
        [VMEM] * 22 + [SMEM] + [VMEM] * 4,
        [pltpu.VMEM((32, 256, 128), BF), *links_scratch],
        flops=900_000_000,
        moved=8_000_000,
    )(*back, *masks, *x_wide, second, at, *nodes)
    part, *hid = lax.optimization_barrier((part, *hid))
    part = lax.all_to_all(part.reshape(32, 128, 128), ("y", "c", "x"), 0, 0, tiled=True)
    tile = shape((16, 128, 128), BF)
    done = call(add_kernel, tile, [VMEM], moved=1_500_000)(part)
    done = lax.all_to_all(done, dom, 0, 0, tiled=True)
    hidden = call(hidden_kernel, shape((256, 1024), BF), [VMEM] * 4 + [SMEM], moved=1_000_000)(*hid, at)
    grad_first, grad_second = call(
        gradient_kernel, (shape((96, 1024), F32), shape((153, 1024), F32)), [VMEM], moved=1_500_000
    )(done)
    return (hidden[None], grad_first, grad_second.T)


def solution(mesh):
    wide = Mesh(mesh.devices.reshape(4, 2, 4, 4), ("y", "c", "x", "z"))
    feat, dom = ("y", "c"), ("x", "z")
    placed = (
        P(feat, dom, None),
        P(feat, None),
        P(),
        P(dom, feat),
        P(dom, feat, None),
        P(dom, feat, None, None, None),
        P(dom, feat, None),
    )
    return jax.shard_map(
        body,
        mesh=wide,
        in_specs=placed,
        out_specs=(P(dom, feat, None), P(feat, None), P()),
        check_vma=False,
    )
```

```python
import jax
import jax.numpy as jnp
from jax import lax
from jax.experimental import pallas as pl
from jax.experimental.pallas import tpu as pltpu
from jax.sharding import Mesh
from jax.sharding import PartitionSpec as P

BF = jnp.bfloat16
F32 = jnp.float32
I32 = jnp.int32
VMEM = pl.BlockSpec(memory_space=pltpu.VMEM)
SMEM = pl.BlockSpec(memory_space=pltpu.SMEM)
MIB = 1024 * 1024
RING = (0, 1, -1, 2)
NT = (((1,), (1,)), ((), ()))


def dot(a, b, dims=(((1,), (0,)), ((), ()))):
    return lax.dot_general(a, b, dims, preferred_element_type=F32)


def halves(a, b):
    low = lax.broadcasted_iota(I32, a.shape, 1) < 64
    return jnp.where(low, a, pltpu.roll(b, 64, 1)), jnp.where(low, pltpu.roll(a, 64, 1), b)


def owner(block):
    return (block % 4) * 4 + block // 4


def mask_kernel(mask_ref, out_ref):
    for b in range(2):
        for k in range(6):
            out_ref[b * 128 : b * 128 + 128, k * 128 : k * 128 + 128] = (
                mask_ref[b, k].astype(F32).astype(BF)
            )


def node_kernel(up_ref, deg_ref, links_ref, out_ref):
    info, inv = [], []
    for b in range(2):
        degree = deg_ref[b : b + 1, :]
        info += [degree >> 5, degree & 31]
        inv.append(lax.rsqrt(degree.astype(F32)))
    scaled = jnp.concatenate(inv, axis=1) * up_ref[...].astype(F32)
    out_ref[0:160, :] = jnp.concatenate([scaled, jnp.zeros((7, 256), F32)], axis=0).astype(BF)
    info = jnp.concatenate(info + [links_ref[...], jnp.zeros((11, 128), I32)], axis=0)
    out_ref[160:176, 0:128] = info.astype(F32).astype(BF)
    out_ref[160:176, 128:256] = jnp.zeros((16, 128), BF)


def pack_kernel(*refs):
    for k in range(4):
        refs[4 + k // 2][k % 2] = refs[k][0:160, :]


def block_of(m_refs, k, b):
    return m_refs[k][b * 128 : b * 128 + 128, :] if k < 3 else m_refs[3 + b][...]


def info_of(i_refs, k):
    return i_refs[k][160:176, 0:128].astype(F32)


def inverse_of(info, b):
    return lax.rsqrt(info[2 * b : 2 * b + 1] * 32.0 + info[2 * b + 1 : 2 * b + 2])


def features_at(refs, k, f):
    return refs[2 * k + f // 4][f % 4]


def weight_kernel(*refs):
    w_refs, at_ref, out_ref, w_ref = refs[:4], refs[4], refs[5], refs[6]
    for k, shift in enumerate(RING):
        for flip in range(2):
            f = ((at_ref[3] + shift + 4) & 3) * 2 + ((at_ref[4] + flip) & 1)
            w_ref[f] = w_refs[k][flip]
    out_ref[...] = w_ref[...].reshape(768, 256).astype(F32).T.astype(BF)


def project_kernel(*refs):
    x_refs, w_ref, i_refs, out_refs = refs[:8], refs[8], refs[9:13], refs[13:15]
    for k in range(4):
        info = info_of(i_refs, k)
        inv = jnp.concatenate([inverse_of(info, 0), inverse_of(info, 1)], axis=1)
        whole = jnp.concatenate([features_at(x_refs, k, f) for f in range(8)], axis=0)
        out_refs[k // 2][k % 2] = (inv * dot(w_ref[...], whole)).astype(BF)


def collect(refs, base, src_ref, at_ref):
    rows = refs[0].shape[1]
    for i, ref in enumerate(refs):
        x = (at_ref[1] + RING[i // 2] + 4) & 3
        for j in range(2):
            d = x * 4 + ((at_ref[2] + RING[(i % 2) * 2 + j] + 4) & 3)
            for h in range(2):
                src_ref[2 * d + h, base : base + rows] = ref[j, :, h * 128 : h * 128 + 128]


def collect_kernel(*refs):
    collect(refs[:8], 0, refs[9], refs[8])


def scalars(i_refs, stage_ref, links_ref, sem):
    rows = [info_of(i_refs, k)[4:5] for k in range(4)]
    stage_ref[...] = jnp.concatenate(rows + [jnp.zeros((4, 128), F32)], axis=0).astype(I32)
    copy = pltpu.make_async_copy(stage_ref, links_ref, sem)
    copy.start()
    copy.wait()


def spread(sources, links_ref, m_refs, k, b, t):
    def field(c):
        parts = [source[c] for source in sources]
        return parts[0] if len(parts) == 1 else jnp.concatenate(parts, axis=0)

    named = [field(links_ref[k, b * 6 + s]) for s in range(6)]
    total = dot(jnp.concatenate(named, axis=1), block_of(m_refs, k, b), NT)
    return field(t).astype(F32) + total


def first_mix_kernel(*refs):
    s_refs, u_ref, m_refs, sw_ref, at_ref = refs[:8], refs[8], refs[9:14], refs[14], refs[15]
    i_refs, hid_refs, back_refs, second_ref = refs[16:20], refs[20:24], refs[24:26], refs[26]
    src_ref, stage_ref, links_ref, sem = refs[27:]
    scalars(i_refs, stage_ref, links_ref, sem)
    collect(s_refs, 0, src_ref, at_ref)
    second = jnp.zeros((160, 256), F32)
    for k, shift in enumerate(RING):
        z = (at_ref[2] + shift + 4) & 3
        info = info_of(i_refs, k)
        for b in range(2):
            inv = inverse_of(info, b)
            lanes = slice(b * 128, b * 128 + 128)
            total = spread((src_ref, u_ref), links_ref, m_refs, k, b, (at_ref[1] * 4 + z) * 2 + b)
            m = inv * total[0:256]
            s = jax.nn.sigmoid(m)
            hid = (m * s).astype(BF)
            hid_refs[k][:, lanes] = hid
            one = (inv * hid.astype(F32)).astype(BF)
            pull = total[256:416].astype(BF)
            second = second + dot(pull, one, NT)
            slope = s * (1.0 + m * (1.0 - s))
            back = inv * inv * dot(sw_ref[...], pull) * slope
            back_refs[k // 2][k % 2, :, lanes] = back.astype(BF)
    second_ref[...] = second


def second_mix_kernel(*refs):
    b_refs, m_refs, x_refs, second_ref, at_ref = refs[:8], refs[8:13], refs[13:21], refs[21], refs[22]
    i_refs, out_ref, src_ref, stage_ref, links_ref, sem = refs[23:27], *refs[27:]
    scalars(i_refs, stage_ref, links_ref, sem)
    collect(b_refs, 0, src_ref, at_ref)
    rights = []
    for k, shift in enumerate(RING):
        z = (at_ref[2] + shift + 4) & 3
        info = info_of(i_refs, k)
        parts = []
        for b in range(2):
            total = spread((src_ref,), links_ref, m_refs, k, b, (at_ref[1] * 4 + z) * 2 + b)
            parts.append((inverse_of(info, b) * total).astype(BF))
        rights.append(jnp.concatenate(parts, axis=1))
    seconds = []
    for p in range(2):
        m = second_ref[:, p * 128 : p * 128 + 128]
        seconds += halves(m[:80], m[80:])
    for f in range(8):
        acc = jnp.zeros((96, 256), F32)
        for k, right in enumerate(rights):
            acc = acc + dot(features_at(x_refs, k, f), right, NT)
        for p in range(2):
            g = acc[:, p * 128 : p * 128 + 128]
            for q, part in enumerate(halves(g[:48], g[48:])):
                both = jnp.concatenate([part, seconds[2 * p + q]], axis=0)
                out_ref[f, 2 * p + q] = both.astype(BF)


def add_kernel(part_ref, out_ref):
    total = part_ref[0].astype(F32)
    for i in range(1, 32):
        total = total + part_ref[i].astype(F32)
    total = total.astype(BF)
    for d in range(16):
        out_ref[d] = total


def hidden_kernel(h0_ref, h1_ref, h2_ref, h3_ref, at_ref, out_ref):
    for ref, shift in zip((h0_ref, h1_ref, h2_ref, h3_ref), RING):
        at = pl.multiple_of(((at_ref[2] - shift + 4) & 3) * 256, 256)
        out_ref[:, pl.ds(at, 256)] = ref[...].astype(F32).T.astype(BF)


def gradient_kernel(in_ref, first_ref, second_ref):
    for j in range(8):
        cols = pl.ds(j * 128, 128)
        one, two = halves(in_ref[owner(2 * j)].astype(F32), in_ref[owner(2 * j + 1)].astype(F32))
        first_ref[0:48, cols] = one[:48]
        first_ref[48:96, cols] = two[:48]
        second_ref[0:80, cols] = one[48:]
        second_ref[80:153, cols] = two[48:121]


def call(kernel, shape, specs, scratch=(), flops=0, moved=0, limit=20):
    return pl.pallas_call(
        kernel,
        out_shape=shape,
        in_specs=specs,
        out_specs=jax.tree.map(lambda _: VMEM, shape),
        scratch_shapes=list(scratch),
        compiler_params=pltpu.CompilerParams(vmem_limit_bytes=limit * MIB),
        cost_estimate=pl.CostEstimate(flops=flops, bytes_accessed=moved, transcendentals=0),
    )


def fetch(value, axis, shift):
    return lax.ppermute(value, axis, [((i + shift) % 4, i) for i in range(4)])


def ring(value, axis):
    return [value] + [fetch(value, axis, shift) for shift in RING[1:]]


def near(value, axis):
    return fetch(value, axis, 1), fetch(value, axis, -1)


def neighbours(low, high, axis):
    return fetch(low, axis, 1), fetch(high, axis, -1), fetch(high, axis, 1), fetch(low, axis, -1)


def rounds(low, high, found, passed, axis):
    far = fetch(passed[0], axis, 1), fetch(passed[1], axis, -1)
    return [low, high, passed[0], found[2], found[3], passed[1], *far]


def body(features, first_weight, second_weight, degree, neighbour_block, neighbour_mask, upstream):
    feat, dom = ("y", "c"), ("x", "z")
    shape = jax.ShapeDtypeStruct
    x, z = lax.axis_index("x"), lax.axis_index("z")
    at = jnp.stack([x * 4 + z, x, z, lax.axis_index("y"), lax.axis_index("c")])
    x_own = lax.all_to_all(
        features.reshape(96, 8, 256).transpose(1, 0, 2), feat, 0, 0, tiled=True
    )
    weight = lax.dynamic_slice(first_weight, (0, z * 256), (96, 256))
    other = lax.ppermute(weight, "c", [(0, 1), (1, 0)])
    other, degree = lax.optimization_barrier((other, degree))
    links = jnp.pad(jnp.maximum(neighbour_block.reshape(1, 12), 0), ((0, 0), (0, 116)))
    nodes = call(node_kernel, shape((176, 256), BF), [VMEM] * 3, moved=200_000)(
        upstream[0].T, degree.reshape(2, 128), links
    )
    nodes = ring(nodes, "z")
    half = shape((2, 160, 256), BF)
    scaled = call(pack_kernel, (half, half), [VMEM] * 4, moved=600_000)(*nodes)
    mask = call(mask_kernel, shape((256, 768), BF), [VMEM], moved=1_200_000)(neighbour_mask[0])
    own_second = lax.dynamic_slice(second_weight, (z * 256, 0), (256, 153))
    own_second = jnp.pad(own_second, ((0, 0), (0, 7)))
    weights = call(
        weight_kernel, shape((256, 768), BF), [VMEM] * 4 + [SMEM], [pltpu.VMEM((8, 96, 256), BF)],
        moved=800_000,
    )(*ring(jnp.stack([weight, other]), "y"), at)
    x_low, x_high, mask, own_second, weights, n1, n2, n3 = lax.optimization_barrier(
        (x_own[:4], x_own[4:], mask, own_second, weights, *nodes[1:])
    )
    nodes = [nodes[0], n1, n2, n3]
    x_near = neighbours(x_low, x_high, "z")
    x0, x1, *scaled = lax.optimization_barrier((*x_near[:2], *scaled))
    x_wide = rounds(x_low, x_high, x_near, (x0, x1), "z")
    u_near = neighbours(*scaled, "x")
    scaled = rounds(*scaled, u_near, u_near[:2], "x")
    scaled = call(collect_kernel, shape((32, 160, 128), BF), [VMEM] * 8 + [SMEM], moved=2_600_000)(
        *scaled, at
    )
    half = shape((2, 256, 256), BF)
    s = call(
        project_kernel,
        (half, half),
        [VMEM] * 13,
        flops=400_000_000,
        moved=3_000_000,
    )(*x_wide, weights, *nodes)
    *s, mask = lax.optimization_barrier((*s, mask))
    s_near = neighbours(*s, "x")
    after, before = near(mask, "z")
    s0, s1, scaled = lax.optimization_barrier((*s_near[:2], scaled))
    s = rounds(*s, s_near, (s0, s1), "x")
    masks = [mask, after, before, fetch(after[:128], "z", 1), fetch(before[128:], "z", -1)]
    links_scratch = [
        pltpu.VMEM((8, 128), I32), pltpu.SMEM((8, 128), I32), pltpu.SemaphoreType.DMA
    ]
    *hid, low, high, second = call(
        first_mix_kernel,
        (shape((256, 256), BF),) * 4 + (half, half, shape((160, 256), F32)),
        [VMEM] * 15 + [SMEM] + [VMEM] * 4,
        [pltpu.VMEM((32, 256, 128), BF), *links_scratch],
        flops=700_000_000,
        moved=8_000_000,
    )(*s, scaled, *masks, own_second, at, *nodes)
    b_near = neighbours(low, high, "x")
    *passed, h1, h2, h3 = lax.optimization_barrier((*b_near[:2], *hid[1:]))
    back = rounds(low, high, b_near, passed, "x")
    hid = [hid[0]] + [fetch(value, "z", -shift) for value, shift in zip((h1, h2, h3), RING[1:])]
    part = call(
        second_mix_kernel,
        shape((8, 4, 128, 128), BF),
        [VMEM] * 22 + [SMEM] + [VMEM] * 4,
        [pltpu.VMEM((32, 256, 128), BF), *links_scratch],
        flops=900_000_000,
        moved=8_000_000,
    )(*back, *masks, *x_wide, second, at, *nodes)
    part, *hid = lax.optimization_barrier((part, *hid))
    part = lax.all_to_all(part.reshape(32, 128, 128), ("y", "c", "x"), 0, 0, tiled=True)
    tile = shape((16, 128, 128), BF)
    done = call(add_kernel, tile, [VMEM], moved=1_500_000)(part)
    done = lax.all_to_all(done, dom, 0, 0, tiled=True)
    hidden = call(hidden_kernel, shape((256, 1024), BF), [VMEM] * 4 + [SMEM], moved=1_000_000)(*hid, at)
    grad_first, grad_second = call(
        gradient_kernel, (shape((96, 1024), F32), shape((153, 1024), F32)), [VMEM], moved=1_500_000
    )(done)
    return (hidden[None], grad_first, grad_second.T)


def solution(mesh):
    wide = Mesh(mesh.devices.reshape(4, 2, 4, 4), ("y", "c", "x", "z"))
    feat, dom = ("y", "c"), ("x", "z")
    placed = (
        P(feat, dom, None),
        P(feat, None),
        P(),
        P(dom, feat),
        P(dom, feat, None),
        P(dom, feat, None, None, None),
        P(dom, feat, None),
    )
    return jax.shard_map(
        body,
        mesh=wide,
        in_specs=placed,
        out_specs=(P(dom, feat, None), P(feat, None), P()),
        check_vma=False,
    )
```

```python
import jax
import jax.numpy as jnp
from jax import lax
from jax.experimental import pallas as pl
from jax.experimental.pallas import tpu as pltpu
from jax.sharding import Mesh
from jax.sharding import PartitionSpec as P

BF = jnp.bfloat16
F32 = jnp.float32
I32 = jnp.int32
VMEM = pl.BlockSpec(memory_space=pltpu.VMEM)
SMEM = pl.BlockSpec(memory_space=pltpu.SMEM)
MIB = 1024 * 1024
RING = (0, 1, -1, 2)
NT = (((1,), (1,)), ((), ()))


def dot(a, b, dims=(((1,), (0,)), ((), ()))):
    return lax.dot_general(a, b, dims, preferred_element_type=F32)


def halves(a, b):
    low = lax.broadcasted_iota(I32, a.shape, 1) < 64
    return jnp.where(low, a, pltpu.roll(b, 64, 1)), jnp.where(low, pltpu.roll(a, 64, 1), b)


def owner(block):
    return (block % 4) * 4 + block // 4


def mask_kernel(mask_ref, out_ref):
    for b in range(2):
        for k in range(6):
            out_ref[b * 128 : b * 128 + 128, k * 128 : k * 128 + 128] = (
                mask_ref[b, k].astype(F32).astype(BF)
            )


def node_kernel(up_ref, deg_ref, links_ref, out_ref):
    info, inv = [], []
    for b in range(2):
        degree = deg_ref[b : b + 1, :]
        info += [degree >> 5, degree & 31]
        inv.append(lax.rsqrt(degree.astype(F32)))
    scaled = jnp.concatenate(inv, axis=1) * up_ref[...].astype(F32)
    out_ref[0:160, :] = jnp.concatenate([scaled, jnp.zeros((7, 256), F32)], axis=0).astype(BF)
    info = jnp.concatenate(info + [links_ref[...], jnp.zeros((11, 128), I32)], axis=0)
    out_ref[160:176, 0:128] = info.astype(F32).astype(BF)
    out_ref[160:176, 128:256] = jnp.zeros((16, 128), BF)


def pack_kernel(*refs):
    for k in range(4):
        refs[4 + k // 2][k % 2] = refs[k][0:160, :]


def block_of(m_refs, k, b):
    return m_refs[k][b * 128 : b * 128 + 128, :] if k < 3 else m_refs[3 + b][...]


def info_of(i_refs, k):
    return i_refs[k][160:176, 0:128].astype(F32)


def inverse_of(info, b):
    return lax.rsqrt(info[2 * b : 2 * b + 1] * 32.0 + info[2 * b + 1 : 2 * b + 2])


def features_at(refs, k, f):
    return refs[2 * k + f // 4][f % 4]


def weight_kernel(*refs):
    w_refs, at_ref, out_ref, w_ref = refs[:4], refs[4], refs[5], refs[6]
    for k, shift in enumerate(RING):
        for flip in range(2):
            f = ((at_ref[3] + shift + 4) & 3) * 2 + ((at_ref[4] + flip) & 1)
            w_ref[f] = w_refs[k][flip]
    out_ref[...] = w_ref[...].reshape(768, 256).astype(F32).T.astype(BF)


def project_kernel(*refs):
    x_refs, w_ref, i_refs, out_refs = refs[:8], refs[8], refs[9:13], refs[13:15]
    for k in range(4):
        info = info_of(i_refs, k)
        inv = jnp.concatenate([inverse_of(info, 0), inverse_of(info, 1)], axis=1)
        whole = jnp.concatenate([features_at(x_refs, k, f) for f in range(8)], axis=0)
        out_refs[k // 2][k % 2] = (inv * dot(w_ref[...], whole)).astype(BF)


def collect(refs, base, src_ref, at_ref):
    rows = refs[0].shape[1]
    for i, ref in enumerate(refs):
        x = (at_ref[1] + RING[i // 2] + 4) & 3
        for j in range(2):
            d = x * 4 + ((at_ref[2] + RING[(i % 2) * 2 + j] + 4) & 3)
            for h in range(2):
                src_ref[2 * d + h, base : base + rows] = ref[j, :, h * 128 : h * 128 + 128]


def collect_kernel(*refs):
    collect(refs[:8], 0, refs[9], refs[8])


def scalars(i_refs, stage_ref, links_ref, sem):
    rows = [info_of(i_refs, k)[4:5] for k in range(4)]
    stage_ref[...] = jnp.concatenate(rows + [jnp.zeros((4, 128), F32)], axis=0).astype(I32)
    copy = pltpu.make_async_copy(stage_ref, links_ref, sem)
    copy.start()
    copy.wait()


def spread(sources, links_ref, m_refs, k, b, t):
    def field(c):
        parts = [source[c] for source in sources]
        return parts[0] if len(parts) == 1 else jnp.concatenate(parts, axis=0)

    named = [field(links_ref[k, b * 6 + s]) for s in range(6)]
    total = dot(jnp.concatenate(named, axis=1), block_of(m_refs, k, b), NT)
    return field(t).astype(F32) + total


def first_mix_kernel(*refs):
    s_refs, u_ref, m_refs, sw_ref, at_ref = refs[:8], refs[8], refs[9:14], refs[14], refs[15]
    i_refs, hid_refs, back_refs, second_ref = refs[16:20], refs[20:24], refs[24:26], refs[26]
    src_ref, stage_ref, links_ref, sem = refs[27:]
    scalars(i_refs, stage_ref, links_ref, sem)
    collect(s_refs, 0, src_ref, at_ref)
    second = jnp.zeros((160, 256), F32)
    for k, shift in enumerate(RING):
        z = (at_ref[2] + shift + 4) & 3
        info = info_of(i_refs, k)
        for b in range(2):
            inv = inverse_of(info, b)
            lanes = slice(b * 128, b * 128 + 128)
            total = spread((src_ref, u_ref), links_ref, m_refs, k, b, (at_ref[1] * 4 + z) * 2 + b)
            m = inv * total[0:256]
            s = jax.nn.sigmoid(m)
            hid = (m * s).astype(BF)
            hid_refs[k][:, lanes] = hid
            one = (inv * hid.astype(F32)).astype(BF)
            pull = total[256:416].astype(BF)
            second = second + dot(pull, one, NT)
            slope = s * (1.0 + m * (1.0 - s))
            back = inv * inv * dot(sw_ref[...], pull) * slope
            back_refs[k // 2][k % 2, :, lanes] = back.astype(BF)
    second_ref[...] = second


def second_mix_kernel(*refs):
    b_refs, m_refs, x_refs, second_ref, at_ref = refs[:8], refs[8:13], refs[13:21], refs[21], refs[22]
    i_refs, out_ref, src_ref, stage_ref, links_ref, sem = refs[23:27], *refs[27:]
    scalars(i_refs, stage_ref, links_ref, sem)
    collect(b_refs, 0, src_ref, at_ref)
    rights = []
    for k, shift in enumerate(RING):
        z = (at_ref[2] + shift + 4) & 3
        info = info_of(i_refs, k)
        parts = []
        for b in range(2):
            total = spread((src_ref,), links_ref, m_refs, k, b, (at_ref[1] * 4 + z) * 2 + b)
            parts.append((inverse_of(info, b) * total).astype(BF))
        rights.append(jnp.concatenate(parts, axis=1))
    seconds = []
    for p in range(2):
        m = second_ref[:, p * 128 : p * 128 + 128]
        seconds += halves(m[:80], m[80:])
    for f in range(8):
        acc = jnp.zeros((96, 256), F32)
        for k, right in enumerate(rights):
            acc = acc + dot(features_at(x_refs, k, f), right, NT)
        for p in range(2):
            g = acc[:, p * 128 : p * 128 + 128]
            for q, part in enumerate(halves(g[:48], g[48:])):
                both = jnp.concatenate([part, seconds[2 * p + q]], axis=0)
                out_ref[f, 2 * p + q] = both.astype(BF)


def add_kernel(part_ref, out_ref):
    total = part_ref[0].astype(F32)
    for i in range(1, 32):
        total = total + part_ref[i].astype(F32)
    total = total.astype(BF)
    for d in range(16):
        out_ref[d] = total


def hidden_kernel(h0_ref, h1_ref, h2_ref, h3_ref, at_ref, out_ref):
    for ref, shift in zip((h0_ref, h1_ref, h2_ref, h3_ref), RING):
        at = pl.multiple_of(((at_ref[2] - shift + 4) & 3) * 256, 256)
        out_ref[:, pl.ds(at, 256)] = ref[...].astype(F32).T.astype(BF)


def gradient_kernel(in_ref, first_ref, second_ref):
    for j in range(8):
        cols = pl.ds(j * 128, 128)
        one, two = halves(in_ref[owner(2 * j)].astype(F32), in_ref[owner(2 * j + 1)].astype(F32))
        first_ref[0:48, cols] = one[:48]
        first_ref[48:96, cols] = two[:48]
        second_ref[0:80, cols] = one[48:]
        second_ref[80:153, cols] = two[48:121]


def call(kernel, shape, specs, scratch=(), flops=0, moved=0, limit=20):
    return pl.pallas_call(
        kernel,
        out_shape=shape,
        in_specs=specs,
        out_specs=jax.tree.map(lambda _: VMEM, shape),
        scratch_shapes=list(scratch),
        compiler_params=pltpu.CompilerParams(vmem_limit_bytes=limit * MIB),
        cost_estimate=pl.CostEstimate(flops=flops, bytes_accessed=moved, transcendentals=0),
    )


def fetch(value, axis, shift):
    return lax.ppermute(value, axis, [((i + shift) % 4, i) for i in range(4)])


def ring(value, axis):
    return [value] + [fetch(value, axis, shift) for shift in RING[1:]]


def near(value, axis):
    return fetch(value, axis, 1), fetch(value, axis, -1)


def neighbours(low, high, axis):
    return fetch(low, axis, 1), fetch(high, axis, -1), fetch(high, axis, 1), fetch(low, axis, -1)


def rounds(low, high, found, passed, axis):
    far = fetch(passed[0], axis, 1), fetch(passed[1], axis, -1)
    return [low, high, passed[0], found[2], found[3], passed[1], *far]


def body(features, first_weight, second_weight, degree, neighbour_block, neighbour_mask, upstream):
    feat, dom = ("y", "c"), ("x", "z")
    shape = jax.ShapeDtypeStruct
    x, z = lax.axis_index("x"), lax.axis_index("z")
    at = jnp.stack([x * 4 + z, x, z, lax.axis_index("y"), lax.axis_index("c")])
    x_own = lax.all_to_all(
        features.reshape(96, 8, 256).transpose(1, 0, 2), feat, 0, 0, tiled=True
    )
    weight = lax.dynamic_slice(first_weight, (0, z * 256), (96, 256))
    other = lax.ppermute(weight, "c", [(0, 1), (1, 0)])
    other, degree = lax.optimization_barrier((other, degree))
    links = jnp.pad(jnp.maximum(neighbour_block.reshape(1, 12), 0), ((0, 0), (0, 116)))
    nodes = call(node_kernel, shape((176, 256), BF), [VMEM] * 3, moved=200_000)(
        upstream[0].T, degree.reshape(2, 128), links
    )
    mask = call(mask_kernel, shape((256, 768), BF), [VMEM], moved=1_200_000)(neighbour_mask[0])
    own_second = lax.dynamic_slice(second_weight, (z * 256, 0), (256, 153))
    own_second = jnp.pad(own_second, ((0, 0), (0, 7)))
    weights = call(
        weight_kernel, shape((256, 768), BF), [VMEM] * 4 + [SMEM], [pltpu.VMEM((8, 96, 256), BF)],
        moved=800_000,
    )(*ring(jnp.stack([weight, other]), "y"), at)
    x_low, x_high, mask, own_second, weights, nodes = lax.optimization_barrier(
        (x_own[:4], x_own[4:], mask, own_second, weights, nodes)
    )
    x_near = neighbours(x_low, x_high, "z")
    nodes = ring(nodes, "z")
    half = shape((2, 160, 256), BF)
    scaled = call(pack_kernel, (half, half), [VMEM] * 4, moved=600_000)(*nodes)
    x0, x1, *scaled = lax.optimization_barrier((*x_near[:2], *scaled))
    x_wide = rounds(x_low, x_high, x_near, (x0, x1), "z")
    u_near = neighbours(*scaled, "x")
    scaled = rounds(*scaled, u_near, u_near[:2], "x")
    scaled = call(collect_kernel, shape((32, 160, 128), BF), [VMEM] * 8 + [SMEM], moved=2_600_000)(
        *scaled, at
    )
    half = shape((2, 256, 256), BF)
    s = call(
        project_kernel,
        (half, half),
        [VMEM] * 13,
        flops=400_000_000,
        moved=3_000_000,
    )(*x_wide, weights, *nodes)
    *s, mask = lax.optimization_barrier((*s, mask))
    s_near = neighbours(*s, "x")
    after, before = near(mask, "z")
    s0, s1, scaled = lax.optimization_barrier((*s_near[:2], scaled))
    s = rounds(*s, s_near, (s0, s1), "x")
    masks = [mask, after, before, fetch(after[:128], "z", 1), fetch(before[128:], "z", -1)]
    links_scratch = [
        pltpu.VMEM((8, 128), I32), pltpu.SMEM((8, 128), I32), pltpu.SemaphoreType.DMA
    ]
    *hid, low, high, second = call(
        first_mix_kernel,
        (shape((256, 256), BF),) * 4 + (half, half, shape((160, 256), F32)),
        [VMEM] * 15 + [SMEM] + [VMEM] * 4,
        [pltpu.VMEM((32, 256, 128), BF), *links_scratch],
        flops=700_000_000,
        moved=8_000_000,
    )(*s, scaled, *masks, own_second, at, *nodes)
    b_near = neighbours(low, high, "x")
    *passed, h1, h2, h3 = lax.optimization_barrier((*b_near[:2], *hid[1:]))
    back = rounds(low, high, b_near, passed, "x")
    hid = [hid[0]] + [fetch(value, "z", -shift) for value, shift in zip((h1, h2, h3), RING[1:])]
    part = call(
        second_mix_kernel,
        shape((8, 4, 128, 128), BF),
        [VMEM] * 22 + [SMEM] + [VMEM] * 4,
        [pltpu.VMEM((32, 256, 128), BF), *links_scratch],
        flops=900_000_000,
        moved=8_000_000,
    )(*back, *masks, *x_wide, second, at, *nodes)
    part, *hid = lax.optimization_barrier((part, *hid))
    part = lax.all_to_all(part.reshape(32, 128, 128), ("y", "c", "x"), 0, 0, tiled=True)
    tile = shape((16, 128, 128), BF)
    done = call(add_kernel, tile, [VMEM], moved=1_500_000)(part)
    done = lax.all_to_all(done, dom, 0, 0, tiled=True)
    hidden = call(hidden_kernel, shape((256, 1024), BF), [VMEM] * 4 + [SMEM], moved=1_000_000)(*hid, at)
    grad_first, grad_second = call(
        gradient_kernel, (shape((96, 1024), F32), shape((153, 1024), F32)), [VMEM], moved=1_500_000
    )(done)
    return (hidden[None], grad_first, grad_second.T)


def solution(mesh):
    wide = Mesh(mesh.devices.reshape(4, 2, 4, 4), ("y", "c", "x", "z"))
    feat, dom = ("y", "c"), ("x", "z")
    placed = (
        P(feat, dom, None),
        P(feat, None),
        P(),
        P(dom, feat),
        P(dom, feat, None),
        P(dom, feat, None, None, None),
        P(dom, feat, None),
    )
    return jax.shard_map(
        body,
        mesh=wide,
        in_specs=placed,
        out_specs=(P(dom, feat, None), P(feat, None), P()),
        check_vma=False,
    )
```

```python
import jax
import jax.numpy as jnp
from jax import lax
from jax.experimental import pallas as pl
from jax.experimental.pallas import tpu as pltpu
from jax.sharding import Mesh
from jax.sharding import PartitionSpec as P

BF = jnp.bfloat16
F32 = jnp.float32
I32 = jnp.int32
VMEM = pl.BlockSpec(memory_space=pltpu.VMEM)
SMEM = pl.BlockSpec(memory_space=pltpu.SMEM)
MIB = 1024 * 1024
RING = (0, 1, -1, 2)
NT = (((1,), (1,)), ((), ()))


def dot(a, b, dims=(((1,), (0,)), ((), ()))):
    return lax.dot_general(a, b, dims, preferred_element_type=F32)


def halves(a, b):
    low = lax.broadcasted_iota(I32, a.shape, 1) < 64
    return jnp.where(low, a, pltpu.roll(b, 64, 1)), jnp.where(low, pltpu.roll(a, 64, 1), b)


def owner(block):
    return (block % 4) * 4 + block // 4


def mask_kernel(mask_ref, out_ref):
    for b in range(2):
        for k in range(6):
            out_ref[b * 128 : b * 128 + 128, k * 128 : k * 128 + 128] = (
                mask_ref[b, k].astype(F32).astype(BF)
            )


def node_kernel(up_ref, deg_ref, links_ref, out_ref):
    info, inv = [], []
    for b in range(2):
        degree = deg_ref[b : b + 1, :]
        info += [degree >> 5, degree & 31]
        inv.append(lax.rsqrt(degree.astype(F32)))
    scaled = jnp.concatenate(inv, axis=1) * up_ref[...].astype(F32)
    out_ref[0:160, :] = jnp.concatenate([scaled, jnp.zeros((7, 256), F32)], axis=0).astype(BF)
    info = jnp.concatenate(info + [links_ref[...], jnp.zeros((11, 128), I32)], axis=0)
    out_ref[160:176, 0:128] = info.astype(F32).astype(BF)
    out_ref[160:176, 128:256] = jnp.zeros((16, 128), BF)


def pack_kernel(*refs):
    for k in range(4):
        refs[4 + k // 2][k % 2] = refs[k][0:160, :]


def block_of(m_refs, k, b):
    return m_refs[k][b * 128 : b * 128 + 128, :] if k < 3 else m_refs[3 + b][...]


def info_of(i_refs, k):
    return i_refs[k][160:176, 0:128].astype(F32)


def inverse_of(info, b):
    return lax.rsqrt(info[2 * b : 2 * b + 1] * 32.0 + info[2 * b + 1 : 2 * b + 2])


def features_at(refs, k, f):
    return refs[2 * k + f // 4][f % 4]


def weight_kernel(*refs):
    w_refs, at_ref, out_ref, w_ref = refs[:4], refs[4], refs[5], refs[6]
    for k, shift in enumerate(RING):
        for flip in range(2):
            f = ((at_ref[3] + shift + 4) & 3) * 2 + ((at_ref[4] + flip) & 1)
            w_ref[f] = w_refs[k][flip]
    out_ref[...] = w_ref[...].reshape(768, 256).astype(F32).T.astype(BF)


def project_kernel(*refs):
    x_refs, w_ref, i_refs, out_refs = refs[:8], refs[8], refs[9:13], refs[13:15]
    for k in range(4):
        info = info_of(i_refs, k)
        inv = jnp.concatenate([inverse_of(info, 0), inverse_of(info, 1)], axis=1)
        whole = jnp.concatenate([features_at(x_refs, k, f) for f in range(8)], axis=0)
        out_refs[k // 2][k % 2] = (inv * dot(w_ref[...], whole)).astype(BF)


def collect(refs, base, src_ref, at_ref):
    rows = refs[0].shape[1]
    for i, ref in enumerate(refs):
        x = (at_ref[1] + RING[i // 2] + 4) & 3
        for j in range(2):
            d = x * 4 + ((at_ref[2] + RING[(i % 2) * 2 + j] + 4) & 3)
            for h in range(2):
                src_ref[2 * d + h, base : base + rows] = ref[j, :, h * 128 : h * 128 + 128]


def collect_kernel(*refs):
    collect(refs[:8], 0, refs[9], refs[8])


def scalars(i_refs, stage_ref, links_ref, sem):
    rows = [info_of(i_refs, k)[4:5] for k in range(4)]
    stage_ref[...] = jnp.concatenate(rows + [jnp.zeros((4, 128), F32)], axis=0).astype(I32)
    copy = pltpu.make_async_copy(stage_ref, links_ref, sem)
    copy.start()
    copy.wait()


def spread(sources, links_ref, m_refs, k, b, t):
    def field(c):
        parts = [source[c] for source in sources]
        return parts[0] if len(parts) == 1 else jnp.concatenate(parts, axis=0)

    named = [field(links_ref[k, b * 6 + s]) for s in range(6)]
    total = dot(jnp.concatenate(named, axis=1), block_of(m_refs, k, b), NT)
    return field(t).astype(F32) + total


def first_mix_kernel(*refs):
    s_refs, u_ref, m_refs, sw_ref, at_ref = refs[:8], refs[8], refs[9:14], refs[14], refs[15]
    i_refs, hid_refs, back_refs, second_ref = refs[16:20], refs[20:24], refs[24:26], refs[26]
    src_ref, stage_ref, links_ref, sem = refs[27:]
    scalars(i_refs, stage_ref, links_ref, sem)
    collect(s_refs, 0, src_ref, at_ref)
    second = jnp.zeros((160, 256), F32)
    for k, shift in enumerate(RING):
        z = (at_ref[2] + shift + 4) & 3
        info = info_of(i_refs, k)
        for b in range(2):
            inv = inverse_of(info, b)
            lanes = slice(b * 128, b * 128 + 128)
            total = spread((src_ref, u_ref), links_ref, m_refs, k, b, (at_ref[1] * 4 + z) * 2 + b)
            m = inv * total[0:256]
            s = jax.nn.sigmoid(m)
            hid = (m * s).astype(BF)
            hid_refs[k][:, lanes] = hid
            one = (inv * hid.astype(F32)).astype(BF)
            pull = total[256:416].astype(BF)
            second = second + dot(pull, one, NT)
            slope = s * (1.0 + m * (1.0 - s))
            back = inv * inv * dot(sw_ref[...], pull) * slope
            back_refs[k // 2][k % 2, :, lanes] = back.astype(BF)
    second_ref[...] = second


def second_mix_kernel(*refs):
    b_refs, m_refs, x_refs, second_ref, at_ref = refs[:8], refs[8:13], refs[13:21], refs[21], refs[22]
    i_refs, out_ref, src_ref, stage_ref, links_ref, sem = refs[23:27], *refs[27:]
    scalars(i_refs, stage_ref, links_ref, sem)
    collect(b_refs, 0, src_ref, at_ref)
    rights = []
    for k, shift in enumerate(RING):
        z = (at_ref[2] + shift + 4) & 3
        info = info_of(i_refs, k)
        parts = []
        for b in range(2):
            total = spread((src_ref,), links_ref, m_refs, k, b, (at_ref[1] * 4 + z) * 2 + b)
            parts.append((inverse_of(info, b) * total).astype(BF))
        rights.append(jnp.concatenate(parts, axis=1))
    seconds = []
    for p in range(2):
        m = second_ref[:, p * 128 : p * 128 + 128]
        seconds += halves(m[:80], m[80:])
    for f in range(8):
        acc = jnp.zeros((96, 256), F32)
        for k, right in enumerate(rights):
            acc = acc + dot(features_at(x_refs, k, f), right, NT)
        for p in range(2):
            g = acc[:, p * 128 : p * 128 + 128]
            for q, part in enumerate(halves(g[:48], g[48:])):
                both = jnp.concatenate([part, seconds[2 * p + q]], axis=0)
                out_ref[f, 2 * p + q] = both.astype(BF)


def add_kernel(part_ref, out_ref):
    total = part_ref[0].astype(F32)
    for i in range(1, 32):
        total = total + part_ref[i].astype(F32)
    total = total.astype(BF)
    for d in range(16):
        out_ref[d] = total


def hidden_kernel(h0_ref, h1_ref, h2_ref, h3_ref, at_ref, out_ref):
    for ref, shift in zip((h0_ref, h1_ref, h2_ref, h3_ref), RING):
        at = pl.multiple_of(((at_ref[2] - shift + 4) & 3) * 256, 256)
        out_ref[:, pl.ds(at, 256)] = ref[...].astype(F32).T.astype(BF)


def gradient_kernel(in_ref, first_ref, second_ref):
    for j in range(8):
        cols = pl.ds(j * 128, 128)
        one, two = halves(in_ref[owner(2 * j)].astype(F32), in_ref[owner(2 * j + 1)].astype(F32))
        first_ref[0:48, cols] = one[:48]
        first_ref[48:96, cols] = two[:48]
        second_ref[0:80, cols] = one[48:]
        second_ref[80:153, cols] = two[48:121]


def call(kernel, shape, specs, scratch=(), flops=0, moved=0, limit=20):
    return pl.pallas_call(
        kernel,
        out_shape=shape,
        in_specs=specs,
        out_specs=jax.tree.map(lambda _: VMEM, shape),
        scratch_shapes=list(scratch),
        compiler_params=pltpu.CompilerParams(vmem_limit_bytes=limit * MIB),
        cost_estimate=pl.CostEstimate(flops=flops, bytes_accessed=moved, transcendentals=0),
    )


def fetch(value, axis, shift):
    return lax.ppermute(value, axis, [((i + shift) % 4, i) for i in range(4)])


def ring(value, axis):
    return [value] + [fetch(value, axis, shift) for shift in RING[1:]]


def near(value, axis):
    return fetch(value, axis, 1), fetch(value, axis, -1)


def neighbours(low, high, axis):
    return fetch(low, axis, 1), fetch(high, axis, -1), fetch(high, axis, 1), fetch(low, axis, -1)


def rounds(low, high, found, passed, axis):
    far = fetch(passed[0], axis, 1), fetch(passed[1], axis, -1)
    return [low, high, passed[0], found[2], found[3], passed[1], *far]


def body(features, first_weight, second_weight, degree, neighbour_block, neighbour_mask, upstream):
    feat, dom = ("y", "c"), ("x", "z")
    shape = jax.ShapeDtypeStruct
    x, z = lax.axis_index("x"), lax.axis_index("z")
    at = jnp.stack([x * 4 + z, x, z, lax.axis_index("y"), lax.axis_index("c")])
    x_own = lax.all_to_all(
        features.reshape(96, 8, 256).transpose(1, 0, 2), feat, 0, 0, tiled=True
    )
    weight = lax.dynamic_slice(first_weight, (0, z * 256), (96, 256))
    other = lax.ppermute(weight, "c", [(0, 1), (1, 0)])
    other, degree = lax.optimization_barrier((other, degree))
    links = jnp.pad(jnp.maximum(neighbour_block.reshape(1, 12), 0), ((0, 0), (0, 116)))
    nodes = call(node_kernel, shape((176, 256), BF), [VMEM] * 3, moved=200_000)(
        upstream[0].T, degree.reshape(2, 128), links
    )
    nodes = ring(nodes, "z")
    half = shape((2, 160, 256), BF)
    scaled = call(pack_kernel, (half, half), [VMEM] * 4, moved=600_000)(*nodes)
    mask = call(mask_kernel, shape((256, 768), BF), [VMEM], moved=1_200_000)(neighbour_mask[0])
    own_second = lax.dynamic_slice(second_weight, (z * 256, 0), (256, 153))
    own_second = jnp.pad(own_second, ((0, 0), (0, 7)))
    weights = call(
        weight_kernel, shape((256, 768), BF), [VMEM] * 4 + [SMEM], [pltpu.VMEM((8, 96, 256), BF)],
        moved=800_000,
    )(*ring(jnp.stack([weight, other]), "y"), at)
    x_low, x_high, mask, own_second, weights, n1, n2, n3 = lax.optimization_barrier(
        (x_own[:4], x_own[4:], mask, own_second, weights, *nodes[1:])
    )
    nodes = [nodes[0], n1, n2, n3]
    x_near = neighbours(x_low, x_high, "z")
    x0, x1 = x_near[:2]
    x_wide = rounds(x_low, x_high, x_near, (x0, x1), "z")
    u_near = neighbours(*scaled, "x")
    scaled = rounds(*scaled, u_near, u_near[:2], "x")
    scaled = call(collect_kernel, shape((32, 160, 128), BF), [VMEM] * 8 + [SMEM], moved=2_600_000)(
        *scaled, at
    )
    half = shape((2, 256, 256), BF)
    s = call(
        project_kernel,
        (half, half),
        [VMEM] * 13,
        flops=400_000_000,
        moved=3_000_000,
    )(*x_wide, weights, *nodes)
    *s, mask = lax.optimization_barrier((*s, mask))
    s_near = neighbours(*s, "x")
    after, before = near(mask, "z")
    s0, s1, scaled = lax.optimization_barrier((*s_near[:2], scaled))
    s = rounds(*s, s_near, (s0, s1), "x")
    masks = [mask, after, before, fetch(after[:128], "z", 1), fetch(before[128:], "z", -1)]
    links_scratch = [
        pltpu.VMEM((8, 128), I32), pltpu.SMEM((8, 128), I32), pltpu.SemaphoreType.DMA
    ]
    *hid, low, high, second = call(
        first_mix_kernel,
        (shape((256, 256), BF),) * 4 + (half, half, shape((160, 256), F32)),
        [VMEM] * 15 + [SMEM] + [VMEM] * 4,
        [pltpu.VMEM((32, 256, 128), BF), *links_scratch],
        flops=700_000_000,
        moved=8_000_000,
    )(*s, scaled, *masks, own_second, at, *nodes)
    b_near = neighbours(low, high, "x")
    *passed, h1, h2, h3 = lax.optimization_barrier((*b_near[:2], *hid[1:]))
    back = rounds(low, high, b_near, passed, "x")
    hid = [hid[0]] + [fetch(value, "z", -shift) for value, shift in zip((h1, h2, h3), RING[1:])]
    part = call(
        second_mix_kernel,
        shape((8, 4, 128, 128), BF),
        [VMEM] * 22 + [SMEM] + [VMEM] * 4,
        [pltpu.VMEM((32, 256, 128), BF), *links_scratch],
        flops=900_000_000,
        moved=8_000_000,
    )(*back, *masks, *x_wide, second, at, *nodes)
    part, *hid = lax.optimization_barrier((part, *hid))
    part = lax.all_to_all(part.reshape(32, 128, 128), ("y", "c", "x"), 0, 0, tiled=True)
    tile = shape((16, 128, 128), BF)
    done = call(add_kernel, tile, [VMEM], moved=1_500_000)(part)
    done = lax.all_to_all(done, dom, 0, 0, tiled=True)
    hidden = call(hidden_kernel, shape((256, 1024), BF), [VMEM] * 4 + [SMEM], moved=1_000_000)(*hid, at)
    grad_first, grad_second = call(
        gradient_kernel, (shape((96, 1024), F32), shape((153, 1024), F32)), [VMEM], moved=1_500_000
    )(done)
    return (hidden[None], grad_first, grad_second.T)


def solution(mesh):
    wide = Mesh(mesh.devices.reshape(4, 2, 4, 4), ("y", "c", "x", "z"))
    feat, dom = ("y", "c"), ("x", "z")
    placed = (
        P(feat, dom, None),
        P(feat, None),
        P(),
        P(dom, feat),
        P(dom, feat, None),
        P(dom, feat, None, None, None),
        P(dom, feat, None),
    )
    return jax.shard_map(
        body,
        mesh=wide,
        in_specs=placed,
        out_specs=(P(dom, feat, None), P(feat, None), P()),
        check_vma=False,
    )
```

```python
import jax
import jax.numpy as jnp
from jax import lax
from jax.experimental import pallas as pl
from jax.experimental.pallas import tpu as pltpu
from jax.sharding import Mesh
from jax.sharding import PartitionSpec as P

BF = jnp.bfloat16
F32 = jnp.float32
I32 = jnp.int32
VMEM = pl.BlockSpec(memory_space=pltpu.VMEM)
SMEM = pl.BlockSpec(memory_space=pltpu.SMEM)
MIB = 1024 * 1024
RING = (0, 1, -1, 2)
NT = (((1,), (1,)), ((), ()))


def dot(a, b, dims=(((1,), (0,)), ((), ()))):
    return lax.dot_general(a, b, dims, preferred_element_type=F32)


def halves(a, b):
    low = lax.broadcasted_iota(I32, a.shape, 1) < 64
    return jnp.where(low, a, pltpu.roll(b, 64, 1)), jnp.where(low, pltpu.roll(a, 64, 1), b)


def owner(block):
    return (block % 4) * 4 + block // 4


def mask_kernel(mask_ref, out_ref):
    for b in range(2):
        for k in range(6):
            out_ref[b * 128 : b * 128 + 128, k * 128 : k * 128 + 128] = (
                mask_ref[b, k].astype(F32).astype(BF)
            )


def node_kernel(up_ref, deg_ref, links_ref, out_ref):
    info, inv = [], []
    for b in range(2):
        degree = deg_ref[b : b + 1, :]
        info += [degree >> 5, degree & 31]
        inv.append(lax.rsqrt(degree.astype(F32)))
    scaled = jnp.concatenate(inv, axis=1) * up_ref[...].astype(F32)
    out_ref[0:160, :] = jnp.concatenate([scaled, jnp.zeros((7, 256), F32)], axis=0).astype(BF)
    info = jnp.concatenate(info + [links_ref[...], jnp.zeros((11, 128), I32)], axis=0)
    out_ref[160:176, 0:128] = info.astype(F32).astype(BF)
    out_ref[160:176, 128:256] = jnp.zeros((16, 128), BF)


def pack_kernel(*refs):
    for k in range(4):
        refs[4 + k // 2][k % 2] = refs[k][0:160, :]


def block_of(m_refs, k, b):
    return m_refs[k][b * 128 : b * 128 + 128, :] if k < 3 else m_refs[3 + b][...]


def info_of(i_refs, k):
    return i_refs[k][160:176, 0:128].astype(F32)


def inverse_of(info, b):
    return lax.rsqrt(info[2 * b : 2 * b + 1] * 32.0 + info[2 * b + 1 : 2 * b + 2])


def features_at(refs, k, f):
    return refs[2 * k + f // 4][f % 4]


def weight_kernel(*refs):
    w_refs, at_ref, out_ref, w_ref = refs[:4], refs[4], refs[5], refs[6]
    for k, shift in enumerate(RING):
        for flip in range(2):
            f = ((at_ref[3] + shift + 4) & 3) * 2 + ((at_ref[4] + flip) & 1)
            w_ref[f] = w_refs[k][flip]
    out_ref[...] = w_ref[...].reshape(768, 256).astype(F32).T.astype(BF)


def project_kernel(*refs):
    x_refs, w_ref, i_refs, out_refs = refs[:8], refs[8], refs[9:13], refs[13:15]
    for k in range(4):
        info = info_of(i_refs, k)
        inv = jnp.concatenate([inverse_of(info, 0), inverse_of(info, 1)], axis=1)
        whole = jnp.concatenate([features_at(x_refs, k, f) for f in range(8)], axis=0)
        out_refs[k // 2][k % 2] = (inv * dot(w_ref[...], whole)).astype(BF)


def collect(refs, base, src_ref, at_ref):
    rows = refs[0].shape[1]
    for i, ref in enumerate(refs):
        x = (at_ref[1] + RING[i // 2] + 4) & 3
        for j in range(2):
            d = x * 4 + ((at_ref[2] + RING[(i % 2) * 2 + j] + 4) & 3)
            for h in range(2):
                src_ref[2 * d + h, base : base + rows] = ref[j, :, h * 128 : h * 128 + 128]


def collect_kernel(*refs):
    collect(refs[:8], 0, refs[9], refs[8])


def scalars(i_refs, stage_ref, links_ref, sem):
    rows = [info_of(i_refs, k)[4:5] for k in range(4)]
    stage_ref[...] = jnp.concatenate(rows + [jnp.zeros((4, 128), F32)], axis=0).astype(I32)
    copy = pltpu.make_async_copy(stage_ref, links_ref, sem)
    copy.start()
    copy.wait()


def spread(sources, links_ref, m_refs, k, b, t):
    def field(c):
        parts = [source[c] for source in sources]
        return parts[0] if len(parts) == 1 else jnp.concatenate(parts, axis=0)

    named = [field(links_ref[k, b * 6 + s]) for s in range(6)]
    total = dot(jnp.concatenate(named, axis=1), block_of(m_refs, k, b), NT)
    return field(t).astype(F32) + total


def first_mix_kernel(*refs):
    s_refs, u_ref, m_refs, sw_ref, at_ref = refs[:8], refs[8], refs[9:14], refs[14], refs[15]
    i_refs, hid_refs, back_refs, second_ref = refs[16:20], refs[20:24], refs[24:26], refs[26]
    src_ref, stage_ref, links_ref, sem = refs[27:]
    scalars(i_refs, stage_ref, links_ref, sem)
    collect(s_refs, 0, src_ref, at_ref)
    second = jnp.zeros((160, 256), F32)
    for k, shift in enumerate(RING):
        z = (at_ref[2] + shift + 4) & 3
        info = info_of(i_refs, k)
        for b in range(2):
            inv = inverse_of(info, b)
            lanes = slice(b * 128, b * 128 + 128)
            total = spread((src_ref, u_ref), links_ref, m_refs, k, b, (at_ref[1] * 4 + z) * 2 + b)
            m = inv * total[0:256]
            s = jax.nn.sigmoid(m)
            hid = (m * s).astype(BF)
            hid_refs[k][:, lanes] = hid
            one = (inv * hid.astype(F32)).astype(BF)
            pull = total[256:416].astype(BF)
            second = second + dot(pull, one, NT)
            slope = s * (1.0 + m * (1.0 - s))
            back = inv * inv * dot(sw_ref[...], pull) * slope
            back_refs[k // 2][k % 2, :, lanes] = back.astype(BF)
    second_ref[...] = second


def second_mix_kernel(*refs):
    b_refs, m_refs, x_refs, second_ref, at_ref = refs[:8], refs[8:13], refs[13:21], refs[21], refs[22]
    i_refs, out_ref, src_ref, stage_ref, links_ref, sem = refs[23:27], *refs[27:]
    scalars(i_refs, stage_ref, links_ref, sem)
    collect(b_refs, 0, src_ref, at_ref)
    rights = []
    for k, shift in enumerate(RING):
        z = (at_ref[2] + shift + 4) & 3
        info = info_of(i_refs, k)
        parts = []
        for b in range(2):
            total = spread((src_ref,), links_ref, m_refs, k, b, (at_ref[1] * 4 + z) * 2 + b)
            parts.append((inverse_of(info, b) * total).astype(BF))
        rights.append(jnp.concatenate(parts, axis=1))
    seconds = []
    for p in range(2):
        m = second_ref[:, p * 128 : p * 128 + 128]
        seconds += halves(m[:80], m[80:])
    for f in range(8):
        acc = jnp.zeros((96, 256), F32)
        for k, right in enumerate(rights):
            acc = acc + dot(features_at(x_refs, k, f), right, NT)
        for p in range(2):
            g = acc[:, p * 128 : p * 128 + 128]
            for q, part in enumerate(halves(g[:48], g[48:])):
                both = jnp.concatenate([part, seconds[2 * p + q]], axis=0)
                out_ref[f, 2 * p + q] = both.astype(BF)


def add_kernel(part_ref, out_ref):
    total = part_ref[0].astype(F32)
    for i in range(1, 32):
        total = total + part_ref[i].astype(F32)
    total = total.astype(BF)
    for d in range(16):
        out_ref[d] = total


def hidden_kernel(h0_ref, h1_ref, h2_ref, h3_ref, at_ref, out_ref):
    for ref, shift in zip((h0_ref, h1_ref, h2_ref, h3_ref), RING):
        at = pl.multiple_of(((at_ref[2] - shift + 4) & 3) * 256, 256)
        out_ref[:, pl.ds(at, 256)] = ref[...].astype(F32).T.astype(BF)


def gradient_kernel(in_ref, first_ref, second_ref):
    for j in range(8):
        cols = pl.ds(j * 128, 128)
        one, two = halves(in_ref[owner(2 * j)].astype(F32), in_ref[owner(2 * j + 1)].astype(F32))
        first_ref[0:48, cols] = one[:48]
        first_ref[48:96, cols] = two[:48]
        second_ref[0:80, cols] = one[48:]
        second_ref[80:153, cols] = two[48:121]


def call(kernel, shape, specs, scratch=(), flops=0, moved=0, limit=20):
    return pl.pallas_call(
        kernel,
        out_shape=shape,
        in_specs=specs,
        out_specs=jax.tree.map(lambda _: VMEM, shape),
        scratch_shapes=list(scratch),
        compiler_params=pltpu.CompilerParams(vmem_limit_bytes=limit * MIB),
        cost_estimate=pl.CostEstimate(flops=flops, bytes_accessed=moved, transcendentals=0),
    )


def fetch(value, axis, shift):
    return lax.ppermute(value, axis, [((i + shift) % 4, i) for i in range(4)])


def ring(value, axis):
    return [value] + [fetch(value, axis, shift) for shift in RING[1:]]


def near(value, axis):
    return fetch(value, axis, 1), fetch(value, axis, -1)


def neighbours(low, high, axis):
    return fetch(low, axis, 1), fetch(high, axis, -1), fetch(high, axis, 1), fetch(low, axis, -1)


def rounds(low, high, found, passed, axis):
    far = fetch(passed[0], axis, 1), fetch(passed[1], axis, -1)
    return [low, high, passed[0], found[2], found[3], passed[1], *far]


def body(features, first_weight, second_weight, degree, neighbour_block, neighbour_mask, upstream):
    feat, dom = ("y", "c"), ("x", "z")
    shape = jax.ShapeDtypeStruct
    x, z = lax.axis_index("x"), lax.axis_index("z")
    at = jnp.stack([x * 4 + z, x, z, lax.axis_index("y"), lax.axis_index("c")])
    x_own = lax.all_to_all(
        features.reshape(96, 8, 256).transpose(1, 0, 2), feat, 0, 0, tiled=True
    )
    weight = lax.dynamic_slice(first_weight, (0, z * 256), (96, 256))
    other = lax.ppermute(weight, "c", [(0, 1), (1, 0)])
    other, degree = lax.optimization_barrier((other, degree))
    links = jnp.pad(jnp.maximum(neighbour_block.reshape(1, 12), 0), ((0, 0), (0, 116)))
    nodes = call(node_kernel, shape((176, 256), BF), [VMEM] * 3, moved=200_000)(
        upstream[0].T, degree.reshape(2, 128), links
    )
    nodes = ring(nodes, "z")
    half = shape((2, 160, 256), BF)
    scaled = call(pack_kernel, (half, half), [VMEM] * 4, moved=600_000)(*nodes)
    mask = call(mask_kernel, shape((256, 768), BF), [VMEM], moved=1_200_000)(neighbour_mask[0])
    own_second = lax.dynamic_slice(second_weight, (z * 256, 0), (256, 153))
    own_second = jnp.pad(own_second, ((0, 0), (0, 7)))
    weights = call(
        weight_kernel, shape((256, 768), BF), [VMEM] * 4 + [SMEM], [pltpu.VMEM((8, 96, 256), BF)],
        moved=800_000,
    )(*ring(jnp.stack([weight, other]), "y"), at)
    x_low, x_high, mask, own_second, weights, n1, n2, n3 = lax.optimization_barrier(
        (x_own[:4], x_own[4:], mask, own_second, weights, *nodes[1:])
    )
    nodes = [nodes[0], n1, n2, n3]
    x_near = neighbours(x_low, x_high, "z")
    x0, x1, mask = lax.optimization_barrier((*x_near[:2], mask))
    x_wide = rounds(x_low, x_high, x_near, (x0, x1), "z")
    u_near = neighbours(*scaled, "x")
    scaled = rounds(*scaled, u_near, u_near[:2], "x")
    scaled = call(collect_kernel, shape((32, 160, 128), BF), [VMEM] * 8 + [SMEM], moved=2_600_000)(
        *scaled, at
    )
    half = shape((2, 256, 256), BF)
    s = call(
        project_kernel,
        (half, half),
        [VMEM] * 13,
        flops=400_000_000,
        moved=3_000_000,
    )(*x_wide, weights, *nodes)
    s_near = neighbours(*s, "x")
    after, before = near(mask, "z")
    s0, s1, scaled = lax.optimization_barrier((*s_near[:2], scaled))
    s = rounds(*s, s_near, (s0, s1), "x")
    masks = [mask, after, before, fetch(after[:128], "z", 1), fetch(before[128:], "z", -1)]
    links_scratch = [
        pltpu.VMEM((8, 128), I32), pltpu.SMEM((8, 128), I32), pltpu.SemaphoreType.DMA
    ]
    *hid, low, high, second = call(
        first_mix_kernel,
        (shape((256, 256), BF),) * 4 + (half, half, shape((160, 256), F32)),
        [VMEM] * 15 + [SMEM] + [VMEM] * 4,
        [pltpu.VMEM((32, 256, 128), BF), *links_scratch],
        flops=700_000_000,
        moved=8_000_000,
    )(*s, scaled, *masks, own_second, at, *nodes)
    b_near = neighbours(low, high, "x")
    *passed, h1, h2, h3 = lax.optimization_barrier((*b_near[:2], *hid[1:]))
    back = rounds(low, high, b_near, passed, "x")
    hid = [hid[0]] + [fetch(value, "z", -shift) for value, shift in zip((h1, h2, h3), RING[1:])]
    part = call(
        second_mix_kernel,
        shape((8, 4, 128, 128), BF),
        [VMEM] * 22 + [SMEM] + [VMEM] * 4,
        [pltpu.VMEM((32, 256, 128), BF), *links_scratch],
        flops=900_000_000,
        moved=8_000_000,
    )(*back, *masks, *x_wide, second, at, *nodes)
    part, *hid = lax.optimization_barrier((part, *hid))
    part = lax.all_to_all(part.reshape(32, 128, 128), ("y", "c", "x"), 0, 0, tiled=True)
    tile = shape((16, 128, 128), BF)
    done = call(add_kernel, tile, [VMEM], moved=1_500_000)(part)
    done = lax.all_to_all(done, dom, 0, 0, tiled=True)
    hidden = call(hidden_kernel, shape((256, 1024), BF), [VMEM] * 4 + [SMEM], moved=1_000_000)(*hid, at)
    grad_first, grad_second = call(
        gradient_kernel, (shape((96, 1024), F32), shape((153, 1024), F32)), [VMEM], moved=1_500_000
    )(done)
    return (hidden[None], grad_first, grad_second.T)


def solution(mesh):
    wide = Mesh(mesh.devices.reshape(4, 2, 4, 4), ("y", "c", "x", "z"))
    feat, dom = ("y", "c"), ("x", "z")
    placed = (
        P(feat, dom, None),
        P(feat, None),
        P(),
        P(dom, feat),
        P(dom, feat, None),
        P(dom, feat, None, None, None),
        P(dom, feat, None),
    )
    return jax.shard_map(
        body,
        mesh=wide,
        in_specs=placed,
        out_specs=(P(dom, feat, None), P(feat, None), P()),
        check_vma=False,
    )
```
